128 devices in a mesh: seq: 32 (over y, x, z_lo), fsdp: 4 (over z_hi, core).
Axes of the slice: x: 4, y: 4, z: 4 (z_hi: 2, z_lo: 2; z = z_hi * 2 + z_lo), core: 2. Of those that a mesh axis runs over, the one named last changes fastest.
Arguments:
- hidden_in: bfloat16 [4, 16384, 640], P('fsdp', 'seq'), may hold values from -6 to 6
- cotangent: bfloat16 [4, 16384, 640], P('fsdp', 'seq'), may hold values from -6 to 6
- segments: int32 [4, 16384], P('fsdp', 'seq'), may hold values from 0 to 2, as said below
- positions: int32 [4, 16384], P('fsdp', 'seq'), may hold values from 0 to 16383, as said below
- query_weight: bfloat16 [640, 1024], P('fsdp'), may hold values from -0.25 to 0.25
- key_weight: bfloat16 [640, 256], P('fsdp'), may hold values from -0.25 to 0.25
- value_weight: bfloat16 [640, 256], P('fsdp'), may hold values from -0.25 to 0.25
- output_weight: bfloat16 [1024, 640], P('fsdp'), may hold values from -0.1875 to 0.1875
- gate_weight: bfloat16 [640, 2048], P('fsdp'), may hold values from -0.25 to 0.25
- up_weight: bfloat16 [640, 2048], P('fsdp'), may hold values from -0.25 to 0.25
- down_weight: bfloat16 [2048, 640], P('fsdp'), may hold values from -0.125 to 0.125
- input_norm: bfloat16 [640], P('fsdp'), may hold values from 0.25 to 1.75
- attention_norm: bfloat16 [640], P('fsdp'), may hold values from 0.25 to 1.75
- feed_norm: bfloat16 [640], P('fsdp'), may hold values from 0.25 to 1.75
- result_norm: bfloat16 [640], P('fsdp'), may hold values from 0.25 to 1.75
- query_norm: bfloat16 [256], P('fsdp'), may hold values from 0.25 to 1.75
- key_norm: bfloat16 [256], P('fsdp'), may hold values from 0.25 to 1.75
Outputs:
- layer_out: bfloat16 [4, 16384, 640], P('fsdp', 'seq')
- input_gradient: bfloat16 [4, 16384, 640], P('fsdp', 'seq')
- query_gradient: float32 [640, 1024], P('fsdp')
- key_gradient: float32 [640, 256], P('fsdp')
- value_gradient: float32 [640, 256], P('fsdp')
- output_gradient: float32 [1024, 640], P('fsdp')
- gate_gradient: float32 [640, 2048], P('fsdp')
- up_gradient: float32 [640, 2048], P('fsdp')
- down_gradient: float32 [2048, 640], P('fsdp')
- input_norm_gradient: float32 [640], P('fsdp')
- attention_norm_gradient: float32 [640], P('fsdp')
- feed_norm_gradient: float32 [640], P('fsdp')
- result_norm_gradient: float32 [640], P('fsdp')
- query_norm_gradient: float32 [256], P('fsdp')
- key_norm_gradient: float32 [256], P('fsdp')
The draws below stay inside these ranges and needn't reach their ends.
Inputs may be any that keep to these rules, and one draw needn't show every extreme that they name: `segments`: in each sequence the ids never fall and take the values 0, 1 and 2 in order; document 1 begins within the first 512 tokens and document 2 within the last 512. Within a document positions rise by one from token to token; document 2 begins at 0, document 0 at a value below 512, and document 1 at a value below 512.
All inputs are finite; a program needn't handle non-finite values.
Results may differ from the reference program's by a relative error of at most 0.03.
Values may be sent and summed in bfloat16 or wider, within the bound.
No kernel may reach another device: no remote copies, remote signals or barrier semaphores. Data moves between devices by JAX's collectives and lax.ppermute only.
A program may use at most 128 MiB of HBM per device.

```python
from functools import partial
import jax
import jax.numpy as jnp
from jax import lax

D = 640
HEADS = 4
HD = 256
FF = 2048
WINDOW = 512
TOK_DEV = 512
LENGTH = 16384
SEQS = 4


def document_layout(key):
    first_key, second_key, third_key = jax.random.split(key, 3)
    first_cut = jax.random.randint(first_key, (SEQS, 1), 1, TOK_DEV, dtype=jnp.int32)
    second_cut = LENGTH - TOK_DEV + jax.random.randint(second_key, (SEQS, 1), 1, TOK_DEV, dtype=jnp.int32)
    offset = jax.random.randint(third_key, (SEQS, 1), 0, WINDOW, dtype=jnp.int32)
    places = jnp.arange(LENGTH, dtype=jnp.int32)[None, :]
    segment_ids = (places >= first_cut).astype(jnp.int32) + (places >= second_cut).astype(jnp.int32)
    middle_start = first_cut - TOK_DEV + (second_cut - LENGTH + TOK_DEV)
    starts = jnp.where(segment_ids == 0, -offset, jnp.where(segment_ids == 1, middle_start, second_cut))
    return (segment_ids, places - starts)


def draw_segments(key, part):
    return document_layout(key)[0]


def draw_positions(key, part):
    return document_layout(key)[1]


def levels(rng, extent, cuts, low, high):
    level, own = 1.0, jax.random.fold_in(rng, 6)
    for dim, parts in cuts:
        heights = jnp.exp(jax.random.uniform(jax.random.fold_in(own, dim), (parts,), jnp.float32, low / len(cuts), high / len(cuts)))
        level = level * jnp.repeat(heights, extent[dim] // parts).reshape([-1 if axis == dim else 1 for axis in range(len(extent))])
    return level


def gaussian(rng, extent, deviation, most, shards=(), kind=jnp.bfloat16):
    array = jax.random.normal(rng, extent, jnp.float32) * deviation
    if len(shards) > 0:
        array = levels(rng, extent, shards, -0.22, 0.18) * array
    return jnp.clip(array, min=-most, max=most).astype(kind)


def setup_inputs(seed: int = 0) -> dict:
    key_of = jax.random.split(jax.random.key(seed), 18)
    hidden_in = gaussian(key_of[0], (SEQS, LENGTH, D), 1.0, 6.0, ((0, 4), (1, 32)))
    cotangent = gaussian(key_of[1], (SEQS, LENGTH, D), 1.0, 6.0, ((0, 4), (1, 32)))
    segments = draw_segments(jax.random.fold_in(key_of[17], 71), 0)
    positions = draw_positions(jax.random.fold_in(key_of[17], 71), 0)
    query_weight = gaussian(key_of[4], (D, HEADS * HD), D ** -0.5, 0.25, ((0, 4),))
    key_weight = gaussian(key_of[5], (D, HD), D ** -0.5, 0.25, ((0, 4),))
    value_weight = gaussian(key_of[6], (D, HD), D ** -0.5, 0.25, ((0, 4),))
    output_weight = gaussian(key_of[7], (HEADS * HD, D), (HEADS * HD) ** -0.5, 0.1875, ((0, 4),))
    gate_weight = gaussian(key_of[8], (D, FF), D ** -0.5, 0.25, ((0, 4),))
    up_weight = gaussian(key_of[9], (D, FF), D ** -0.5, 0.25, ((0, 4),))
    down_weight = gaussian(key_of[10], (FF, D), FF ** -0.5, 0.125, ((0, 4),))
    input_norm = jnp.clip(1.0 + 0.15 * jax.random.normal(key_of[11], (D,), jnp.float32), 0.25, 1.75).astype(jnp.bfloat16)
    attention_norm = jnp.clip(1.0 + 0.15 * jax.random.normal(key_of[12], (D,), jnp.float32), 0.25, 1.75).astype(jnp.bfloat16)
    feed_norm = jnp.clip(1.0 + 0.15 * jax.random.normal(key_of[13], (D,), jnp.float32), 0.25, 1.75).astype(jnp.bfloat16)
    result_norm = jnp.clip(1.0 + 0.15 * jax.random.normal(key_of[14], (D,), jnp.float32), 0.25, 1.75).astype(jnp.bfloat16)
    query_norm = jnp.clip(1.0 + 0.15 * jax.random.normal(key_of[15], (HD,), jnp.float32), 0.25, 1.75).astype(jnp.bfloat16)
    key_norm = jnp.clip(1.0 + 0.15 * jax.random.normal(key_of[16], (HD,), jnp.float32), 0.25, 1.75).astype(jnp.bfloat16)
    return {"hidden_in": hidden_in, "cotangent": cotangent, "segments": segments, "positions": positions, "query_weight": query_weight, "key_weight": key_weight, "value_weight": value_weight, "output_weight": output_weight, "gate_weight": gate_weight, "up_weight": up_weight, "down_weight": down_weight, "input_norm": input_norm, "attention_norm": attention_norm, "feed_norm": feed_norm, "result_norm": result_norm, "query_norm": query_norm, "key_norm": key_norm}


@jax.custom_vjp
def low(v):
    return lax.optimization_barrier(v.astype(jnp.bfloat16)).astype(jnp.float32)

@jax.custom_vjp
def low_back(v):
    return v

def low_keep(v):
    return (low(v), None)

def low_pass(kept, grad):
    return (grad,)

def back_keep(v):
    return (v, None)

def back_low(kept, grad):
    return (low(grad),)
low.defvjp(low_keep, low_pass)
low_back.defvjp(back_keep, back_low)
EPSILON = 1e-06
ROPE_BASE = 10000.0

def rms_scale(values, gain):
    return values * lax.rsqrt(lax.optimization_barrier(jnp.mean(values * values, axis=-1, keepdims=True)) + EPSILON) * gain

def rotate(values, places):
    half_size = values.shape[-1] // 2
    freqs = jnp.exp(-jnp.log(ROPE_BASE) * jnp.arange(half_size, dtype=jnp.float32) * 2.0 / values.shape[-1])
    angles = places.astype(jnp.float32)[..., None] * freqs
    cosine = jnp.cos(angles)[..., None, :]
    sine = jnp.sin(angles)[..., None, :]
    first = values[..., :half_size]
    second = values[..., half_size:]
    return jnp.concatenate([first * cosine - second * sine, second * cosine + first * sine], axis=-1)

def matmul(left, right):
    return jnp.dot(left, right, precision=lax.Precision.HIGHEST, preferred_element_type=jnp.float32)

def attention_block(operands):
    queries, key_win, value_win, seg_query, seg_key, pos_query, pos_key = operands
    scores = jnp.einsum('qhd,kd->hqk', queries, key_win, precision=lax.Precision.HIGHEST) * HD ** (-0.5)
    scores = low_back(scores)
    distance = pos_query[:, None] - pos_key[None, :]
    visible = (seg_query[:, None] == seg_key[None, :]) & (distance >= 0) & (distance < WINDOW)
    scores = jnp.where(visible[None], scores, -1e+30)
    row_max = lax.optimization_barrier(jnp.max(scores, axis=-1, keepdims=True))
    row_total = lax.optimization_barrier(jnp.sum(jnp.exp(scores - row_max), axis=-1, keepdims=True))
    log_total = row_max + jnp.log(row_total)
    probs_low = low(jnp.exp(scores - log_total))
    return jnp.einsum('hqk,kd->qhd', probs_low, value_win, precision=lax.Precision.HIGHEST)

def windowed_attention(query_rot, key_rot, value_low, segments, positions):
    blocks = LENGTH // WINDOW

    def windows(values, fill_value):
        seq_shaped = values.reshape((SEQS, LENGTH) + values.shape[1:])
        padding = jnp.full((SEQS, WINDOW) + values.shape[1:], fill_value, values.dtype)
        earlier = jnp.concatenate([padding, seq_shaped], axis=1)[:, :LENGTH]
        block_shape = (SEQS, blocks, WINDOW) + values.shape[1:]
        joined = jnp.concatenate([earlier.reshape(block_shape), seq_shaped.reshape(block_shape)], axis=2)
        return joined.reshape((SEQS * blocks, 2 * WINDOW) + values.shape[1:])
    queries = query_rot.reshape(SEQS * blocks, WINDOW, HEADS, HD)
    key_win = windows(key_rot, 0.0)
    value_win = windows(value_low, 0.0)
    seg_flat = segments.reshape(-1).astype(jnp.int32)
    pos_flat = positions.reshape(-1).astype(jnp.int32)
    seg_query = seg_flat.reshape(SEQS * blocks, WINDOW)
    pos_query = pos_flat.reshape(SEQS * blocks, WINDOW)
    seg_key = windows(seg_flat, -1)
    pos_key = windows(pos_flat, 0)
    attended = lax.map(jax.checkpoint(attention_block), (queries, key_win, value_win, seg_query, seg_key, pos_query, pos_key))
    return attended.reshape(-1, HEADS, HD)

def layer(hidden, query_weight, key_weight, value_weight, output_weight, gate_weight, up_weight, down_weight, input_norm, attention_norm, feed_norm, result_norm, query_norm, key_norm, segments, positions):
    inputs = hidden.reshape(-1, D)
    flat_pos = positions.reshape(-1)
    normed = low(rms_scale(inputs, input_norm))
    query_raw = low_back(matmul(normed, query_weight))
    key_raw = low_back(matmul(normed, key_weight))
    value_raw = low_back(matmul(normed, value_weight))
    query_rot = low(rotate(rms_scale(query_raw.reshape(-1, HEADS, HD), query_norm), flat_pos))
    key_rot = low(rotate(rms_scale(key_raw.reshape(-1, 1, HD), key_norm), flat_pos))[:, 0]
    value_low = low(value_raw)
    attended = windowed_attention(query_rot, key_rot, value_low, segments, positions)
    attended = low(low_back(attended.reshape(-1, HEADS * HD)))
    out_raw = low_back(matmul(attended, output_weight))
    residual = inputs + rms_scale(out_raw, attention_norm)
    feed_in = low(rms_scale(residual, feed_norm))
    gate_raw = low_back(matmul(feed_in, gate_weight))
    up_raw = low_back(matmul(feed_in, up_weight))
    activated = low(jax.nn.gelu(gate_raw, approximate=True) * up_raw)
    down_raw = low_back(matmul(activated, down_weight))
    return (residual + rms_scale(down_raw, result_norm)).reshape(hidden.shape)

def reference(hidden_in, cotangent, segments, positions, query_weight, key_weight, value_weight, output_weight, gate_weight, up_weight, down_weight, input_norm, attention_norm, feed_norm, result_norm, query_norm, key_norm):
    forward = partial(layer, segments=segments, positions=positions)
    layer_out, pullback = jax.vjp(forward, hidden_in.astype(jnp.float32), query_weight.astype(jnp.float32), key_weight.astype(jnp.float32), value_weight.astype(jnp.float32), output_weight.astype(jnp.float32), gate_weight.astype(jnp.float32), up_weight.astype(jnp.float32), down_weight.astype(jnp.float32), input_norm.astype(jnp.float32), attention_norm.astype(jnp.float32), feed_norm.astype(jnp.float32), result_norm.astype(jnp.float32), query_norm.astype(jnp.float32), key_norm.astype(jnp.float32))
    grads = pullback(cotangent.astype(jnp.float32))
    return (layer_out.astype(jnp.bfloat16), grads[0].astype(jnp.bfloat16), grads[1], grads[2], grads[3], grads[4], grads[5], grads[6], grads[7], grads[8], grads[9], grads[10], grads[11], grads[12], grads[13])
```

```python
from functools import partial

import jax
import jax.numpy as jnp
from jax import lax
from jax.sharding import Mesh, PartitionSpec as P

WINDOW = 512
EPSILON = 1e-06
ROPE_BASE = 10000.0
AXES = ("y", "x", "zl", "zh", "c")
SIZES = (4, 4, 2, 2, 2)
PLANE = ("y", "x")


def route(move):
    def index(y, x, zl, zh, c):
        return (((y * 4 + x) * 2 + zl) * 2 + zh) * 2 + c

    return [
        (index(y, x, zl, zh, c), index(*move(y, x, zl, zh, c)))
        for y in range(4)
        for x in range(4)
        for zl in range(2)
        for zh in range(2)
        for c in range(2)
    ]


TO_CORE = route(lambda y, x, zl, zh, c: (y, x, zl, zh, 1 - c))
TO_HALF = route(lambda y, x, zl, zh, c: (y, x, 1 - zl, 1 - zh, c))
TO_LOW = route(lambda y, x, zl, zh, c: (y, x, 1 - zl, zh, c))
TO_NEXT = [(i * 4 + f, i * 4 + 4 + f) for i in range(31) for f in range(4)]
TO_PREVIOUS = [(j, i) for i, j in TO_NEXT]


def send(block, pairs):
    return lax.ppermute(block, AXES, pairs)


def rms_scale(values, gain):
    return values * lax.rsqrt(jnp.mean(values * values, axis=-1, keepdims=True) + EPSILON) * gain


def rotate(values, places):
    half_size = values.shape[-1] // 2
    freqs = jnp.exp(
        -jnp.log(ROPE_BASE) * jnp.arange(half_size, dtype=jnp.float32) * 2.0 / values.shape[-1]
    )
    angles = places.astype(jnp.float32)[..., None] * freqs
    cosine = jnp.cos(angles)[..., None, :]
    sine = jnp.sin(angles)[..., None, :]
    first = values[..., :half_size]
    second = values[..., half_size:]
    return jnp.concatenate(
        [first * cosine - second * sine, second * cosine + first * sine], axis=-1
    )


def head_path(projected, gain, places):
    heads = projected.reshape(projected.shape[0], -1, gain.shape[0])
    return rotate(rms_scale(heads, gain), places)


def key_path(projected, gain, places):
    return head_path(projected, gain, places)[:, 0]


def feed_inner(gate_raw, up_raw):
    return jax.nn.gelu(gate_raw, approximate=True) * up_raw


def product(left, right):
    return jnp.dot(left, right, preferred_element_type=jnp.float32)


def gram_product(left, right):
    return lax.dot_general(
        left, right, (((0,), (0,)), ((), ())), preferred_element_type=jnp.float32
    )


def back_product(left, right):
    return lax.dot_general(
        left, right, (((1,), (1,)), ((), ())), preferred_element_type=jnp.float32
    )


def masked_scores(query_rot, all_keys, visible, score_scale):
    scores = (
        jnp.einsum("qhd,kd->hqk", query_rot, all_keys, preferred_element_type=jnp.float32)
        * score_scale
    )
    return jnp.where(visible[None], scores, -1e30)


def spread(own):
    far = send(own, TO_HALF)
    return own, send(own, TO_CORE), far, send(far, TO_CORE)


def assemble(pieces, me):
    whole = jnp.zeros((4,) + pieces[0].shape, pieces[0].dtype)
    for turn, piece in enumerate(pieces):
        whole = lax.dynamic_update_index_in_dim(whole, piece, me ^ turn, 0)
    return whole


def to_core_sum(shards_by_owner, core):
    keep = lax.dynamic_index_in_dim(shards_by_owner, core, 1, keepdims=False)
    give = lax.dynamic_index_in_dim(shards_by_owner, 1 - core, 1, keepdims=False)
    got = send(give.astype(jnp.bfloat16), TO_CORE)
    return keep.astype(jnp.float32) + got.astype(jnp.float32)


def sum_over_slice(chunks, half):
    parts = lax.all_to_all(chunks.astype(jnp.bfloat16), PLANE, 0, 0)
    part = jnp.sum(parts.astype(jnp.float32), axis=0)
    keep = lax.dynamic_index_in_dim(part, half, 0, keepdims=False)
    give = lax.dynamic_index_in_dim(part, 1 - half, 0, keepdims=False)
    part = keep + send(give.astype(jnp.bfloat16), TO_HALF).astype(jnp.float32)
    part = part.astype(jnp.bfloat16)
    part = part.astype(jnp.float32) + send(part, TO_LOW).astype(jnp.float32)
    part = part.astype(jnp.bfloat16)
    return lax.all_to_all(jnp.broadcast_to(part[None], (16,) + part.shape), PLANE, 0, 0)


def shards(
    hidden_in,
    cotangent,
    segments,
    positions,
    query_weight,
    key_weight,
    value_weight,
    output_weight,
    gate_weight,
    up_weight,
    down_weight,
    input_norm,
    attention_norm,
    feed_norm,
    result_norm,
    query_norm,
    key_norm,
):
    half = lax.axis_index("zh")
    core = lax.axis_index("c")
    me = half * 2 + core
    gains_own = jnp.concatenate(
        [input_norm, attention_norm, feed_norm, result_norm, query_norm, key_norm]
    )
    first_pack = jnp.concatenate(
        [
            jnp.concatenate([query_weight, key_weight, value_weight], axis=1),
            jnp.pad(gains_own[None], ((0, 15), (0, 768))),
        ],
        axis=0,
    )
    first_all = assemble(spread(first_pack), me)
    full_first = first_all[:, :160].reshape(640, 1536)
    full_query = full_first[:, :1024]
    full_key = full_first[:, 1024:1280]
    full_value = full_first[:, 1280:]
    gains = first_all[:, 160, :768].astype(jnp.float32)
    gain_input = gains[:, :160].reshape(-1)
    gain_attention = gains[:, 160:320].reshape(-1)
    gain_feed = gains[:, 320:480].reshape(-1)
    gain_result = gains[:, 480:640].reshape(-1)
    gain_query = gains[:, 640:704].reshape(-1)
    gain_key = gains[:, 704:768].reshape(-1)
    full_output = assemble(spread(output_weight), me).reshape(1024, 640)
    full_gate = assemble(spread(gate_weight), me).reshape(640, 2048)
    full_up = assemble(spread(up_weight), me).reshape(640, 2048)
    full_down = assemble(spread(down_weight), me).reshape(2048, 640)

    model_width = hidden_in.shape[-1]
    hidden_low = hidden_in.reshape(-1, model_width)
    inputs = hidden_low.astype(jnp.float32)
    token_count = inputs.shape[0]
    head_size = gain_query.shape[0]
    head_count = full_query.shape[1] // head_size
    score_scale = head_size ** (-0.5)
    seg_own = segments.reshape(-1) + 1
    pos_own = positions.reshape(-1)
    layout = jnp.stack([seg_own, pos_own])
    hidden_before = send(hidden_low, TO_NEXT)
    layout_before = send(layout, TO_NEXT)
    key_segs = jnp.concatenate([layout_before[0], seg_own])
    key_places = jnp.concatenate([layout_before[1], pos_own])
    inputs_all = jnp.concatenate([hidden_before.astype(jnp.float32), inputs], axis=0)
    normed_all = rms_scale(inputs_all, gain_input).astype(jnp.bfloat16)
    normed = normed_all[token_count:]
    query_raw = product(normed, full_query)
    key_raw = product(normed_all, full_key)
    value_raw = product(normed_all, full_value)
    query_rot = head_path(query_raw, gain_query, pos_own).astype(jnp.bfloat16)
    all_keys = key_path(key_raw, gain_key, key_places).astype(jnp.bfloat16)
    all_values = value_raw.astype(jnp.bfloat16)
    distance = pos_own[:, None] - key_places[None, :]
    visible = (seg_own[:, None] == key_segs[None, :]) & (distance >= 0) & (distance < WINDOW)
    scores = masked_scores(query_rot, all_keys, visible, score_scale)
    row_max = jnp.max(scores, axis=-1, keepdims=True)
    row_total = jnp.sum(jnp.exp(scores - row_max), axis=-1, keepdims=True)
    log_total = row_max + jnp.log(row_total)
    probs_low = jnp.exp(scores - log_total).astype(jnp.bfloat16)
    attended = jnp.einsum("hqk,kd->qhd", probs_low, all_values, preferred_element_type=jnp.float32)
    attended = attended.reshape(token_count, -1).astype(jnp.bfloat16)
    out_raw = product(attended, full_output)
    residual = inputs + rms_scale(out_raw, gain_attention)
    feed_in = rms_scale(residual, gain_feed).astype(jnp.bfloat16)
    gate_raw = product(feed_in, full_gate)
    up_raw = product(feed_in, full_up)
    activated = feed_inner(gate_raw, up_raw).astype(jnp.bfloat16)
    down_raw = product(activated, full_down)
    result = residual + rms_scale(down_raw, gain_result)
    layer_out = result.astype(jnp.bfloat16).reshape(hidden_in.shape)
    upstream = cotangent.reshape(-1, model_width).astype(jnp.float32)
    result_pull = jax.vjp(rms_scale, down_raw, gain_result)[1]
    down_back, result_gain_back = result_pull(upstream)
    down_low = down_back.astype(jnp.bfloat16)
    down_gradient = gram_product(activated, down_low)
    activated_back = back_product(down_low, full_down)
    inner_pull = jax.vjp(feed_inner, gate_raw, up_raw)[1]
    gate_back, up_back = inner_pull(activated_back)
    gate_low = gate_back.astype(jnp.bfloat16)
    up_low = up_back.astype(jnp.bfloat16)
    gate_gradient = gram_product(feed_in, gate_low)
    up_gradient = gram_product(feed_in, up_low)
    feed_back = back_product(gate_low, full_gate) + back_product(up_low, full_up)
    feed_pull = jax.vjp(rms_scale, residual, gain_feed)[1]
    residual_part, feed_gain_back = feed_pull(feed_back)
    residual_back = upstream + residual_part
    attention_pull = jax.vjp(rms_scale, out_raw, gain_attention)[1]
    out_back, attention_gain_back = attention_pull(residual_back)
    out_low = out_back.astype(jnp.bfloat16)
    output_gradient = gram_product(attended, out_low)
    attended_back = back_product(out_low, full_output).astype(jnp.bfloat16)
    attended_back = attended_back.reshape(token_count, head_count, head_size)
    scores_again = masked_scores(query_rot, all_keys, visible, score_scale)
    probability = jnp.exp(scores_again - log_total)
    prob_low = probability.astype(jnp.bfloat16)
    prob_back = jnp.einsum(
        "qhd,kd->hqk", attended_back, all_values, preferred_element_type=jnp.float32
    )
    row_delta = jnp.sum(probability * prob_back, axis=-1, keepdims=True)
    score_back = (probability * (prob_back - row_delta)).astype(jnp.bfloat16)
    query_back = (
        jnp.einsum("hqk,kd->qhd", score_back, all_keys, preferred_element_type=jnp.float32)
        * score_scale
    )
    key_back_all = (
        jnp.einsum("hqk,qhd->kd", score_back, query_rot, preferred_element_type=jnp.float32)
        * score_scale
    )
    value_back_all = jnp.einsum(
        "hqk,qhd->kd", prob_low, attended_back, preferred_element_type=jnp.float32
    )
    query_pull = jax.vjp(partial(head_path, places=pos_own), query_raw, gain_query)[1]
    query_raw_back, query_gain_back = query_pull(query_back)
    key_pull = jax.vjp(partial(key_path, places=key_places), key_raw, gain_key)[1]
    key_raw_back, key_gain_back = key_pull(key_back_all)
    query_low = query_raw_back.astype(jnp.bfloat16)
    key_low = key_raw_back.astype(jnp.bfloat16)
    value_low_back = value_back_all.astype(jnp.bfloat16)
    query_gradient = gram_product(normed, query_low)
    key_gradient = gram_product(normed_all, key_low)
    value_gradient = gram_product(normed_all, value_low_back)
    returned = send(
        jnp.concatenate([key_low[:token_count], value_low_back[:token_count]], axis=1), TO_PREVIOUS
    ).astype(jnp.float32)
    key_total = (returned[:, :head_size] + key_low[token_count:].astype(jnp.float32)).astype(jnp.bfloat16)
    value_total = (returned[:, head_size:] + value_low_back[token_count:].astype(jnp.float32)).astype(jnp.bfloat16)
    normed_back = (
        back_product(query_low, full_query)
        + back_product(key_total, full_key)
        + back_product(value_total, full_value)
    )
    input_pull = jax.vjp(rms_scale, inputs, gain_input)[1]
    input_part, input_gain_back = input_pull(normed_back)
    input_gradient = (residual_back + input_part).astype(jnp.bfloat16).reshape(hidden_in.shape)

    down_sum = to_core_sum(down_gradient.reshape(2, 2, 16, 32, 640), core)
    down_done = sum_over_slice(jnp.swapaxes(down_sum, 0, 1), half)
    down_out = down_done.reshape(512, 640).astype(jnp.float32)
    wide = jnp.stack([gate_gradient, up_gradient]).reshape(2, 2, 2, 160, 16, 128)
    wide = jnp.moveaxis(wide, 0, 2)
    wide_sum = to_core_sum(wide, core)
    wide_done = sum_over_slice(jnp.moveaxis(wide_sum, 3, 0), half)
    wide_out = jnp.moveaxis(wide_done, 0, 2).reshape(2, 160, 2048).astype(jnp.float32)
    out_sum = to_core_sum(output_gradient.reshape(2, 2, 16, 16, 640), core)
    out_done = sum_over_slice(jnp.swapaxes(out_sum, 0, 1), half)
    output_out = out_done.reshape(256, 640).astype(jnp.float32)
    gain_backs = jnp.concatenate(
        [
            input_gain_back.reshape(4, 160),
            attention_gain_back.reshape(4, 160),
            feed_gain_back.reshape(4, 160),
            result_gain_back.reshape(4, 160),
            query_gain_back.reshape(4, 64),
            key_gain_back.reshape(4, 64),
        ],
        axis=1,
    )
    gain_rows = jnp.pad(gain_backs.reshape(4, 16, 1, 48), ((0, 0), (0, 0), (0, 7), (0, 336)))
    first_back = jnp.concatenate([query_gradient, key_gradient, value_gradient], axis=1)
    first_back = first_back.reshape(4, 4, 40, 4, 384).transpose(0, 1, 3, 2, 4).reshape(4, 16, 40, 384)
    first_back = jnp.concatenate([first_back, gain_rows], axis=2).reshape(2, 2, 16, 48, 384)
    first_sum = to_core_sum(first_back, core)
    first_done = sum_over_slice(jnp.swapaxes(first_sum, 0, 1), half).astype(jnp.float32)
    first_out = first_done[:, :40].reshape(4, 4, 40, 384).transpose(0, 2, 1, 3).reshape(160, 1536)
    gains_out = first_done[:, 40, :48].reshape(768)
    return (
        layer_out,
        input_gradient,
        first_out[:, :1024],
        first_out[:, 1024:1280],
        first_out[:, 1280:],
        output_out,
        wide_out[0],
        wide_out[1],
        down_out,
        gains_out[:160],
        gains_out[160:320],
        gains_out[320:480],
        gains_out[480:640],
        gains_out[640:704],
        gains_out[704:768],
    )


def solution(mesh):
    fine = Mesh(mesh.devices.reshape(SIZES), AXES)
    seq, fsdp = ("y", "x", "zl"), ("zh", "c")
    tokens, rows, line = P(fsdp, seq, None), P(fsdp, None), P(fsdp)
    placed = (tokens, tokens, P(fsdp, seq), P(fsdp, seq)) + (rows,) * 7 + (line,) * 6
    return jax.shard_map(
        shards,
        mesh=fine,
        in_specs=placed,
        out_specs=(tokens, tokens) + (rows,) * 7 + (line,) * 6,
        check_vma=False,
    )
```

```python
import jax
import jax.numpy as jnp
from jax import lax
from jax.experimental import pallas as pl
from jax.experimental.pallas import tpu as pltpu
from jax.sharding import Mesh, PartitionSpec as P

WINDOW = 512
EPSILON = 1e-06
ROPE_BASE = 10000.0
AXES = ("y", "x", "zl", "zh", "c")
SIZES = (4, 4, 2, 2, 2)
PLANE = ("y", "x")
T, D, HEADS, HD, FF = 512, 640, 4, 256, 2048
SCALE = HD ** (-0.5)
TILE = 128
SPAN = WINDOW + TILE
PART = 512
F32, BF16 = jnp.float32, jnp.bfloat16


def route(move):
    def index(y, x, zl, zh, c):
        return (((y * 4 + x) * 2 + zl) * 2 + zh) * 2 + c

    return [
        (index(y, x, zl, zh, c), index(*move(y, x, zl, zh, c)))
        for y in range(4)
        for x in range(4)
        for zl in range(2)
        for zh in range(2)
        for c in range(2)
    ]


TO_CORE = route(lambda y, x, zl, zh, c: (y, x, zl, zh, 1 - c))
TO_HALF = route(lambda y, x, zl, zh, c: (y, x, 1 - zl, 1 - zh, c))
TO_LOW = route(lambda y, x, zl, zh, c: (y, x, 1 - zl, zh, c))
TO_SAME = route(lambda y, x, zl, zh, c: (y, x, zl, 1 - zh, c))
TO_NEXT = [(i * 4 + f, i * 4 + 4 + f) for i in range(31) for f in range(4)]
TO_PREVIOUS = [(j, i) for i, j in TO_NEXT]


def send(block, pairs):
    return lax.ppermute(block, AXES, pairs)


def dot(left, right):
    return jnp.dot(left, right, preferred_element_type=F32)


def dot_tn(left, right):
    return lax.dot_general(left, right, (((0,), (0,)), ((), ())), preferred_element_type=F32)


def dot_nt(left, right):
    return lax.dot_general(left, right, (((1,), (1,)), ((), ())), preferred_element_type=F32)


def inverse_rms(values):
    return lax.rsqrt(jnp.mean(values * values, axis=-1, keepdims=True) + EPSILON)


def norm_back(values, gain, upstream):
    inverse = inverse_rms(values)
    unit = values * inverse
    scaled = upstream * gain
    back = inverse * (scaled - unit * jnp.mean(scaled * unit, axis=-1, keepdims=True))
    return back, upstream * unit


def turned(values, cosine, sine):
    first, second = values[:, : HD // 2], values[:, HD // 2 :]
    return jnp.concatenate([first * cosine - second * sine, second * cosine + first * sine], axis=-1)


def pack_kernel(place, wq, wk, wv, g_in, g_att, g_feed, g_res, g_q, g_k, gate, up, first, chunk):
    me = place[0]
    first[:160, :1024] = wq[...]
    first[:160, 1024:1280] = wk[...]
    first[:160, 1280:] = wv[...]

    def placed(upper, lower, width):
        count = upper.shape[0]
        rows = lax.broadcasted_iota(jnp.int32, (16, count), 0)
        both = jnp.where(rows == 0, upper[...].astype(F32)[None, :], jnp.where(rows == 1, lower[...].astype(F32)[None, :], 0.0))
        source = lax.broadcasted_iota(jnp.int32, (count, width), 0)
        target = lax.broadcasted_iota(jnp.int32, (count, width), 1)
        pick = jnp.where(target == source + me * count, 1.0, 0.0).astype(BF16)
        return dot(both.astype(BF16), pick).astype(BF16)

    first[160:, :640] = placed(g_in, g_feed, 640)
    first[160:, 640:1280] = placed(g_att, g_res, 640)
    first[160:, 1280:] = placed(g_q, g_k, 256)
    chunk[0:160, :] = gate[...]
    chunk[160:320, :] = up[...]


def project_kernel(place, own, own_c, far, far_c, before, here, cosine, sine,
                   weight, gains, normed, query_raw, key_raw, query_rot, key_rot, value_low):
    me = place[0]
    for turn, piece in enumerate((own, own_c, far, far_c)):
        weight[pl.ds(pl.multiple_of((me ^ turn) * 160, 32), 160), :] = piece[:160, :]
    total = sum(piece[160:, :].astype(F32) for piece in (own, own_c, far, far_c))
    gains[...] = total
    gain_in, gain_q, gain_k = total[0:1, :640], total[0:1, 1280:], total[1:2, 1280:]
    for base, source in ((0, before), (T, here)):
        values = source[...].astype(F32)
        normed[base : base + T, :] = (values * inverse_rms(values) * gain_in).astype(BF16)
    for base in (0, T):
        low = normed[base : base + T, :]
        cos, sin = cosine[base : base + T, :], sine[base : base + T, :]
        raw = dot(low, weight[:, 1024:1280])
        key_raw[base : base + T, :] = raw
        key_rot[base : base + T, :] = turned(raw * inverse_rms(raw) * gain_k, cos, sin).astype(BF16)
        value_low[base : base + T, :] = dot(low, weight[:, 1280:]).astype(BF16)
    low = normed[T:, :]
    cos, sin = cosine[T:, :], sine[T:, :]
    for h in range(HEADS):
        cols = slice(h * HD, (h + 1) * HD)
        raw = dot(low, weight[:, cols])
        query_raw[:, cols] = raw
        query_rot[:, cols] = turned(raw * inverse_rms(raw) * gain_q, cos, sin).astype(BF16)


def stacked(ref, rows):
    return jnp.concatenate([ref[rows, h * HD : (h + 1) * HD] for h in range(HEADS)], axis=0)


def attend_kernel(query_rot, key_rot, value_low, code_q, code_k, attended, probs):
    for i in range(T // TILE):
        rows, span = slice(i * TILE, (i + 1) * TILE), slice(i * TILE, i * TILE + SPAN)
        scores = dot_nt(stacked(query_rot, rows), key_rot[span, :]) * SCALE
        gap = code_q[rows, :] - code_k[:, span]
        visible = (gap >= 0) & (gap < WINDOW)
        scores = jnp.where(visible[None], scores.reshape(HEADS, TILE, SPAN), -1e30)
        top = jnp.max(scores, axis=-1, keepdims=True)
        raised = jnp.exp(scores - top)
        weight = raised * (1.0 / jnp.sum(raised, axis=-1, keepdims=True))
        low = weight.reshape(HEADS * TILE, SPAN).astype(BF16)
        probs[i] = low
        out = dot(low, value_low[span, :])
        for h in range(HEADS):
            attended[rows, h * HD : (h + 1) * HD] = out[h * TILE : (h + 1) * TILE].astype(BF16)


GELU_A, GELU_B = 0.7978845608028654, 0.044715
ROWS = 480


def feed_kernel(place, hidden, cotangent, attended, gains,
                wo_own, wo_c, wo_far, wo_far_c,
                g_own, u_own, d_own, g_c, u_c, d_c, far, far_c, d_far, d_far_c,
                layer_out, give, keep, wo, out_keep, residual_keep, feed_back, gain_back,
                wg, wu, wd, gate, up, activated, feed_in, turn_low, down_low):
    me, core = place[0], place[2]
    for turn, (wo_p, g_p, u_p, d_p) in enumerate(((wo_own, g_own, u_own, d_own), (wo_c, g_c, u_c, d_c))):
        j = me ^ turn
        wg[pl.ds(pl.multiple_of(j * 160, 32), 160), :] = g_p[...]
        wu[pl.ds(pl.multiple_of(j * 160, 32), 160), :] = u_p[...]
        wd[pl.ds(pl.multiple_of(j * 512, 512), 512), :] = d_p[...]
        wo[pl.ds(pl.multiple_of(j * 256, 256), 256), :] = wo_p[...]
    for turn, (wo_p, piece, d_p) in enumerate(((wo_far, far, d_far), (wo_far_c, far_c, d_far_c))):
        j = me ^ (2 + turn)
        wo[pl.ds(pl.multiple_of(j * 256, 256), 256), :] = wo_p[...]
        for k in range(16):
            cols = slice(128 * k, 128 * k + 128)
            wg[pl.ds(pl.multiple_of(j * 160, 32), 160), cols] = piece[k, 0:160, :]
            wu[pl.ds(pl.multiple_of(j * 160, 32), 160), cols] = piece[k, 160:320, :]
        wd[pl.ds(pl.multiple_of(j * 512, 512), 512), :] = d_p[...]
    gain_att, gain_feed, gain_res = gains[0:1, 640:1280], gains[1:2, :640], gains[1:2, 640:1280]

    def put(owner, write):
        pl.when(core == owner % 2)(lambda: write(keep))
        pl.when(core != owner % 2)(lambda: write(give))

    out_raw = dot(attended[...], wo[...])
    residual = hidden[...].astype(F32) + out_raw * inverse_rms(out_raw) * gain_att
    out_keep[...] = out_raw
    residual_keep[...] = residual
    feed_in[...] = (residual * inverse_rms(residual) * gain_feed).astype(BF16)
    turn_low[...] = feed_in[...].T

    def forward(n, carry):
        cols = pl.ds(pl.multiple_of(n * PART, PART), PART)
        g = dot(feed_in[...], wg[:, cols])
        u = dot(feed_in[...], wu[:, cols])
        t = jnp.tanh(GELU_A * (g + GELU_B * g * g * g))
        half = 0.5 * (1.0 + t)
        slope = half + 0.5 * g * (1.0 - t * t) * (GELU_A * (1.0 + 3.0 * GELU_B * g * g))
        gelu = g * half
        gate[:, cols] = gelu
        up[:, cols] = u * slope
        activated[:, cols] = (gelu * u).astype(BF16)
        return carry

    lax.fori_loop(0, FF // PART, forward, 0)
    down_raw = dot(activated[...], wd[...])
    layer_out[...] = (residual + down_raw * inverse_rms(down_raw) * gain_res).astype(BF16)
    upstream = cotangent[...].astype(F32)
    down_back, share = norm_back(down_raw, gain_res, upstream)
    gain_back[...] = jnp.broadcast_to(jnp.sum(share, axis=0, keepdims=True), (8, D))
    down_low[...] = down_back.astype(BF16)
    turn_down = down_low[...].T
    feed_back[...] = jnp.zeros_like(feed_back)

    def backward(n, carry):
        cols = pl.ds(pl.multiple_of(n * PART, PART), PART)
        act_back = dot_nt(down_low[...], wd[cols, :])
        gate_low = (act_back * up[:, cols]).astype(BF16)
        up_low = (act_back * gate[:, cols]).astype(BF16)
        feed_back[...] += dot_nt(gate_low, wg[:, cols]) + dot_nt(up_low, wu[:, cols])
        for base, low in ((0, gate_low), (160, up_low)):
            grad = dot(turn_low[...], low).astype(BF16)
            for j in range(4):
                def write(ref, j=j, base=base, grad=grad):
                    for b in range(PART // 128):
                        ref[n * (PART // 128) + b, j // 2, base : base + 160, :] = grad[
                            160 * j : 160 * j + 160, 128 * b : 128 * b + 128
                        ]
                put(j, write)
        grad = dot(turn_down, activated[:, cols]).astype(BF16)
        j = n // (512 // PART)
        first = (n % (512 // PART)) * (PART // 128)

        def write_down(ref):
            for b in range(PART // 128):
                for r in range(4):
                    ref[(first + b) * 4 + r, j // 2, 320:480, :] = grad[160 * r : 160 * r + 160, 128 * b : 128 * b + 128]
        put(j, write_down)
        return carry

    lax.fori_loop(0, FF // PART, backward, 0)


def output_kernel(place, cotangent, attended, gains, wo, out_raw, residual, feed_back, result_gain_back,
                  give, keep, attended_back, residual_back, gain_back):
    core = place[2]
    gain_att, gain_feed = gains[0:1, 640:1280], gains[1:2, :640]
    part, share = norm_back(residual[...], gain_feed, feed_back[...])
    gain_back[1:2, :] = jnp.sum(share, axis=0, keepdims=True)
    back = cotangent[...].astype(F32) + part
    residual_back[...] = back
    out_back, share = norm_back(out_raw[...], gain_att, back)
    gain_back[0:1, :] = jnp.sum(share, axis=0, keepdims=True)
    gain_back[2:, :] = result_gain_back[2:, :]
    out_low = out_back.astype(BF16)
    attended_back[...] = dot_nt(out_low, wo[...]).astype(BF16)
    turn_out = out_low.T
    for j in range(4):
        grad = dot(turn_out, attended[:, 256 * j : 256 * j + 256]).astype(BF16)

        def write(ref, j=j, grad=grad):
            for b in range(2):
                for r in range(8):
                    ref[8 * b + r, j // 2, :, :] = grad[80 * r : 80 * r + 80, 128 * b : 128 * b + 128]
        pl.when(core == j % 2)(lambda write=write: write(keep))
        pl.when(core != j % 2)(lambda write=write: write(give))


FEED_SCRATCH = [((D, FF), BF16), ((D, FF), BF16), ((FF, D), BF16), ((T, FF), F32), ((T, FF), F32),
                ((T, FF), BF16), ((T, D), BF16), ((D, T), BF16), ((T, D), BF16)]
FEED_OUTS = [((T, D), BF16), ((16, 2, ROWS, 128), BF16), ((16, 2, ROWS, 128), BF16), ((1024, D), BF16),
             ((T, D), F32), ((T, D), F32), ((T, D), F32), ((8, D), F32)]
OUTPUT_OUTS = [((16, 2, 80, 128), BF16), ((16, 2, 80, 128), BF16), ((T, 1024), BF16), ((T, D), F32), ((8, D), F32)]


def bench(nm, mk, place):
    if nm == "feed":
        args = [mk((T, D), BF16), mk((T, D), BF16), mk((T, 1024), BF16), mk((16, 1536), F32)] + [mk((256, D), BF16)] * 4 + [
            mk((160, FF), BF16), mk((160, FF), BF16), mk((512, D), BF16)] * 2 + [mk((16, 480, 128), BF16)] * 2
        return (lambda *a: call(feed_kernel, FEED_OUTS, FEED_SCRATCH, 14_000_000_000, *a)), [place] + args


def back_kernel(place, query_rot, key_rot, value_low, probs, attended, attended_back,
                query_raw, key_raw, normed, weight, gains, cosine, sine, gain_back, before, here,
                give, keep, own_back, before_back,
                query_low, pair_low, key_sum, value_sum):
    core = place[2]
    key_sum[...] = jnp.zeros_like(key_sum)
    value_sum[...] = jnp.zeros_like(value_sum)
    gain_in, gain_q, gain_k = gains[0:1, :640], gains[0:1, 1280:], gains[1:2, 1280:]
    gain_q_back = jnp.zeros((1, HD), F32)
    for i in range(T // TILE):
        rows, span = slice(i * TILE, (i + 1) * TILE), slice(i * TILE, i * TILE + SPAN)
        back = stacked(attended_back, rows)
        delta = jnp.sum(back.astype(F32) * stacked(attended, rows).astype(F32), axis=-1, keepdims=True)
        prob = probs[i]
        prob_back = dot_nt(back, value_low[span, :])
        score_back = (prob.astype(F32) * (prob_back - delta)).astype(BF16)
        value_sum[span, :] += dot_tn(prob, back)
        key_sum[span, :] += dot_tn(score_back, stacked(query_rot, rows)) * SCALE
        query_back = dot(score_back, key_rot[span, :]) * SCALE
        cos, sin = cosine[T + i * TILE : T + (i + 1) * TILE, :], sine[T + i * TILE : T + (i + 1) * TILE, :]
        for h in range(HEADS):
            unturned = turned(query_back[h * TILE : (h + 1) * TILE], cos, -sin)
            raw_back, share = norm_back(query_raw[rows, h * HD : (h + 1) * HD], gain_q, unturned)
            gain_q_back += jnp.sum(share, axis=0, keepdims=True)
            query_low[rows, h * HD : (h + 1) * HD] = raw_back.astype(BF16)
    raw_back, share = norm_back(key_raw[...], gain_k, turned(key_sum[...], cosine[...], -sine[...]))
    gain_k_back = jnp.sum(share, axis=0, keepdims=True)
    pair_low[:, :HD] = raw_back.astype(BF16)
    pair_low[:, HD:] = value_sum[...].astype(BF16)

    def store(grad, block):
        for j in range(4):
            def put(ref, j=j):
                for b in range(grad.shape[1] // 128):
                    ref[j // 2, 160 * (block + b) : 160 * (block + b) + 160, :] = grad[
                        160 * j : 160 * j + 160, 128 * b : 128 * b + 128
                    ]
            pl.when(core == j % 2)(lambda put=put: put(keep))
            pl.when(core != j % 2)(lambda put=put: put(give))

    for h in range(HEADS):
        store(dot_tn(normed[T:, :], query_low[:, h * HD : (h + 1) * HD]).astype(BF16), 2 * h)
    for h in range(2):
        store(dot_tn(normed[...], pair_low[:, h * HD : (h + 1) * HD]).astype(BF16), 8 + 2 * h)

    earlier = dot_nt(pair_low[:T, :], weight[:, 1024:])
    before_back[...] = earlier.astype(BF16)
    later = dot_nt(pair_low[T:, :], weight[:, 1024:]) + dot_nt(query_low[...], weight[:, :1024])
    own_back[...] = later
    values, values_before = here[...].astype(F32), before[...].astype(F32)
    gain_in_back = jnp.sum(later * (values * inverse_rms(values)), axis=0, keepdims=True) + jnp.sum(
        earlier * (values_before * inverse_rms(values_before)), axis=0, keepdims=True
    )
    rows = lax.broadcasted_iota(jnp.int32, (128, 128), 0)
    block = jnp.zeros((128, 128), F32)
    lines = [gain_in_back] + [gain_back[r : r + 1, :] for r in range(3)] + [gain_q_back, gain_k_back]
    at = 0
    for line in lines:
        for b in range(line.shape[1] // 128):
            block = jnp.where(rows == at, line[:, 128 * b : 128 * b + 128], block)
            at += 1
    low = block.astype(BF16)
    for j in range(2):
        keep[j, 1920:, :] = low
        give[j, 1920:, :] = low


def finish_wide_kernel(place, own, other, gate, up):
    low = place[4]
    for k in range(16):
        cols = slice(128 * k, 128 * k + 128)
        mine, theirs = own[k].astype(F32), other[k].astype(F32)
        gate[:, cols] = jnp.where(low == 0, mine, theirs)
        up[:, cols] = jnp.where(low == 0, theirs, mine)


def finish_rest_kernel(place, done, query, key, value, down, out, *gains):
    me = place[0]
    for b in range(4):
        block = jnp.concatenate([done[4 * b + r, 128:288, :] for r in range(4)], axis=0)
        down[128 * b : 128 * b + 128, :] = block.astype(F32).T
    for b in range(2):
        block = jnp.concatenate([done[8 * b + r, 288:368, :] for r in range(8)], axis=0)
        out[128 * b : 128 * b + 128, :] = block.astype(F32).T
    for block in range(12):
        ref, at = ((query, block), (key, block - 8), (value, block - 10))[(block >= 8) + (block >= 10)]
        row = 0
        while row < 160:
            flat = 160 * block + row
            chunk, start = flat // 128, flat % 128
            size = min(160 - row, 128 - start)
            ref[row : row + size, 128 * at : 128 * at + 128] = done[chunk, start : start + size, :].astype(F32)
            row += size
    lines = done[15, 0:32, :]

    def pick(count, size):
        parts = []
        for b in range(count):
            source = lax.broadcasted_iota(jnp.int32, (128, size), 0) + 128 * b
            target = lax.broadcasted_iota(jnp.int32, (128, size), 1) + me * size
            parts.append(dot(lines, jnp.where(source == target, 1.0, 0.0).astype(BF16)))
        return parts

    for i, ref in enumerate(gains[:4]):
        parts = pick(5, 160) if i == 0 else parts
        ref[...] = sum(parts[b][5 * i + b : 5 * i + b + 1, :] for b in range(5)).reshape(160)
    parts = pick(2, 64)
    for i, ref in enumerate(gains[4:]):
        ref[...] = sum(parts[b][20 + 2 * i + b : 21 + 2 * i + b, :] for b in range(2)).reshape(64)


def call(kernel, outs, scratch, flops, *args):
    spec = [pl.BlockSpec(memory_space=pltpu.SMEM)] + [pl.BlockSpec(memory_space=pltpu.VMEM)] * (len(args) - 1)
    if kernel is attend_kernel:
        spec = [pl.BlockSpec(memory_space=pltpu.VMEM)] * len(args)
    shapes = [jax.ShapeDtypeStruct(s, d) for s, d in outs]
    size = sum(a.size * a.dtype.itemsize for a in args) + sum(s.size * s.dtype.itemsize for s in shapes)
    return pl.pallas_call(
        kernel,
        out_shape=shapes,
        in_specs=spec,
        out_specs=[pl.BlockSpec(memory_space=pltpu.VMEM)] * len(shapes),
        scratch_shapes=[pltpu.VMEM(s, d) for s, d in scratch],
        compiler_params=pltpu.CompilerParams(vmem_limit_bytes=58 * 2**20),
        cost_estimate=pl.CostEstimate(flops=flops, bytes_accessed=size, transcendentals=0),
    )(*args)


def pick(block, index, axis):
    return lax.dynamic_index_in_dim(block, index, axis, keepdims=False)


def add(*terms):
    return sum(t.astype(F32) for t in terms).astype(BF16)


def plane_swap(chunks):
    return lax.all_to_all(chunks, PLANE, 0, 0)


def plane_total(chunks):
    return jnp.sum(chunks.astype(F32), axis=0)


def plane_gather(chunk):
    return lax.all_to_all(jnp.broadcast_to(chunk[None], (16,) + chunk.shape), PLANE, 0, 0)


def line_sum(part, half):
    keep, give = pick(part, half, 0).astype(BF16), pick(part, 1 - half, 0).astype(BF16)
    return add(keep, send(keep, TO_LOW), send(give, TO_HALF), send(give, TO_SAME))


def shards(
    hidden_in, cotangent, segments, positions,
    query_weight, key_weight, value_weight, output_weight, gate_weight, up_weight, down_weight,
    input_norm, attention_norm, feed_norm, result_norm, query_norm, key_norm,
):
    half, core, low = lax.axis_index("zh"), lax.axis_index("c"), lax.axis_index("zl")
    me = half * 2 + core
    spot = lax.axis_index("y") * 4 + lax.axis_index("x")
    place = jnp.stack([me, half, core, spot, low]).astype(jnp.int32)
    hidden = hidden_in.reshape(T, D)
    code = (segments * 65536 + positions).reshape(T) + 2**20

    gain_rows = [input_norm, attention_norm, feed_norm, result_norm, query_norm, key_norm]
    whole = pl.BlockSpec(memory_space=pltpu.VMEM)
    first, chunk = pl.pallas_call(
        pack_kernel,
        out_shape=[jax.ShapeDtypeStruct((176, 1536), BF16), jax.ShapeDtypeStruct((320, 128), BF16)],
        grid_spec=pltpu.PrefetchScalarGridSpec(
            num_scalar_prefetch=1,
            grid=(1,),
            in_specs=[pl.BlockSpec(a.shape, lambda i, s: (0, 0)) for a in (query_weight, key_weight, value_weight)]
            + [pl.BlockSpec(a.shape, lambda i, s: (0,)) for a in gain_rows]
            + [
                pl.BlockSpec((160, 128), lambda i, s: (0, s[3])),
                pl.BlockSpec((160, 128), lambda i, s: (0, s[3])),
            ],
            out_specs=[
                pl.BlockSpec((176, 1536), lambda i, s: (0, 0)),
                pl.BlockSpec((320, 128), lambda i, s: (0, 0)),
            ],
        ),
        compiler_params=pltpu.CompilerParams(vmem_limit_bytes=32 * 2**20),
    )(place, query_weight, key_weight, value_weight, *gain_rows, gate_weight, up_weight)

    far_chunk = send(chunk, TO_HALF)
    first_far = send(first, TO_HALF)
    first_core = send(first, TO_CORE)
    hidden_before = send(hidden, TO_NEXT)
    code_before = send(code, TO_NEXT)
    first_far_core = send(first_far, TO_CORE)
    far = plane_gather(far_chunk)
    out_far = send(output_weight, TO_HALF)
    down_far = send(down_weight, TO_HALF)
    out_core = send(output_weight, TO_CORE)
    gate_core = send(gate_weight, TO_CORE)
    up_core = send(up_weight, TO_CORE)
    down_core = send(down_weight, TO_CORE)

    codes = jnp.concatenate([code_before, code])
    freqs = jnp.exp(-jnp.log(ROPE_BASE) * jnp.arange(HD // 2, dtype=F32) * 2.0 / HD)
    angles = (codes & 65535).astype(F32)[:, None] * freqs
    cosine, sine = jnp.cos(angles), jnp.sin(angles)

    weight, gains, normed, query_raw, key_raw, query_rot, key_rot, value_low = call(
        project_kernel,
        [((D, 1536), BF16), ((16, 1536), F32), ((2 * T, D), BF16), ((T, 1024), F32), ((2 * T, HD), F32),
         ((T, 1024), BF16), ((2 * T, HD), BF16), ((2 * T, HD), BF16)],
        [],
        1_400_000_000,
        place, first, first_core, first_far, first_far_core, hidden_before, hidden, cosine, sine,
    )
    attended, probs = call(
        attend_kernel,
        [((T, 1024), BF16), ((T // TILE, HEADS * TILE, SPAN), BF16)],
        [],
        1_400_000_000,
        query_rot, key_rot, value_low, code.reshape(T, 1), codes.reshape(1, 2 * T),
    )
    far, out_far, down_far, attended = lax.optimization_barrier((far, out_far, down_far, attended))
    out_far_core = send(out_far, TO_CORE)
    down_far_core = send(down_far, TO_CORE)
    far_core = send(far, TO_CORE)
    layer_out, give, keep, wo, out_raw, residual, feed_back, result_gain_back = call(
        feed_kernel, FEED_OUTS, FEED_SCRATCH, 14_000_000_000,
        place, hidden, cotangent.reshape(T, D), attended, gains,
        output_weight, out_core, out_far, out_far_core,
        gate_weight, up_weight, down_weight, gate_core, up_core, down_core, far, far_core, down_far, down_far_core,
    )
    out_give, out_keep, attended_back, residual_back, gain_back = call(
        output_kernel, OUTPUT_OUTS, [], 1_400_000_000,
        place, cotangent.reshape(T, D), attended, gains, wo, out_raw, residual, feed_back, result_gain_back,
    )
    got = send(give, TO_CORE)
    out_got = send(out_give, TO_CORE)
    wide = add(keep[:, :, :320], got[:, :, :320])
    deep = jnp.concatenate([add(keep[:, :, 320:], got[:, :, 320:]), add(out_keep, out_got)], axis=2)
    wide, deep, attended_back = lax.optimization_barrier((wide, deep, attended_back))
    first_give, first_keep, own_back, before_back = call(
        back_kernel,
        [((2, 2048, 128), BF16), ((2, 2048, 128), BF16), ((T, D), F32), ((T, D), BF16)],
        [((T, 1024), BF16), ((2 * T, 512), BF16), ((2 * T, HD), F32), ((2 * T, HD), F32)],
        8_000_000_000,
        place, query_rot, key_rot, value_low, probs, attended, attended_back,
        query_raw, key_raw, normed, weight, gains, cosine, sine, gain_back, hidden_before, hidden,
    )
    wide_got = plane_swap(wide)
    deep = add(pick(deep, half, 1), send(pick(deep, 1 - half, 1), TO_HALF))
    deep = deep.reshape(16, 2, 120, 128)
    deep = add(pick(deep, low, 1), send(pick(deep, 1 - low, 1), TO_LOW))
    slim = add(first_keep, send(first_give, TO_CORE))
    slim = jnp.swapaxes(slim.reshape(2, 16, 128, 128), 0, 1).reshape(16, 256, 128)
    rest = jnp.concatenate([slim, deep], axis=1)
    rest, wide_got = lax.optimization_barrier((rest, wide_got))
    rest_got = plane_swap(rest)
    wide_part = plane_total(wide_got).reshape(2, 2, 160, 128)
    near, away = pick(wide_part, half, 0), pick(wide_part, 1 - half, 0)
    wide_part = add(
        pick(near, low, 0),
        send(pick(near, 1 - low, 0).astype(BF16), TO_LOW),
        send(pick(away, 1 - low, 0).astype(BF16), TO_HALF),
        send(pick(away, low, 0).astype(BF16), TO_SAME),
    )
    wide_part, rest_got = lax.optimization_barrier((wide_part, rest_got))
    wide_done = plane_gather(wide_part)
    rest_part = plane_total(rest_got)
    deep = rest_part[256:].astype(BF16)
    deep_got = send(deep, TO_LOW)
    slim_part = line_sum(rest_part[:256].reshape(2, 128, 128), half)
    rest_part = jnp.concatenate(
        [slim_part, jnp.where(low == 0, deep, deep_got), jnp.where(low == 0, deep_got, deep)]
    )
    rest_part, wide_done = lax.optimization_barrier((rest_part, wide_done))
    wide_other = send(wide_done, TO_LOW)
    rest_done = plane_gather(rest_part)

    normed_back = own_back + send(before_back, TO_PREVIOUS).astype(F32)
    gain_in = gains[0, :640]
    inputs = hidden.astype(F32)
    part, _ = norm_back(inputs, gain_in, normed_back)
    input_gradient = (residual_back + part).astype(BF16)

    gate_out, up_out = call(
        finish_wide_kernel, [((160, FF), F32), ((160, FF), F32)], [], 1_000_000, place, wide_done, wide_other
    )
    rest_out = call(
        finish_rest_kernel,
        [((160, 1024), F32), ((160, HD), F32), ((160, HD), F32), ((512, D), F32), ((256, D), F32)]
        + [((160,), F32)] * 4 + [((64,), F32)] * 2,
        [], 1_000_000, place, rest_done,
    )
    return (
        layer_out.reshape(hidden_in.shape),
        input_gradient.reshape(hidden_in.shape),
        *rest_out[:3],
        rest_out[4],
        gate_out,
        up_out,
        rest_out[3],
        *rest_out[5:],
    )


def solution(mesh):
    fine = Mesh(mesh.devices.reshape(SIZES), AXES)
    seq, fsdp = ("y", "x", "zl"), ("zh", "c")
    tokens, rows, line = P(fsdp, seq, None), P(fsdp, None), P(fsdp)
    placed = (tokens, tokens, P(fsdp, seq), P(fsdp, seq)) + (rows,) * 7 + (line,) * 6
    return jax.shard_map(
        shards,
        mesh=fine,
        in_specs=placed,
        out_specs=(tokens, tokens) + (rows,) * 7 + (line,) * 6,
        check_vma=False,
    )
```

```python
import jax
import jax.numpy as jnp
from jax import lax
from jax.experimental import pallas as pl
from jax.experimental.pallas import tpu as pltpu
from jax.sharding import Mesh, PartitionSpec as P

WINDOW = 512
EPSILON = 1e-06
ROPE_BASE = 10000.0
AXES = ("y", "x", "zl", "zh", "c")
SIZES = (4, 4, 2, 2, 2)
PLANE = ("y", "x")
T, D, HEADS, HD, FF = 512, 640, 4, 256, 2048
SCALE = HD ** (-0.5)
TILE = 128
SPAN = WINDOW + TILE
PART = 512
F32, BF16 = jnp.float32, jnp.bfloat16


def route(move):
    def index(y, x, zl, zh, c):
        return (((y * 4 + x) * 2 + zl) * 2 + zh) * 2 + c

    return [
        (index(y, x, zl, zh, c), index(*move(y, x, zl, zh, c)))
        for y in range(4)
        for x in range(4)
        for zl in range(2)
        for zh in range(2)
        for c in range(2)
    ]


TO_CORE = route(lambda y, x, zl, zh, c: (y, x, zl, zh, 1 - c))
TO_HALF = route(lambda y, x, zl, zh, c: (y, x, 1 - zl, 1 - zh, c))
TO_LOW = route(lambda y, x, zl, zh, c: (y, x, 1 - zl, zh, c))
TO_SAME = route(lambda y, x, zl, zh, c: (y, x, zl, 1 - zh, c))
TO_NEXT = [(i * 4 + f, i * 4 + 4 + f) for i in range(31) for f in range(4)]
TO_PREVIOUS = [(j, i) for i, j in TO_NEXT]


def send(block, pairs):
    return lax.ppermute(block, AXES, pairs)


def dot(left, right):
    return jnp.dot(left, right, preferred_element_type=F32)


def dot_tn(left, right):
    return lax.dot_general(left, right, (((0,), (0,)), ((), ())), preferred_element_type=F32)


def dot_nt(left, right):
    return lax.dot_general(left, right, (((1,), (1,)), ((), ())), preferred_element_type=F32)


def inverse_rms(values):
    return lax.rsqrt(jnp.mean(values * values, axis=-1, keepdims=True) + EPSILON)


def norm_back(values, gain, upstream):
    inverse = inverse_rms(values)
    unit = values * inverse
    scaled = upstream * gain
    back = inverse * (scaled - unit * jnp.mean(scaled * unit, axis=-1, keepdims=True))
    return back, upstream * unit


def turned(values, cosine, sine):
    first, second = values[:, : HD // 2], values[:, HD // 2 :]
    return jnp.concatenate([first * cosine - second * sine, second * cosine + first * sine], axis=-1)


def pack_kernel(place, wq, wk, wv, g_in, g_att, g_feed, g_res, g_q, g_k, gate, up, first, chunk):
    me = place[0]
    first[:160, :1024] = wq[...]
    first[:160, 1024:1280] = wk[...]
    first[:160, 1280:] = wv[...]

    def placed(upper, lower, width):
        count = upper.shape[0]
        rows = lax.broadcasted_iota(jnp.int32, (16, count), 0)
        both = jnp.where(rows == 0, upper[...].astype(F32)[None, :], jnp.where(rows == 1, lower[...].astype(F32)[None, :], 0.0))
        source = lax.broadcasted_iota(jnp.int32, (count, width), 0)
        target = lax.broadcasted_iota(jnp.int32, (count, width), 1)
        pick = jnp.where(target == source + me * count, 1.0, 0.0).astype(BF16)
        return dot(both.astype(BF16), pick).astype(BF16)

    first[160:, :640] = placed(g_in, g_feed, 640)
    first[160:, 640:1280] = placed(g_att, g_res, 640)
    first[160:, 1280:] = placed(g_q, g_k, 256)
    chunk[0:160, :] = gate[...]
    chunk[160:320, :] = up[...]


def project_kernel(place, own, own_c, far, far_c, before, here, cosine, sine,
                   weight, gains, normed, query_raw, key_raw, query_rot, key_rot, value_low):
    me = place[0]
    for turn, piece in enumerate((own, own_c, far, far_c)):
        weight[pl.ds(pl.multiple_of((me ^ turn) * 160, 32), 160), :] = piece[:160, :]
    total = sum(piece[160:, :].astype(F32) for piece in (own, own_c, far, far_c))
    gains[...] = total
    gain_in, gain_q, gain_k = total[0:1, :640], total[0:1, 1280:], total[1:2, 1280:]
    for base, source in ((0, before), (T, here)):
        values = source[...].astype(F32)
        normed[base : base + T, :] = (values * inverse_rms(values) * gain_in).astype(BF16)
    for base in (0, T):
        low = normed[base : base + T, :]
        cos, sin = cosine[base : base + T, :], sine[base : base + T, :]
        raw = dot(low, weight[:, 1024:1280])
        key_raw[base : base + T, :] = raw
        key_rot[base : base + T, :] = turned(raw * inverse_rms(raw) * gain_k, cos, sin).astype(BF16)
        value_low[base : base + T, :] = dot(low, weight[:, 1280:]).astype(BF16)
    low = normed[T:, :]
    cos, sin = cosine[T:, :], sine[T:, :]
    for h in range(HEADS):
        cols = slice(h * HD, (h + 1) * HD)
        raw = dot(low, weight[:, cols])
        query_raw[:, cols] = raw
        query_rot[:, cols] = turned(raw * inverse_rms(raw) * gain_q, cos, sin).astype(BF16)


def stacked(ref, rows):
    return jnp.concatenate([ref[rows, h * HD : (h + 1) * HD] for h in range(HEADS)], axis=0)


def attend_kernel(query_rot, key_rot, value_low, code_q, code_k, attended, probs):
    for i in range(T // TILE):
        rows, span = slice(i * TILE, (i + 1) * TILE), slice(i * TILE, i * TILE + SPAN)
        scores = dot_nt(stacked(query_rot, rows), key_rot[span, :]) * SCALE
        gap = code_q[rows, :] - code_k[:, span]
        visible = (gap >= 0) & (gap < WINDOW)
        scores = jnp.where(visible[None], scores.reshape(HEADS, TILE, SPAN), -1e30)
        top = jnp.max(scores, axis=-1, keepdims=True)
        raised = jnp.exp(scores - top)
        weight = raised * (1.0 / jnp.sum(raised, axis=-1, keepdims=True))
        low = weight.reshape(HEADS * TILE, SPAN).astype(BF16)
        probs[i] = low
        out = dot(low, value_low[span, :])
        for h in range(HEADS):
            attended[rows, h * HD : (h + 1) * HD] = out[h * TILE : (h + 1) * TILE].astype(BF16)


GELU_A, GELU_B = 0.7978845608028654, 0.044715
ROWS = 480


def mix_kernel(place, hidden, attended, gains, wo_own, wo_c, wo_far, wo_far_c,
               wo, out_raw, residual, feed_in, turn_low):
    me = place[0]
    for turn, piece in enumerate((wo_own, wo_c, wo_far, wo_far_c)):
        wo[pl.ds(pl.multiple_of((me ^ turn) * 256, 256), 256), :] = piece[...]
    out = dot(attended[...], wo[...])
    out_raw[...] = out
    total = hidden[...].astype(F32) + out * inverse_rms(out) * gains[0:1, 640:1280]
    residual[...] = total
    low = (total * inverse_rms(total) * gains[1:2, :640]).astype(BF16)
    feed_in[...] = low
    turn_low[...] = low.T


def feed_kernel(place, residual, cotangent, gains, feed_in, turn_low,
                g_own, u_own, d_own, g_c, u_c, d_c, far, far_c, d_far, d_far_c,
                layer_out, give, keep, feed_back, gain_back,
                wg, wu, wd, gate, up, activated, down_low):
    me, core = place[0], place[2]
    for turn, (g_p, u_p, d_p) in enumerate(((g_own, u_own, d_own), (g_c, u_c, d_c))):
        j = me ^ turn
        wg[pl.ds(pl.multiple_of(j * 160, 32), 160), :] = g_p[...]
        wu[pl.ds(pl.multiple_of(j * 160, 32), 160), :] = u_p[...]
        wd[pl.ds(pl.multiple_of(j * 512, 512), 512), :] = d_p[...]
    for turn, (piece, d_p) in enumerate(((far, d_far), (far_c, d_far_c))):
        j = me ^ (2 + turn)
        for k in range(16):
            cols = slice(128 * k, 128 * k + 128)
            wg[pl.ds(pl.multiple_of(j * 160, 32), 160), cols] = piece[k, 0:160, :]
            wu[pl.ds(pl.multiple_of(j * 160, 32), 160), cols] = piece[k, 160:320, :]
        wd[pl.ds(pl.multiple_of(j * 512, 512), 512), :] = d_p[...]
    gain_res = gains[1:2, 640:1280]

    def put(owner, write):
        pl.when(core == owner % 2)(lambda: write(keep))
        pl.when(core != owner % 2)(lambda: write(give))

    def forward(n, carry):
        cols = pl.ds(pl.multiple_of(n * PART, PART), PART)
        g = dot(feed_in[...], wg[:, cols])
        u = dot(feed_in[...], wu[:, cols])
        t = jnp.tanh(GELU_A * (g + GELU_B * g * g * g))
        half = 0.5 * (1.0 + t)
        slope = half + 0.5 * g * (1.0 - t * t) * (GELU_A * (1.0 + 3.0 * GELU_B * g * g))
        gelu = g * half
        gate[:, cols] = gelu
        up[:, cols] = u * slope
        activated[:, cols] = (gelu * u).astype(BF16)
        return carry

    lax.fori_loop(0, FF // PART, forward, 0)
    down_raw = dot(activated[...], wd[...])
    layer_out[...] = (residual[...] + down_raw * inverse_rms(down_raw) * gain_res).astype(BF16)
    upstream = cotangent[...].astype(F32)
    down_back, share = norm_back(down_raw, gain_res, upstream)
    gain_back[...] = jnp.broadcast_to(jnp.sum(share, axis=0, keepdims=True), (8, D))
    down_low[...] = down_back.astype(BF16)
    turn_down = down_low[...].T
    feed_back[...] = jnp.zeros_like(feed_back)

    def backward(n, carry):
        cols = pl.ds(pl.multiple_of(n * PART, PART), PART)
        act_back = dot_nt(down_low[...], wd[cols, :])
        gate_low = (act_back * up[:, cols]).astype(BF16)
        up_low = (act_back * gate[:, cols]).astype(BF16)
        feed_back[...] += dot_nt(gate_low, wg[:, cols]) + dot_nt(up_low, wu[:, cols])
        for base, low in ((0, gate_low), (160, up_low)):
            grad = dot(turn_low[...], low).astype(BF16)
            for j in range(4):
                def write(ref, j=j, base=base, grad=grad):
                    for b in range(PART // 128):
                        ref[n * (PART // 128) + b, j // 2, base : base + 160, :] = grad[
                            160 * j : 160 * j + 160, 128 * b : 128 * b + 128
                        ]
                put(j, write)
        grad = dot(turn_down, activated[:, cols]).astype(BF16)
        j = n // (512 // PART)
        first = (n % (512 // PART)) * (PART // 128)

        def write_down(ref):
            for b in range(PART // 128):
                for r in range(4):
                    ref[(first + b) * 4 + r, j // 2, 320:480, :] = grad[160 * r : 160 * r + 160, 128 * b : 128 * b + 128]
        put(j, write_down)
        return carry

    lax.fori_loop(0, FF // PART, backward, 0)


def output_kernel(place, cotangent, attended, gains, wo, out_raw, residual, feed_back, result_gain_back,
                  give, keep, attended_back, residual_back, gain_back):
    core = place[2]
    gain_att, gain_feed = gains[0:1, 640:1280], gains[1:2, :640]
    part, share = norm_back(residual[...], gain_feed, feed_back[...])
    gain_back[1:2, :] = jnp.sum(share, axis=0, keepdims=True)
    back = cotangent[...].astype(F32) + part
    residual_back[...] = back
    out_back, share = norm_back(out_raw[...], gain_att, back)
    gain_back[0:1, :] = jnp.sum(share, axis=0, keepdims=True)
    gain_back[2:, :] = result_gain_back[2:, :]
    out_low = out_back.astype(BF16)
    attended_back[...] = dot_nt(out_low, wo[...]).astype(BF16)
    turn_out = out_low.T
    for j in range(4):
        grad = dot(turn_out, attended[:, 256 * j : 256 * j + 256]).astype(BF16)

        def write(ref, j=j, grad=grad):
            for b in range(2):
                for r in range(8):
                    ref[8 * b + r, j // 2, :, :] = grad[80 * r : 80 * r + 80, 128 * b : 128 * b + 128]
        pl.when(core == j % 2)(lambda write=write: write(keep))
        pl.when(core != j % 2)(lambda write=write: write(give))


FEED_SCRATCH = [((D, FF), BF16), ((D, FF), BF16), ((FF, D), BF16), ((T, FF), F32), ((T, FF), F32),
                ((T, FF), BF16), ((T, D), BF16)]
FEED_OUTS = [((T, D), BF16), ((16, 2, ROWS, 128), BF16), ((16, 2, ROWS, 128), BF16), ((T, D), F32), ((8, D), F32)]
MIX_OUTS = [((1024, D), BF16), ((T, D), F32), ((T, D), F32), ((T, D), BF16), ((D, T), BF16)]
OUTPUT_OUTS = [((16, 2, 80, 128), BF16), ((16, 2, 80, 128), BF16), ((T, 1024), BF16), ((T, D), F32), ((8, D), F32)]


def bench(nm, mk, place):
    if nm == "feed":
        args = [mk((T, D), F32), mk((T, D), BF16), mk((16, 1536), F32), mk((T, D), BF16), mk((D, T), BF16)] + [
            mk((160, FF), BF16), mk((160, FF), BF16), mk((512, D), BF16)] * 2 + [mk((16, 320, 128), BF16)] * 2 + [mk((512, D), BF16)] * 2
        return (lambda *a: call(feed_kernel, FEED_OUTS, FEED_SCRATCH, 1_000_000, *a)), [place] + args


def back_kernel(query_rot, key_rot, value_low, probs, attended, attended_back,
                query_raw, key_raw, gains, cosine, sine,
                query_low, pair_low, head_back, key_sum, value_sum):
    key_sum[...] = jnp.zeros_like(key_sum)
    value_sum[...] = jnp.zeros_like(value_sum)
    gain_q, gain_k = gains[0:1, 1280:], gains[1:2, 1280:]
    gain_q_back = jnp.zeros((1, HD), F32)
    for i in range(T // TILE):
        rows, span = slice(i * TILE, (i + 1) * TILE), slice(i * TILE, i * TILE + SPAN)
        back = stacked(attended_back, rows)
        delta = jnp.sum(back.astype(F32) * stacked(attended, rows).astype(F32), axis=-1, keepdims=True)
        prob = probs[i]
        prob_back = dot_nt(back, value_low[span, :])
        score_back = (prob.astype(F32) * (prob_back - delta)).astype(BF16)
        value_sum[span, :] += dot_tn(prob, back)
        key_sum[span, :] += dot_tn(score_back, stacked(query_rot, rows)) * SCALE
        query_back = dot(score_back, key_rot[span, :]) * SCALE
        cos, sin = cosine[T + i * TILE : T + (i + 1) * TILE, :], sine[T + i * TILE : T + (i + 1) * TILE, :]
        for h in range(HEADS):
            unturned = turned(query_back[h * TILE : (h + 1) * TILE], cos, -sin)
            raw_back, share = norm_back(query_raw[rows, h * HD : (h + 1) * HD], gain_q, unturned)
            gain_q_back += jnp.sum(share, axis=0, keepdims=True)
            query_low[rows, h * HD : (h + 1) * HD] = raw_back.astype(BF16)
    raw_back, share = norm_back(key_raw[...], gain_k, turned(key_sum[...], cosine[...], -sine[...]))
    gain_k_back = jnp.sum(share, axis=0, keepdims=True)
    pair_low[:, :HD] = raw_back.astype(BF16)
    pair_low[:, HD:] = value_sum[...].astype(BF16)

    rows = lax.broadcasted_iota(jnp.int32, (8, HD), 0)
    head_back[...] = jnp.where(rows == 0, gain_q_back, gain_k_back)


def first_kernel(place, normed, query_low, pair_low, weight, head_back, gain_back, before, here,
                 give, keep, own_back, before_back):
    core = place[2]

    def store(grad, block):
        for j in range(4):
            def put(ref, j=j):
                for b in range(grad.shape[1] // 128):
                    ref[j // 2, 160 * (block + b) : 160 * (block + b) + 160, :] = grad[
                        160 * j : 160 * j + 160, 128 * b : 128 * b + 128
                    ]
            pl.when(core == j % 2)(lambda put=put: put(keep))
            pl.when(core != j % 2)(lambda put=put: put(give))

    for h in range(HEADS):
        store(dot_tn(normed[T:, :], query_low[:, h * HD : (h + 1) * HD]).astype(BF16), 2 * h)
    for h in range(2):
        store(dot_tn(normed[...], pair_low[:, h * HD : (h + 1) * HD]).astype(BF16), 8 + 2 * h)

    earlier = dot_nt(pair_low[:T, :], weight[:, 1024:])
    before_back[...] = earlier.astype(BF16)
    later = dot_nt(pair_low[T:, :], weight[:, 1024:]) + dot_nt(query_low[...], weight[:, :1024])
    own_back[...] = later
    values, values_before = here[...].astype(F32), before[...].astype(F32)
    gain_in_back = jnp.sum(later * (values * inverse_rms(values)), axis=0, keepdims=True) + jnp.sum(
        earlier * (values_before * inverse_rms(values_before)), axis=0, keepdims=True
    )
    rows = lax.broadcasted_iota(jnp.int32, (128, 128), 0)
    block = jnp.zeros((128, 128), F32)
    lines = [gain_in_back] + [gain_back[r : r + 1, :] for r in range(3)] + [head_back[0:1, :], head_back[1:2, :]]
    at = 0
    for line in lines:
        for b in range(line.shape[1] // 128):
            block = jnp.where(rows == at, line[:, 128 * b : 128 * b + 128], block)
            at += 1
    low = block.astype(BF16)
    for j in range(2):
        keep[j, 1920:, :] = low
        give[j, 1920:, :] = low


MERGED = 4


def merge_kernel(place, keep, got, out_keep, out_got, wide, up_keep, up_give, down_keep, down_give):
    half, mixed = place[1], place[5]
    for k in range(MERGED):
        for z in range(2):
            def added(rows, k=k, z=z):
                return keep[k, z, rows, :].astype(F32) + got[k, z, rows, :].astype(F32)

            wide[k, z, :160, :] = added(slice(0, 160)).astype(BF16)
            wide[k, z, 160:240, :] = (out_keep[k, z].astype(F32) + out_got[k, z].astype(F32)).astype(BF16)
            wide[k, z, 240:, :] = jnp.zeros((16, 128), BF16)
            one, two = added(slice(320, 400)), added(slice(400, 480))
            down_keep[k, z] = jnp.where(mixed == 0, one, two).astype(BF16)
            down_give[k, z] = jnp.where(mixed == 0, two, one).astype(BF16)
        one, two = (keep[k, z, 160:320, :].astype(F32) + got[k, z, 160:320, :].astype(F32) for z in range(2))
        up_keep[k] = jnp.where(half == 0, one, two).astype(BF16)
        up_give[k] = jnp.where(half == 0, two, one).astype(BF16)


def merge(place, keep, got, out_keep, out_got):
    def spec(*shape):
        return pl.BlockSpec((MERGED, *shape), lambda i: (i,) + (0,) * len(shape))

    outs = [(2, 256, 128), (160, 128), (160, 128), (2, 80, 128), (2, 80, 128)]
    return pl.pallas_call(
        merge_kernel,
        grid=(16 // MERGED,),
        out_shape=[jax.ShapeDtypeStruct((16, *o), BF16) for o in outs],
        in_specs=[pl.BlockSpec(memory_space=pltpu.SMEM)] + [spec(2, 480, 128)] * 2 + [spec(2, 80, 128)] * 2,
        out_specs=[spec(*o) for o in outs],
        compiler_params=pltpu.CompilerParams(vmem_limit_bytes=58 * 2**20),
        cost_estimate=pl.CostEstimate(flops=1_000_000, bytes_accessed=1_000_000, transcendentals=0),
    )(place, keep, got, out_keep, out_got)


def line_kernel(place, up_keep, up_got, down_keep, down_got, up_next, up_give, down_next, down_give):
    half, low = place[1], place[4]

    def parted(one, two, choice, stay, leave):
        stay[...] = jnp.where(choice == 0, one, two).astype(BF16)
        leave[...] = jnp.where(choice == 0, two, one).astype(BF16)

    one, two = (up_keep[:, r : r + 80, :].astype(F32) + up_got[:, r : r + 80, :].astype(F32) for r in (0, 80))
    parted(one, two, low, up_next, up_give)
    one, two = (down_keep[:, z].astype(F32) + down_got[:, z].astype(F32) for z in range(2))
    parted(one, two, half, down_next, down_give)


def rest_kernel(keep, got, up_keep, up_got, down_keep, down_got, rest):
    for z in range(2):
        for k in range(16):
            rows = slice(128 * k, 128 * k + 128)
            rest[k, 128 * z : 128 * z + 128, :] = (keep[z, rows, :].astype(F32) + got[z, rows, :].astype(F32)).astype(BF16)
    rest[:, 256:336, :] = (up_keep[...].astype(F32) + up_got[...].astype(F32)).astype(BF16)
    rest[:, 336:, :] = (down_keep[...].astype(F32) + down_got[...].astype(F32)).astype(BF16)


def finish_wide_kernel(place, own, other, gate, up, out):
    low = place[4]
    blocks = []
    for k in range(16):
        cols = slice(128 * k, 128 * k + 128)
        mine, theirs = own[k].astype(F32), other[k].astype(F32)
        one = jnp.where(low == 0, mine, theirs)
        two = jnp.where(low == 0, theirs, mine)
        gate[:128, cols] = one[:128]
        gate[128:, cols] = two[:32]
        up[:80, cols] = one[128:]
        up[80:, cols] = two[128:]
        blocks.append(two[32:112])
    for b in range(2):
        out[128 * b : 128 * b + 128, :] = jnp.concatenate(blocks[8 * b : 8 * b + 8], axis=0).T


def finish_rest_kernel(place, done, query, key, value, down, *gains):
    me = place[0]
    for b in range(4):
        block = jnp.concatenate([done[4 * b + r, 128:288, :] for r in range(4)], axis=0)
        down[128 * b : 128 * b + 128, :] = block.astype(F32).T
    for block in range(12):
        ref, at = ((query, block), (key, block - 8), (value, block - 10))[(block >= 8) + (block >= 10)]
        row = 0
        while row < 160:
            flat = 160 * block + row
            chunk, start = flat // 128, flat % 128
            size = min(160 - row, 128 - start)
            ref[row : row + size, 128 * at : 128 * at + 128] = done[chunk, start : start + size, :].astype(F32)
            row += size
    lines = done[15, 0:32, :]

    def pick(count, size):
        parts = []
        for b in range(count):
            source = lax.broadcasted_iota(jnp.int32, (128, size), 0) + 128 * b
            target = lax.broadcasted_iota(jnp.int32, (128, size), 1) + me * size
            parts.append(dot(lines, jnp.where(source == target, 1.0, 0.0).astype(BF16)))
        return parts

    for i, ref in enumerate(gains[:4]):
        parts = pick(5, 160) if i == 0 else parts
        ref[...] = sum(parts[b][5 * i + b : 5 * i + b + 1, :] for b in range(5)).reshape(160)
    parts = pick(2, 64)
    for i, ref in enumerate(gains[4:]):
        ref[...] = sum(parts[b][20 + 2 * i + b : 21 + 2 * i + b, :] for b in range(2)).reshape(64)


def call(kernel, outs, scratch, flops, *args):
    spec = [pl.BlockSpec(memory_space=pltpu.SMEM)] + [pl.BlockSpec(memory_space=pltpu.VMEM)] * (len(args) - 1)
    if kernel in (attend_kernel, rest_kernel, back_kernel):
        spec = [pl.BlockSpec(memory_space=pltpu.VMEM)] * len(args)
    shapes = [jax.ShapeDtypeStruct(s, d) for s, d in outs]
    size = sum(a.size * a.dtype.itemsize for a in args) + sum(s.size * s.dtype.itemsize for s in shapes)
    return pl.pallas_call(
        kernel,
        out_shape=shapes,
        in_specs=spec,
        out_specs=[pl.BlockSpec(memory_space=pltpu.VMEM)] * len(shapes),
        scratch_shapes=[pltpu.VMEM(s, d) for s, d in scratch],
        compiler_params=pltpu.CompilerParams(vmem_limit_bytes=58 * 2**20),
        cost_estimate=pl.CostEstimate(flops=flops, bytes_accessed=min(size, flops), transcendentals=0),
    )(*args)


def pick(block, index, axis):
    return lax.dynamic_index_in_dim(block, index, axis, keepdims=False)


def add(*terms):
    return sum(t.astype(F32) for t in terms).astype(BF16)


def plane_swap(chunks):
    return lax.all_to_all(chunks, PLANE, 0, 0)


def plane_total(chunks):
    return jnp.sum(chunks.astype(F32), axis=0)


def plane_gather(chunk):
    return lax.all_to_all(jnp.broadcast_to(chunk[None], (16,) + chunk.shape), PLANE, 0, 0)


def line_sum(part, half):
    keep, give = pick(part, half, 0).astype(BF16), pick(part, 1 - half, 0).astype(BF16)
    return add(keep, send(keep, TO_LOW), send(give, TO_HALF), send(give, TO_SAME))


def shards(
    hidden_in, cotangent, segments, positions,
    query_weight, key_weight, value_weight, output_weight, gate_weight, up_weight, down_weight,
    input_norm, attention_norm, feed_norm, result_norm, query_norm, key_norm,
):
    half, core, low = lax.axis_index("zh"), lax.axis_index("c"), lax.axis_index("zl")
    me = half * 2 + core
    spot = lax.axis_index("y") * 4 + lax.axis_index("x")
    place = jnp.stack([me, half, core, spot, low, low ^ half]).astype(jnp.int32)
    hidden = hidden_in.reshape(T, D)
    code = (segments * 65536 + positions).reshape(T) + 2**20

    gain_rows = [input_norm, attention_norm, feed_norm, result_norm, query_norm, key_norm]
    whole = pl.BlockSpec(memory_space=pltpu.VMEM)
    first, chunk = pl.pallas_call(
        pack_kernel,
        out_shape=[jax.ShapeDtypeStruct((176, 1536), BF16), jax.ShapeDtypeStruct((320, 128), BF16)],
        grid_spec=pltpu.PrefetchScalarGridSpec(
            num_scalar_prefetch=1,
            grid=(1,),
            in_specs=[pl.BlockSpec(a.shape, lambda i, s: (0, 0)) for a in (query_weight, key_weight, value_weight)]
            + [pl.BlockSpec(a.shape, lambda i, s: (0,)) for a in gain_rows]
            + [
                pl.BlockSpec((160, 128), lambda i, s: (0, s[3])),
                pl.BlockSpec((160, 128), lambda i, s: (0, s[3])),
            ],
            out_specs=[
                pl.BlockSpec((176, 1536), lambda i, s: (0, 0)),
                pl.BlockSpec((320, 128), lambda i, s: (0, 0)),
            ],
        ),
        compiler_params=pltpu.CompilerParams(vmem_limit_bytes=58 * 2**20),
    )(place, query_weight, key_weight, value_weight, *gain_rows, gate_weight, up_weight)

    far_chunk = send(chunk, TO_HALF)
    first_far = send(first, TO_HALF)
    hidden_before = send(hidden, TO_NEXT)
    code_before = send(code, TO_NEXT)
    first_core = send(first, TO_CORE)
    codes = jnp.concatenate([code_before, code])
    own_places = positions.reshape(T)
    places = jnp.concatenate([own_places[0] - T + jnp.arange(T, dtype=jnp.int32), own_places])
    freqs = jnp.exp(-jnp.log(ROPE_BASE) * jnp.arange(HD // 2, dtype=F32) * 2.0 / HD)
    angles = places.astype(F32)[:, None] * freqs
    cosine, sine = jnp.cos(angles), jnp.sin(angles)
    far_chunk, first_far, hidden_before, codes, cosine, sine, output_late, down_late = lax.optimization_barrier(
        (far_chunk, first_far, hidden_before, codes, cosine, sine, output_weight, down_weight)
    )
    first_far_core = send(first_far, TO_CORE)
    far = plane_gather(far_chunk)
    out_far = send(output_late, TO_HALF)
    down_far = send(down_late, TO_HALF)
    out_core, gate_core, up_core, down_core = (
        send(w, TO_CORE) for w in (output_weight, gate_weight, up_weight, down_weight)
    )

    weight, gains, normed, query_raw, key_raw, query_rot, key_rot, value_low = call(
        project_kernel,
        [((D, 1536), BF16), ((16, 1536), F32), ((2 * T, D), BF16), ((T, 1024), F32), ((2 * T, HD), F32),
         ((T, 1024), BF16), ((2 * T, HD), BF16), ((2 * T, HD), BF16)],
        [],
        1_000_000,
        place, first, first_core, first_far, first_far_core, hidden_before, hidden, cosine, sine,
    )
    query_rot, out_core, gate_core, up_core, down_core, out_far = lax.optimization_barrier(
        (query_rot, out_core, gate_core, up_core, down_core, out_far)
    )
    out_far_core = send(out_far, TO_CORE)
    attended, probs = call(
        attend_kernel,
        [((T, 1024), BF16), ((T // TILE, HEADS * TILE, SPAN), BF16)],
        [],
        1_000_000,
        query_rot, key_rot, value_low, code.reshape(T, 1), codes.reshape(1, 2 * T),
    )
    attended, out_far_core, down_far = lax.optimization_barrier((attended, out_far_core, down_far))
    down_far_core = send(down_far, TO_CORE)
    wo, out_raw, residual, feed_in, turn_low = call(
        mix_kernel, MIX_OUTS, [], 1_000_000,
        place, hidden, attended, gains, output_weight, out_core, out_far, out_far_core,
    )
    far, down_far_core, feed_in = lax.optimization_barrier((far, down_far_core, feed_in))
    layer_out, give, keep, feed_back, result_gain_back = call(
        feed_kernel, FEED_OUTS, FEED_SCRATCH, 1_000_000,
        place, residual, cotangent.reshape(T, D), gains, feed_in, turn_low,
        gate_weight, up_weight, down_weight, gate_core, up_core, down_core,
        far, send(far, TO_CORE), down_far, down_far_core,
    )
    out_give, out_keep, attended_back, residual_back, gain_back = call(
        output_kernel, OUTPUT_OUTS, [], 1_000_000,
        place, cotangent.reshape(T, D), attended, gains, wo, out_raw, residual, feed_back, result_gain_back,
    )
    got = send(give, TO_CORE)
    out_got = send(out_give, TO_CORE)
    wide, up_keep, up_give, down_keep, down_give, attended_back = lax.optimization_barrier(
        (*merge(place, keep, got, out_keep, out_got), attended_back)
    )
    wide_got = plane_swap(wide)
    up_got, down_got = send(up_give, TO_HALF), send(down_give, TO_LOW)
    query_low, pair_low, head_back = call(
        back_kernel,
        [((T, 1024), BF16), ((2 * T, 512), BF16), ((8, HD), F32)],
        [((2 * T, HD), F32), ((2 * T, HD), F32)],
        1_000_000,
        query_rot, key_rot, value_low, probs, attended, attended_back, query_raw, key_raw, gains, cosine, sine,
    )
    up_keep, up_give, down_keep, down_give = call(
        line_kernel, [((16, 80, 128), BF16)] * 4, [], 0, place, up_keep, up_got, down_keep, down_got
    )
    query_low, up_keep, up_give, down_keep, down_give = lax.optimization_barrier(
        (query_low, up_keep, up_give, down_keep, down_give)
    )
    up_got, down_got = send(up_give, TO_LOW), send(down_give, TO_HALF)
    first_give, first_keep, own_back, before_back = call(
        first_kernel,
        [((2, 2048, 128), BF16), ((2, 2048, 128), BF16), ((T, D), F32), ((T, D), BF16)],
        [],
        1_000_000,
        place, normed, query_low, pair_low, weight, head_back, gain_back, hidden_before, hidden,
    )
    first_give, up_got, down_got = lax.optimization_barrier((first_give, up_got, down_got))
    (rest,) = call(
        rest_kernel, [((16, 416, 128), BF16)], [], 0,
        first_keep, send(first_give, TO_CORE), up_keep, up_got, down_keep, down_got,
    )
    rest, wide_got = lax.optimization_barrier((rest, wide_got))
    rest_got = plane_swap(rest)
    wide_part = plane_total(wide_got).reshape(2, 2, 128, 128)
    near, away = pick(wide_part, half, 0), pick(wide_part, 1 - half, 0)
    wide_part = add(
        pick(near, low, 0),
        send(pick(near, 1 - low, 0).astype(BF16), TO_LOW),
        send(pick(away, 1 - low, 0).astype(BF16), TO_HALF),
        send(pick(away, low, 0).astype(BF16), TO_SAME),
    )
    wide_part, rest_got = lax.optimization_barrier((wide_part, rest_got))
    rest_part = plane_total(rest_got)
    wide_done = plane_gather(jnp.concatenate([wide_part, rest_part[256:336].astype(BF16)]))
    down_part = rest_part[336:].astype(BF16)
    down_got = send(down_part, TO_LOW)
    slim_part = line_sum(rest_part[:256].reshape(2, 128, 128), half)
    mixed = low ^ half
    rest_part = jnp.concatenate(
        [slim_part, jnp.where(mixed == 0, down_part, down_got), jnp.where(mixed == 0, down_got, down_part)]
    )
    rest_part, wide_done = lax.optimization_barrier((rest_part, wide_done))
    wide_other = send(wide_done, TO_LOW)
    rest_done = plane_gather(rest_part)

    normed_back = own_back + send(before_back, TO_PREVIOUS).astype(F32)
    gain_in = gains[0, :640]
    inputs = hidden.astype(F32)
    part, _ = norm_back(inputs, gain_in, normed_back)
    input_gradient = (residual_back + part).astype(BF16)

    gate_out, up_out, output_out = call(
        finish_wide_kernel, [((160, FF), F32), ((160, FF), F32), ((256, D), F32)], [], 1_000_000, place, wide_done, wide_other
    )
    rest_out = call(
        finish_rest_kernel,
        [((160, 1024), F32), ((160, HD), F32), ((160, HD), F32), ((512, D), F32)]
        + [((160,), F32)] * 4 + [((64,), F32)] * 2,
        [], 1_000_000, place, rest_done,
    )
    return (
        layer_out.reshape(hidden_in.shape),
        input_gradient.reshape(hidden_in.shape),
        *rest_out[:3],
        output_out,
        gate_out,
        up_out,
        rest_out[3],
        *rest_out[4:],
    )


def solution(mesh):
    fine = Mesh(mesh.devices.reshape(SIZES), AXES)
    seq, fsdp = ("y", "x", "zl"), ("zh", "c")
    tokens, rows, line = P(fsdp, seq, None), P(fsdp, None), P(fsdp)
    placed = (tokens, tokens, P(fsdp, seq), P(fsdp, seq)) + (rows,) * 7 + (line,) * 6
    return jax.shard_map(
        shards,
        mesh=fine,
        in_specs=placed,
        out_specs=(tokens, tokens) + (rows,) * 7 + (line,) * 6,
        check_vma=False,
    )
```

```python
import jax
import jax.numpy as jnp
from jax import lax
from jax.experimental import pallas as pl
from jax.experimental.pallas import tpu as pltpu
from jax.sharding import Mesh, PartitionSpec as P

WINDOW = 512
EPSILON = 1e-06
ROPE_BASE = 10000.0
AXES = ("y", "x", "zl", "zh", "c")
SIZES = (4, 4, 2, 2, 2)
PLANE = ("y", "x")
T, D, HEADS, HD, FF = 512, 640, 4, 256, 2048
SCALE = HD ** (-0.5)
TILE = 128
SPAN = WINDOW + TILE
PART = 512
F32, BF16 = jnp.float32, jnp.bfloat16


def route(move):
    def index(y, x, zl, zh, c):
        return (((y * 4 + x) * 2 + zl) * 2 + zh) * 2 + c

    return [
        (index(y, x, zl, zh, c), index(*move(y, x, zl, zh, c)))
        for y in range(4)
        for x in range(4)
        for zl in range(2)
        for zh in range(2)
        for c in range(2)
    ]


TO_CORE = route(lambda y, x, zl, zh, c: (y, x, zl, zh, 1 - c))
TO_HALF = route(lambda y, x, zl, zh, c: (y, x, 1 - zl, 1 - zh, c))
TO_LOW = route(lambda y, x, zl, zh, c: (y, x, 1 - zl, zh, c))
TO_SAME = route(lambda y, x, zl, zh, c: (y, x, zl, 1 - zh, c))
TO_NEXT = [(i * 4 + f, i * 4 + 4 + f) for i in range(31) for f in range(4)]
TO_PREVIOUS = [(j, i) for i, j in TO_NEXT]


def send(block, pairs):
    return lax.ppermute(block, AXES, pairs)


def dot(left, right):
    return jnp.dot(left, right, preferred_element_type=F32)


def dot_nt(left, right):
    return lax.dot_general(left, right, (((1,), (1,)), ((), ())), preferred_element_type=F32)


def inverse_rms(values):
    return lax.rsqrt(jnp.mean(values * values, axis=-1, keepdims=True) + EPSILON)


def norm_back(values, gain, upstream):
    inverse = inverse_rms(values)
    unit = values * inverse
    scaled = upstream * gain
    back = inverse * (scaled - unit * jnp.mean(scaled * unit, axis=-1, keepdims=True))
    return back, upstream * unit


def turned(values, cosine, sine):
    first, second = values[:, : HD // 2], values[:, HD // 2 :]
    return jnp.concatenate([first * cosine - second * sine, second * cosine + first * sine], axis=-1)


BLOCK = 176


def pack_kernel(place, wq, wk, wv, g_in, g_att, g_feed, g_res, g_q, g_k, gate, up, first):
    me = place[0]
    for b in range(12):
        ref, at = ((wq, b), (wk, b - 8), (wv, b - 10))[(b >= 8) + (b >= 10)]
        first[BLOCK * b : BLOCK * b + 160, :] = ref[:, 128 * at : 128 * at + 128]

    def placed(upper, lower, width):
        count = upper.shape[0]
        rows = lax.broadcasted_iota(jnp.int32, (16, count), 0)
        both = jnp.where(rows == 0, upper[...].astype(F32)[None, :], jnp.where(rows == 1, lower[...].astype(F32)[None, :], 0.0))
        source = lax.broadcasted_iota(jnp.int32, (count, width), 0)
        target = lax.broadcasted_iota(jnp.int32, (count, width), 1)
        pick = jnp.where(target == source + me * count, 1.0, 0.0).astype(BF16)
        return dot(both.astype(BF16), pick).astype(BF16)

    at = 0
    for upper, lower, width in ((g_in, g_feed, 640), (g_att, g_res, 640), (g_q, g_k, 256)):
        row = placed(upper, lower, width)
        for b in range(width // 128):
            first[BLOCK * at + 160 : BLOCK * at + BLOCK, :] = row[:, 128 * b : 128 * b + 128]
            at += 1
    first[12 * BLOCK : 12 * BLOCK + 160, :] = gate[...]
    first[12 * BLOCK + 160 :, :] = up[...]


def project_kernel(place, own, own_c, far, far_c, before, here, cosine, sine,
                   weight, gains, normed, query_raw, key_raw, query_rot, key_rot, value_low):
    me = place[0]
    for turn, piece in enumerate((own, own_c, far, far_c)):
        for b in range(12):
            weight[pl.ds(pl.multiple_of((me ^ turn) * 160, 32), 160), 128 * b : 128 * b + 128] = piece[
                BLOCK * b : BLOCK * b + 160, :
            ]
    for b in range(12):
        gains[:, 128 * b : 128 * b + 128] = sum(
            piece[BLOCK * b + 160 : BLOCK * b + BLOCK, :].astype(F32) for piece in (own, own_c, far, far_c)
        )
    total = gains[...]
    gain_in, gain_q, gain_k = total[0:1, :640], total[0:1, 1280:], total[1:2, 1280:]
    for base, source in ((0, before), (T, here)):
        values = source[...].astype(F32)
        normed[base : base + T, :] = (values * inverse_rms(values) * gain_in).astype(BF16)
    for base in (0, T):
        low = normed[base : base + T, :]
        cos, sin = cosine[base : base + T, :], sine[base : base + T, :]
        raw = dot(low, weight[:, 1024:1280])
        key_raw[base : base + T, :] = raw
        key_rot[base : base + T, :] = turned(raw * inverse_rms(raw) * gain_k, cos, sin).astype(BF16)
        value_low[base : base + T, :] = dot(low, weight[:, 1280:]).astype(BF16)
    low = normed[T:, :]
    cos, sin = cosine[T:, :], sine[T:, :]
    for h in range(HEADS):
        cols = slice(h * HD, (h + 1) * HD)
        raw = dot(low, weight[:, cols])
        query_raw[:, cols] = raw
        query_rot[:, cols] = turned(raw * inverse_rms(raw) * gain_q, cos, sin).astype(BF16)


def stacked(ref, rows):
    return jnp.concatenate([ref[rows, h * HD : (h + 1) * HD] for h in range(HEADS)], axis=0)


def attend_kernel(query_rot, key_rot, value_low, codes, attended, probs):
    for i in range(T // TILE):
        rows, span = slice(i * TILE, (i + 1) * TILE), slice(i * TILE, i * TILE + SPAN)
        scores = dot_nt(stacked(query_rot, rows), key_rot[span, :]) * SCALE
        own = slice(T + i * TILE, T + (i + 1) * TILE)
        gap = jnp.broadcast_to(codes[:, own], (8, TILE)).T[:, 0:1] - codes[:, span]
        visible = (gap >= 0) & (gap < WINDOW)
        scores = jnp.where(visible[None], scores.reshape(HEADS, TILE, SPAN), -1e30)
        top = jnp.max(scores, axis=-1, keepdims=True)
        raised = jnp.exp(scores - top)
        weight = raised * (1.0 / jnp.sum(raised, axis=-1, keepdims=True))
        low = weight.reshape(HEADS * TILE, SPAN).astype(BF16)
        probs[i] = low
        out = dot(low, value_low[span, :])
        for h in range(HEADS):
            attended[rows, h * HD : (h + 1) * HD] = out[h * TILE : (h + 1) * TILE].astype(BF16)


GELU_A, GELU_B = 0.7978845608028654, 0.044715
ROWS = 480


def by_owner(ref, rows, core):
    for j in range(4):
        at = 2 * ((core + j) % 2) + j // 2
        ref[pl.ds(pl.multiple_of(at * 160, 32), 160), :] = rows[160 * j : 160 * j + 160, :]


def mix_kernel(place, hidden, attended, gains, wo_own, wo_c, wo_far, wo_far_c,
               wo, out_raw, residual, feed_in, turn_low):
    me = place[0]
    for turn, piece in enumerate((wo_own, wo_c, wo_far, wo_far_c)):
        wo[pl.ds(pl.multiple_of((me ^ turn) * 256, 256), 256), :] = piece[...]
    out = dot(attended[...], wo[...])
    out_raw[...] = out
    total = hidden[...].astype(F32) + out * inverse_rms(out) * gains[0:1, 640:1280]
    residual[...] = total
    low = (total * inverse_rms(total) * gains[1:2, :640]).astype(BF16)
    feed_in[...] = low
    by_owner(turn_low, low.T, place[2])


def feed_kernel(place, residual, cotangent, gains, feed_in, turn_low,
                g_own, u_own, d_own, g_c, u_c, d_c, far, far_c, d_far, d_far_c,
                layer_out, give, keep, feed_back, gain_back,
                wg, wu, wd, gate, up, activated, down_low):
    me, core = place[0], place[2]
    for turn, (g_p, u_p, d_p) in enumerate(((g_own, u_own, d_own), (g_c, u_c, d_c))):
        j = me ^ turn
        wg[pl.ds(pl.multiple_of(j * 160, 32), 160), :] = g_p[...]
        wu[pl.ds(pl.multiple_of(j * 160, 32), 160), :] = u_p[...]
        wd[pl.ds(pl.multiple_of(j * 512, 512), 512), :] = d_p[...]
    for turn, (piece, d_p) in enumerate(((far, d_far), (far_c, d_far_c))):
        j = me ^ (2 + turn)
        for k in range(16):
            cols = slice(128 * k, 128 * k + 128)
            wg[pl.ds(pl.multiple_of(j * 160, 32), 160), cols] = piece[k, 0:160, :]
            wu[pl.ds(pl.multiple_of(j * 160, 32), 160), cols] = piece[k, 160:320, :]
        wd[pl.ds(pl.multiple_of(j * 512, 512), 512), :] = d_p[...]
    gain_res = gains[1:2, 640:1280]

    def put(owner, write):
        pl.when(core == owner % 2)(lambda: write(keep))
        pl.when(core != owner % 2)(lambda: write(give))

    def forward(n, carry):
        cols = pl.ds(pl.multiple_of(n * PART, PART), PART)
        g = dot(feed_in[...], wg[:, cols])
        u = dot(feed_in[...], wu[:, cols])
        t = jnp.tanh(GELU_A * (g + GELU_B * g * g * g))
        half = 0.5 * (1.0 + t)
        slope = half + 0.5 * g * (1.0 - t * t) * (GELU_A * (1.0 + 3.0 * GELU_B * g * g))
        gelu = g * half
        gate[:, cols] = gelu
        up[:, cols] = u * slope
        activated[:, cols] = (gelu * u).astype(BF16)
        return carry

    lax.fori_loop(0, FF // PART, forward, 0)
    down_raw = dot(activated[...], wd[...])
    layer_out[...] = (residual[...] + down_raw * inverse_rms(down_raw) * gain_res).astype(BF16)
    upstream = cotangent[...].astype(F32)
    down_back, share = norm_back(down_raw, gain_res, upstream)
    gain_back[...] = jnp.broadcast_to(jnp.sum(share, axis=0, keepdims=True), (8, D))
    down_low[...] = down_back.astype(BF16)
    turn_down = down_low[...].T
    feed_back[...] = jnp.zeros_like(feed_back)

    def backward(n, carry):
        cols = pl.ds(pl.multiple_of(n * PART, PART), PART)
        act_back = dot_nt(down_low[...], wd[cols, :])
        gate_low = (act_back * up[:, cols]).astype(BF16)
        up_low = (act_back * gate[:, cols]).astype(BF16)
        feed_back[...] += dot_nt(gate_low, wg[:, cols]) + dot_nt(up_low, wu[:, cols])
        for base, low in ((0, gate_low), (160, up_low)):
            grad = dot(turn_low[...], low).astype(BF16)
            for i, ref in enumerate((keep, keep, give, give)):
                for b in range(PART // 128):
                    ref[n * (PART // 128) + b, i % 2, base : base + 160, :] = grad[
                        160 * i : 160 * i + 160, 128 * b : 128 * b + 128
                    ]
        grad = dot(turn_down, activated[:, cols]).astype(BF16)
        j = n // (512 // PART)
        first = (n % (512 // PART)) * (PART // 128)

        def write_down(ref):
            for b in range(PART // 128):
                for r in range(4):
                    ref[(first + b) * 4 + r, j // 2, 320:480, :] = grad[160 * r : 160 * r + 160, 128 * b : 128 * b + 128]
        put(j, write_down)
        return carry

    lax.fori_loop(0, FF // PART, backward, 0)


def output_kernel(place, cotangent, attended, gains, wo, out_raw, residual, feed_back, result_gain_back,
                  give, keep, attended_back, residual_back, gain_back):
    core = place[2]
    gain_att, gain_feed = gains[0:1, 640:1280], gains[1:2, :640]
    part, share = norm_back(residual[...], gain_feed, feed_back[...])
    gain_back[1:2, :] = jnp.sum(share, axis=0, keepdims=True)
    back = cotangent[...].astype(F32) + part
    residual_back[...] = back
    out_back, share = norm_back(out_raw[...], gain_att, back)
    gain_back[0:1, :] = jnp.sum(share, axis=0, keepdims=True)
    gain_back[2:, :] = result_gain_back[2:, :]
    out_low = out_back.astype(BF16)
    attended_back[...] = dot_nt(out_low, wo[...]).astype(BF16)
    turn_out = out_low.T
    for ref, side in ((keep, core), (give, 1 - core)):
        for z in range(2):
            cols = pl.ds(pl.multiple_of((2 * z + side) * 256, 256), 256)
            grad = dot(turn_out, attended[:, cols]).astype(BF16)
            for b in range(2):
                for r in range(8):
                    ref[8 * b + r, z, :, :] = grad[80 * r : 80 * r + 80, 128 * b : 128 * b + 128]


FEED_SCRATCH = [((D, FF), BF16), ((D, FF), BF16), ((FF, D), BF16), ((T, FF), F32), ((T, FF), F32),
                ((T, FF), BF16), ((T, D), BF16)]
FEED_OUTS = [((T, D), BF16), ((16, 2, ROWS, 128), BF16), ((16, 2, ROWS, 128), BF16), ((T, D), F32), ((8, D), F32)]
MIX_OUTS = [((1024, D), BF16), ((T, D), F32), ((T, D), F32), ((T, D), BF16), ((D, T), BF16)]
OUTPUT_OUTS = [((16, 2, 80, 128), BF16), ((16, 2, 80, 128), BF16), ((T, 1024), BF16), ((T, D), F32), ((8, D), F32)]


def back_kernel(query_rot, key_rot, value_low, probs, attended, attended_back,
                query_raw, key_raw, gains, cosine, sine, weight,
                query_low, pair_low, head_back, before_back, key_sum, value_sum):
    key_sum[...] = jnp.zeros_like(key_sum)
    value_sum[...] = jnp.zeros_like(value_sum)
    gain_q, gain_k = gains[0:1, 1280:], gains[1:2, 1280:]
    gain_q_back = jnp.zeros((1, HD), F32)
    for i in range(T // TILE):
        rows, span = slice(i * TILE, (i + 1) * TILE), slice(i * TILE, i * TILE + SPAN)
        back = stacked(attended_back, rows)
        delta = jnp.sum(back.astype(F32) * stacked(attended, rows).astype(F32), axis=-1, keepdims=True)
        prob = probs[i]
        prob_back = dot_nt(back, value_low[span, :])
        score_back = (prob.astype(F32) * (prob_back - delta)).astype(BF16)
        value_sum[:, span] += dot(back.T, prob)
        key_sum[:, span] += dot(stacked(query_rot, rows).T, score_back) * SCALE
        query_back = dot(score_back, key_rot[span, :]) * SCALE
        cos, sin = cosine[T + i * TILE : T + (i + 1) * TILE, :], sine[T + i * TILE : T + (i + 1) * TILE, :]
        for h in range(HEADS):
            unturned = turned(query_back[h * TILE : (h + 1) * TILE], cos, -sin)
            raw_back, share = norm_back(query_raw[rows, h * HD : (h + 1) * HD], gain_q, unturned)
            gain_q_back += jnp.sum(share, axis=0, keepdims=True)
            query_low[rows, h * HD : (h + 1) * HD] = raw_back.astype(BF16)
    raw_back, share = norm_back(key_raw[...], gain_k, turned(key_sum[...].T, cosine[...], -sine[...]))
    gain_k_back = jnp.sum(share, axis=0, keepdims=True)
    pair_low[:, :HD] = raw_back.astype(BF16)
    pair_low[:, HD:] = value_sum[...].T.astype(BF16)

    before_back[...] = dot_nt(pair_low[:T, :], weight[:, 1024:]).astype(BF16)
    rows = lax.broadcasted_iota(jnp.int32, (8, HD), 0)
    head_back[...] = jnp.where(rows == 0, gain_q_back, gain_k_back)


def first_kernel(place, normed, query_low, pair_low, weight, head_back, gain_back, before, here, before_back,
                 give, keep, own_back, turned_all):
    def store(grad, block):
        for i, ref in enumerate((keep, keep, give, give)):
            for b in range(grad.shape[1] // 128):
                ref[i % 2, 160 * (block + b) : 160 * (block + b) + 160, :] = grad[
                    160 * i : 160 * i + 160, 128 * b : 128 * b + 128
                ]

    by_owner(turned_all, normed[...].T, place[2])
    for h in range(2):
        store(dot(turned_all[:, T:], query_low[:, 512 * h : 512 * h + 512]).astype(BF16), 4 * h)
    store(dot(turned_all[...], pair_low[...]).astype(BF16), 8)

    earlier = before_back[...].astype(F32)
    later = dot_nt(pair_low[T:, :], weight[:, 1024:]) + dot_nt(query_low[...], weight[:, :1024])
    own_back[...] = later
    values, values_before = here[...].astype(F32), before[...].astype(F32)
    gain_in_back = jnp.sum(later * (values * inverse_rms(values)), axis=0, keepdims=True) + jnp.sum(
        earlier * (values_before * inverse_rms(values_before)), axis=0, keepdims=True
    )
    rows = lax.broadcasted_iota(jnp.int32, (128, 128), 0)
    block = jnp.zeros((128, 128), F32)
    lines = [gain_in_back] + [gain_back[r : r + 1, :] for r in range(3)] + [head_back[0:1, :], head_back[1:2, :]]
    at = 0
    for line in lines:
        for b in range(line.shape[1] // 128):
            block = jnp.where(rows == at, line[:, 128 * b : 128 * b + 128], block)
            at += 1
    low = block.astype(BF16)
    for j in range(2):
        keep[j, 1920:, :] = low
        give[j, 1920:, :] = low


MERGED = 4


def merge_kernel(place, keep, got, out_keep, out_got, wide, up_keep, up_give, down_keep, down_give):
    half, mixed = place[1], place[5]
    for k in range(MERGED):
        for z in range(2):
            def added(rows, k=k, z=z):
                return keep[k, z, rows, :].astype(F32) + got[k, z, rows, :].astype(F32)

            wide[k, z, :160, :] = added(slice(0, 160)).astype(BF16)
            wide[k, z, 160:240, :] = (out_keep[k, z].astype(F32) + out_got[k, z].astype(F32)).astype(BF16)
            wide[k, z, 240:, :] = jnp.zeros((16, 128), BF16)
            one, two = added(slice(320, 400)), added(slice(400, 480))
            down_keep[k, z] = jnp.where(mixed == 0, one, two).astype(BF16)
            down_give[k, z] = jnp.where(mixed == 0, two, one).astype(BF16)
        one, two = (keep[k, z, 160:320, :].astype(F32) + got[k, z, 160:320, :].astype(F32) for z in range(2))
        up_keep[k] = jnp.where(half == 0, one, two).astype(BF16)
        up_give[k] = jnp.where(half == 0, two, one).astype(BF16)


def merge(place, keep, got, out_keep, out_got):
    def spec(*shape):
        return pl.BlockSpec((MERGED, *shape), lambda i: (i,) + (0,) * len(shape))

    outs = [(2, 256, 128), (160, 128), (160, 128), (2, 80, 128), (2, 80, 128)]
    return pl.pallas_call(
        merge_kernel,
        grid=(16 // MERGED,),
        out_shape=[jax.ShapeDtypeStruct((16, *o), BF16) for o in outs],
        in_specs=[pl.BlockSpec(memory_space=pltpu.SMEM)] + [spec(2, 480, 128)] * 2 + [spec(2, 80, 128)] * 2,
        out_specs=[spec(*o) for o in outs],
        compiler_params=pltpu.CompilerParams(vmem_limit_bytes=60 * 2**20),
        cost_estimate=pl.CostEstimate(flops=1_000_000, bytes_accessed=1_000_000, transcendentals=0),
    )(place, keep, got, out_keep, out_got)


def line_kernel(place, up_keep, up_got, down_keep, down_got, up_next, up_give, down_next, down_give):
    half, low = place[1], place[4]

    def parted(one, two, choice, stay, leave):
        stay[...] = jnp.where(choice == 0, one, two).astype(BF16)
        leave[...] = jnp.where(choice == 0, two, one).astype(BF16)

    one, two = (up_keep[:, r : r + 80, :].astype(F32) + up_got[:, r : r + 80, :].astype(F32) for r in (0, 80))
    parted(one, two, low, up_next, up_give)
    one, two = (down_keep[:, z].astype(F32) + down_got[:, z].astype(F32) for z in range(2))
    parted(one, two, half, down_next, down_give)


def rest_kernel(keep, got, up_keep, up_got, down_keep, down_got, rest):
    for z in range(2):
        for k in range(16):
            rows = slice(128 * k, 128 * k + 128)
            rest[k, 128 * z : 128 * z + 128, :] = (keep[z, rows, :].astype(F32) + got[z, rows, :].astype(F32)).astype(BF16)
    rest[:, 256:336, :] = (up_keep[...].astype(F32) + up_got[...].astype(F32)).astype(BF16)
    rest[:, 336:, :] = (down_keep[...].astype(F32) + down_got[...].astype(F32)).astype(BF16)


def finish_wide_kernel(place, own, other, gate, up, out):
    low = place[4]
    blocks = []
    for k in range(16):
        cols = slice(128 * k, 128 * k + 128)
        mine, theirs = own[k].astype(F32), other[k].astype(F32)
        one = jnp.where(low == 0, mine, theirs)
        two = jnp.where(low == 0, theirs, mine)
        gate[:128, cols] = one[:128]
        gate[128:, cols] = two[:32]
        up[:80, cols] = one[128:]
        up[80:, cols] = two[128:]
        blocks.append(two[32:112])
    for b in range(2):
        out[128 * b : 128 * b + 128, :] = jnp.concatenate(blocks[8 * b : 8 * b + 8], axis=0).T


def finish_rest_kernel(place, done, query, key, value, down, *gains):
    me = place[0]
    for b in range(4):
        block = jnp.concatenate([done[4 * b + r, 128:288, :] for r in range(4)], axis=0)
        down[128 * b : 128 * b + 128, :] = block.astype(F32).T
    for block in range(12):
        ref, at = ((query, block), (key, block - 8), (value, block - 10))[(block >= 8) + (block >= 10)]
        row = 0
        while row < 160:
            flat = 160 * block + row
            chunk, start = flat // 128, flat % 128
            size = min(160 - row, 128 - start)
            ref[row : row + size, 128 * at : 128 * at + 128] = done[chunk, start : start + size, :].astype(F32)
            row += size
    lines = done[15, 0:32, :]

    def pick(count, size):
        parts = []
        for b in range(count):
            source = lax.broadcasted_iota(jnp.int32, (128, size), 0) + 128 * b
            target = lax.broadcasted_iota(jnp.int32, (128, size), 1) + me * size
            parts.append(dot(lines, jnp.where(source == target, 1.0, 0.0).astype(BF16)))
        return parts

    for i, ref in enumerate(gains[:4]):
        parts = pick(5, 160) if i == 0 else parts
        ref[...] = sum(parts[b][5 * i + b : 5 * i + b + 1, :] for b in range(5)).reshape(160)
    parts = pick(2, 64)
    for i, ref in enumerate(gains[4:]):
        ref[...] = sum(parts[b][20 + 2 * i + b : 21 + 2 * i + b, :] for b in range(2)).reshape(64)


def call(kernel, outs, scratch, flops, *args):
    spec = [pl.BlockSpec(memory_space=pltpu.SMEM)] + [pl.BlockSpec(memory_space=pltpu.VMEM)] * (len(args) - 1)
    if kernel in (attend_kernel, rest_kernel, back_kernel):
        spec = [pl.BlockSpec(memory_space=pltpu.VMEM)] * len(args)
    shapes = [jax.ShapeDtypeStruct(s, d) for s, d in outs]
    size = sum(a.size * a.dtype.itemsize for a in args) + sum(s.size * s.dtype.itemsize for s in shapes)
    return pl.pallas_call(
        kernel,
        out_shape=shapes,
        in_specs=spec,
        out_specs=[pl.BlockSpec(memory_space=pltpu.VMEM)] * len(shapes),
        scratch_shapes=[pltpu.VMEM(s, d) for s, d in scratch],
        compiler_params=pltpu.CompilerParams(vmem_limit_bytes=60 * 2**20),
        cost_estimate=pl.CostEstimate(flops=flops, bytes_accessed=min(size, flops), transcendentals=0),
    )(*args)


def pick(block, index, axis):
    return lax.dynamic_index_in_dim(block, index, axis, keepdims=False)


def add(*terms):
    return sum(t.astype(F32) for t in terms).astype(BF16)


def plane_swap(chunks):
    return lax.all_to_all(chunks, PLANE, 0, 0)


def plane_total(chunks):
    return jnp.sum(chunks.astype(F32), axis=0)


def plane_gather(chunk):
    return lax.all_to_all(jnp.broadcast_to(chunk[None], (16,) + chunk.shape), PLANE, 0, 0)


def line_sum(part, half):
    keep, give = pick(part, half, 0).astype(BF16), pick(part, 1 - half, 0).astype(BF16)
    return add(keep, send(keep, TO_LOW), send(give, TO_HALF), send(give, TO_SAME))


def shards(
    hidden_in, cotangent, segments, positions,
    query_weight, key_weight, value_weight, output_weight, gate_weight, up_weight, down_weight,
    input_norm, attention_norm, feed_norm, result_norm, query_norm, key_norm,
):
    half, core, low = lax.axis_index("zh"), lax.axis_index("c"), lax.axis_index("zl")
    me = half * 2 + core
    spot = lax.axis_index("y") * 4 + lax.axis_index("x")
    place = jnp.stack([me, half, core, spot, low, low ^ half]).astype(jnp.int32)
    hidden = hidden_in.reshape(T, D)
    code = (segments * 65536 + positions).reshape(T) + 2**20

    gain_rows = [input_norm, attention_norm, feed_norm, result_norm, query_norm, key_norm]
    whole = pl.BlockSpec(memory_space=pltpu.VMEM)
    (first,) = pl.pallas_call(
        pack_kernel,
        out_shape=[jax.ShapeDtypeStruct((12 * BLOCK + 320, 128), BF16)],
        grid_spec=pltpu.PrefetchScalarGridSpec(
            num_scalar_prefetch=1,
            grid=(1,),
            in_specs=[pl.BlockSpec(a.shape, lambda i, s: (0, 0)) for a in (query_weight, key_weight, value_weight)]
            + [pl.BlockSpec(a.shape, lambda i, s: (0,)) for a in gain_rows]
            + [
                pl.BlockSpec((160, 128), lambda i, s: (0, s[3])),
                pl.BlockSpec((160, 128), lambda i, s: (0, s[3])),
            ],
            out_specs=[
                pl.BlockSpec((12 * BLOCK + 320, 128), lambda i, s: (0, 0)),
            ],
        ),
        compiler_params=pltpu.CompilerParams(vmem_limit_bytes=60 * 2**20),
    )(place, query_weight, key_weight, value_weight, *gain_rows, gate_weight, up_weight)

    first_far = send(first, TO_HALF)
    hidden_before = send(hidden, TO_NEXT)
    code_before = send(code, TO_NEXT)
    first_core = send(first, TO_CORE)
    codes = jnp.concatenate([code_before, code])
    own_places = positions.reshape(T)
    places = jnp.concatenate([own_places[0] - T + jnp.arange(T, dtype=jnp.int32), own_places])
    freqs = jnp.exp(-jnp.log(ROPE_BASE) * jnp.arange(HD // 2, dtype=F32) * 2.0 / HD)
    angles = places.astype(F32)[:, None] * freqs
    cosine, sine = jnp.cos(angles), jnp.sin(angles)
    first_far, hidden_before, codes, cosine, sine, output_late, down_late = lax.optimization_barrier(
        (first_far, hidden_before, codes, cosine, sine, output_weight, down_weight)
    )
    first_far_core = send(first_far, TO_CORE)
    far = plane_gather(first_far[12 * BLOCK :])
    out_far = send(output_late, TO_HALF)
    down_far = send(down_late, TO_HALF)
    out_core, gate_core, up_core, down_core = (
        send(w, TO_CORE) for w in (output_weight, gate_weight, up_weight, down_weight)
    )

    weight, gains, normed, query_raw, key_raw, query_rot, key_rot, value_low = call(
        project_kernel,
        [((D, 1536), BF16), ((16, 1536), F32), ((2 * T, D), BF16), ((T, 1024), F32), ((2 * T, HD), F32),
         ((T, 1024), BF16), ((2 * T, HD), BF16), ((2 * T, HD), BF16)],
        [],
        1_000_000,
        place, first, first_core, first_far, first_far_core, hidden_before, hidden, cosine, sine,
    )
    query_rot, out_core, gate_core, up_core, down_core, out_far = lax.optimization_barrier(
        (query_rot, out_core, gate_core, up_core, down_core, out_far)
    )
    out_far_core = send(out_far, TO_CORE)
    attended, probs = call(
        attend_kernel,
        [((T, 1024), BF16), ((T // TILE, HEADS * TILE, SPAN), BF16)],
        [],
        1_000_000,
        query_rot, key_rot, value_low, codes.reshape(1, 2 * T),
    )
    attended, out_far_core, down_far = lax.optimization_barrier((attended, out_far_core, down_far))
    down_far_core = send(down_far, TO_CORE)
    wo, out_raw, residual, feed_in, turn_low = call(
        mix_kernel, MIX_OUTS, [], 1_000_000,
        place, hidden, attended, gains, output_weight, out_core, out_far, out_far_core,
    )
    far, down_far_core, feed_in = lax.optimization_barrier((far, down_far_core, feed_in))
    layer_out, give, keep, feed_back, result_gain_back = call(
        feed_kernel, FEED_OUTS, FEED_SCRATCH, 1_000_000,
        place, residual, cotangent.reshape(T, D), gains, feed_in, turn_low,
        gate_weight, up_weight, down_weight, gate_core, up_core, down_core,
        far, send(far, TO_CORE), down_far, down_far_core,
    )
    out_give, out_keep, attended_back, residual_back, gain_back = call(
        output_kernel, OUTPUT_OUTS, [], 1_000_000,
        place, cotangent.reshape(T, D), attended, gains, wo, out_raw, residual, feed_back, result_gain_back,
    )
    got = send(give, TO_CORE)
    out_got = send(out_give, TO_CORE)
    wide, up_keep, up_give, down_keep, down_give, attended_back = lax.optimization_barrier(
        (*merge(place, keep, got, out_keep, out_got), attended_back)
    )
    wide_got = plane_swap(wide)
    up_got, down_got = send(up_give, TO_HALF), send(down_give, TO_LOW)
    query_low, pair_low, head_back, before_back = call(
        back_kernel,
        [((T, 1024), BF16), ((2 * T, 512), BF16), ((8, HD), F32), ((T, D), BF16)],
        [((HD, 2 * T), F32), ((HD, 2 * T), F32)],
        1_000_000,
        query_rot, key_rot, value_low, probs, attended, attended_back, query_raw, key_raw, gains, cosine, sine, weight,
    )
    up_keep, up_give, down_keep, down_give = call(
        line_kernel, [((16, 80, 128), BF16)] * 4, [], 0, place, up_keep, up_got, down_keep, down_got
    )
    query_low, up_keep, up_give, down_keep, down_give = lax.optimization_barrier(
        (query_low, up_keep, up_give, down_keep, down_give)
    )
    up_got, down_got = send(up_give, TO_LOW), send(down_give, TO_HALF)
    first_give, first_keep, own_back = call(
        first_kernel,
        [((2, 2048, 128), BF16), ((2, 2048, 128), BF16), ((T, D), F32)],
        [((D, 2 * T), BF16)],
        1_000_000,
        place, normed, query_low, pair_low, weight, head_back, gain_back, hidden_before, hidden, before_back,
    )
    first_give, up_got, down_got, before_back = lax.optimization_barrier((first_give, up_got, down_got, before_back))
    returned = send(before_back, TO_PREVIOUS)
    (rest,) = call(
        rest_kernel, [((16, 416, 128), BF16)], [], 0,
        first_keep, send(first_give, TO_CORE), up_keep, up_got, down_keep, down_got,
    )
    rest, wide_got = lax.optimization_barrier((rest, wide_got))
    rest_got = plane_swap(rest)
    wide_part = plane_total(wide_got).reshape(2, 2, 128, 128)
    near, away = pick(wide_part, half, 0), pick(wide_part, 1 - half, 0)
    wide_part = add(
        pick(near, low, 0),
        send(pick(near, 1 - low, 0).astype(BF16), TO_LOW),
        send(pick(away, 1 - low, 0).astype(BF16), TO_HALF),
        send(pick(away, low, 0).astype(BF16), TO_SAME),
    )
    wide_part, rest_got, returned = lax.optimization_barrier((wide_part, rest_got, returned))
    rest_part = plane_total(rest_got)
    wide_done = plane_gather(jnp.concatenate([wide_part, rest_part[256:336].astype(BF16)]))
    down_part = rest_part[336:].astype(BF16)
    down_got = send(down_part, TO_LOW)
    slim_part = line_sum(rest_part[:256].reshape(2, 128, 128), half)
    mixed = low ^ half
    rest_part = jnp.concatenate(
        [slim_part, jnp.where(mixed == 0, down_part, down_got), jnp.where(mixed == 0, down_got, down_part)]
    )
    wide_other = send(wide_done, TO_LOW)
    rest_part, wide_done = lax.optimization_barrier((rest_part, wide_done))
    rest_done = plane_gather(rest_part)

    normed_back = own_back + returned.astype(F32)
    gain_in = gains[0, :640]
    inputs = hidden.astype(F32)
    part, _ = norm_back(inputs, gain_in, normed_back)
    input_gradient = (residual_back + part).astype(BF16)

    gate_out, up_out, output_out = call(
        finish_wide_kernel, [((160, FF), F32), ((160, FF), F32), ((256, D), F32)], [], 1_000_000, place, wide_done, wide_other
    )
    rest_out = call(
        finish_rest_kernel,
        [((160, 1024), F32), ((160, HD), F32), ((160, HD), F32), ((512, D), F32)]
        + [((160,), F32)] * 4 + [((64,), F32)] * 2,
        [], 1_000_000, place, rest_done,
    )
    return (
        layer_out.reshape(hidden_in.shape),
        input_gradient.reshape(hidden_in.shape),
        *rest_out[:3],
        output_out,
        gate_out,
        up_out,
        rest_out[3],
        *rest_out[4:],
    )


def solution(mesh):
    fine = Mesh(mesh.devices.reshape(SIZES), AXES)
    seq, fsdp = ("y", "x", "zl"), ("zh", "c")
    tokens, rows, line = P(fsdp, seq, None), P(fsdp, None), P(fsdp)
    placed = (tokens, tokens, P(fsdp, seq), P(fsdp, seq)) + (rows,) * 7 + (line,) * 6
    return jax.shard_map(
        shards,
        mesh=fine,
        in_specs=placed,
        out_specs=(tokens, tokens) + (rows,) * 7 + (line,) * 6,
        check_vma=False,
    )
```

```python
import jax
import jax.numpy as jnp
from jax import lax
from jax.experimental import pallas as pl
from jax.experimental.pallas import tpu as pltpu
from jax.sharding import Mesh, PartitionSpec as P

WINDOW = 512
EPSILON = 1e-06
ROPE_BASE = 10000.0
AXES = ("y", "x", "zl", "zh", "c")
SIZES = (4, 4, 2, 2, 2)
PLANE = ("y", "x")
T, D, HEADS, HD, FF = 512, 640, 4, 256, 2048
SCALE = HD ** (-0.5)
TILE = 128
SPAN = WINDOW + TILE
PART = 512
F32, BF16 = jnp.float32, jnp.bfloat16


def route(move):
    def index(y, x, zl, zh, c):
        return (((y * 4 + x) * 2 + zl) * 2 + zh) * 2 + c

    return [
        (index(y, x, zl, zh, c), index(*move(y, x, zl, zh, c)))
        for y in range(4)
        for x in range(4)
        for zl in range(2)
        for zh in range(2)
        for c in range(2)
    ]


TO_CORE = route(lambda y, x, zl, zh, c: (y, x, zl, zh, 1 - c))
TO_HALF = route(lambda y, x, zl, zh, c: (y, x, 1 - zl, 1 - zh, c))
TO_LOW = route(lambda y, x, zl, zh, c: (y, x, 1 - zl, zh, c))
TO_SAME = route(lambda y, x, zl, zh, c: (y, x, zl, 1 - zh, c))
TO_NEXT = [(i * 4 + f, i * 4 + 4 + f) for i in range(31) for f in range(4)]
TO_PREVIOUS = [(j, i) for i, j in TO_NEXT]
TO_PREVIOUS_PAIR = [(i * 8 + 12 + f, i * 8 + 4 + f) for i in range(15) for f in range(4)]


def send(block, pairs):
    return lax.ppermute(block, AXES, pairs)


def dot(left, right):
    return jnp.dot(left, right, preferred_element_type=F32)


def dot_nt(left, right):
    return lax.dot_general(left, right, (((1,), (1,)), ((), ())), preferred_element_type=F32)


def inverse_rms(values):
    return lax.rsqrt(jnp.mean(values * values, axis=-1, keepdims=True) + EPSILON)


def norm_back(values, gain, upstream):
    inverse = inverse_rms(values)
    unit = values * inverse
    scaled = upstream * gain
    back = inverse * (scaled - unit * jnp.mean(scaled * unit, axis=-1, keepdims=True))
    return back, upstream * unit


def turned(values, cosine, sine):
    first, second = values[:, : HD // 2], values[:, HD // 2 :]
    return jnp.concatenate([first * cosine - second * sine, second * cosine + first * sine], axis=-1)


BLOCK = 176


def pack_kernel(place, wq, wk, wv, g_in, g_att, g_feed, g_res, g_q, g_k, gate, up, first):
    me = place[0]
    for b in range(12):
        ref, at = ((wq, b), (wk, b - 8), (wv, b - 10))[(b >= 8) + (b >= 10)]
        first[BLOCK * b : BLOCK * b + 160, :] = ref[:, 128 * at : 128 * at + 128]

    def placed(upper, lower, width):
        count = upper.shape[0]
        rows = lax.broadcasted_iota(jnp.int32, (16, count), 0)
        both = jnp.where(rows == 0, upper[...].astype(F32)[None, :], jnp.where(rows == 1, lower[...].astype(F32)[None, :], 0.0))
        source = lax.broadcasted_iota(jnp.int32, (count, width), 0)
        target = lax.broadcasted_iota(jnp.int32, (count, width), 1)
        pick = jnp.where(target == source + me * count, 1.0, 0.0).astype(BF16)
        return dot(both.astype(BF16), pick).astype(BF16)

    at = 0
    for upper, lower, width in ((g_in, g_feed, 640), (g_att, g_res, 640), (g_q, g_k, 256)):
        row = placed(upper, lower, width)
        for b in range(width // 128):
            first[BLOCK * at + 160 : BLOCK * at + BLOCK, :] = row[:, 128 * b : 128 * b + 128]
            at += 1
    first[12 * BLOCK : 12 * BLOCK + 160, :] = gate[...]
    first[12 * BLOCK + 160 :, :] = up[...]


def project_kernel(place, own, own_c, far, far_c, before, here, cosine, sine,
                   weight, gains, normed, query_raw, key_raw, query_rot, key_rot, value_low):
    me = place[0]
    for turn, piece in enumerate((own, own_c, far, far_c)):
        for b in range(12):
            weight[pl.ds(pl.multiple_of((me ^ turn) * 160, 32), 160), 128 * b : 128 * b + 128] = piece[
                BLOCK * b : BLOCK * b + 160, :
            ]
    for b in range(12):
        gains[:, 128 * b : 128 * b + 128] = sum(
            piece[BLOCK * b + 160 : BLOCK * b + BLOCK, :].astype(F32) for piece in (own, own_c, far, far_c)
        )
    total = gains[...]
    gain_in, gain_q, gain_k = total[0:1, :640], total[0:1, 1280:], total[1:2, 1280:]
    for base, source in ((0, before), (T, here)):
        values = source[...].astype(F32)
        normed[base : base + T, :] = (values * inverse_rms(values) * gain_in).astype(BF16)
    for base in (0, T):
        low = normed[base : base + T, :]
        cos, sin = cosine[base : base + T, :], sine[base : base + T, :]
        raw = dot(low, weight[:, 1024:1280])
        key_raw[base : base + T, :] = raw
        key_rot[base : base + T, :] = turned(raw * inverse_rms(raw) * gain_k, cos, sin).astype(BF16)
        value_low[base : base + T, :] = dot(low, weight[:, 1280:]).astype(BF16)
    low = normed[T:, :]
    cos, sin = cosine[T:, :], sine[T:, :]
    for h in range(HEADS):
        cols = slice(h * HD, (h + 1) * HD)
        raw = dot(low, weight[:, cols])
        query_raw[:, cols] = raw
        query_rot[:, cols] = turned(raw * inverse_rms(raw) * gain_q, cos, sin).astype(BF16)


def stacked(ref, rows):
    return jnp.concatenate([ref[rows, h * HD : (h + 1) * HD] for h in range(HEADS)], axis=0)


def attend_kernel(query_rot, key_rot, value_low, codes, attended, probs):
    for i in range(T // TILE):
        rows, span = slice(i * TILE, (i + 1) * TILE), slice(i * TILE, i * TILE + SPAN)
        scores = dot_nt(stacked(query_rot, rows), key_rot[span, :]) * SCALE
        own = slice(T + i * TILE, T + (i + 1) * TILE)
        gap = jnp.broadcast_to(codes[:, own], (8, TILE)).T[:, 0:1] - codes[:, span]
        visible = (gap >= 0) & (gap < WINDOW)
        scores = jnp.where(visible[None], scores.reshape(HEADS, TILE, SPAN), -1e30)
        top = jnp.max(scores, axis=-1, keepdims=True)
        raised = jnp.exp(scores - top)
        weight = raised * (1.0 / jnp.sum(raised, axis=-1, keepdims=True))
        low = weight.reshape(HEADS * TILE, SPAN).astype(BF16)
        probs[i] = low
        out = dot(low, value_low[span, :])
        for h in range(HEADS):
            attended[rows, h * HD : (h + 1) * HD] = out[h * TILE : (h + 1) * TILE].astype(BF16)


GELU_A, GELU_B = 0.7978845608028654, 0.044715
ROWS = 480


def by_owner(ref, rows, core):
    for j in range(4):
        at = 2 * ((core + j) % 2) + j // 2
        ref[pl.ds(pl.multiple_of(at * 160, 32), 160), :] = rows[160 * j : 160 * j + 160, :]


def mix_kernel(place, hidden, attended, gains, wo_own, wo_c, wo_far, wo_far_c,
               wo, out_raw, residual, feed_in, turn_low):
    me = place[0]
    for turn, piece in enumerate((wo_own, wo_c, wo_far, wo_far_c)):
        wo[pl.ds(pl.multiple_of((me ^ turn) * 256, 256), 256), :] = piece[...]
    out = dot(attended[...], wo[...])
    out_raw[...] = out
    total = hidden[...].astype(F32) + out * inverse_rms(out) * gains[0:1, 640:1280]
    residual[...] = total
    low = (total * inverse_rms(total) * gains[1:2, :640]).astype(BF16)
    feed_in[...] = low
    by_owner(turn_low, low.T, place[2])


def feed_kernel(place, residual, cotangent, gains, feed_in, turn_low,
                g_own, u_own, d_own, g_c, u_c, d_c, far, far_c, d_far, d_far_c,
                layer_out, give, keep, feed_back, gain_back,
                wg, wu, wd, gate, up, activated, down_low):
    me, core = place[0], place[2]
    for turn, (g_p, u_p, d_p) in enumerate(((g_own, u_own, d_own), (g_c, u_c, d_c))):
        j = me ^ turn
        wg[pl.ds(pl.multiple_of(j * 160, 32), 160), :] = g_p[...]
        wu[pl.ds(pl.multiple_of(j * 160, 32), 160), :] = u_p[...]
        wd[pl.ds(pl.multiple_of(j * 512, 512), 512), :] = d_p[...]
    for turn, (piece, d_p) in enumerate(((far, d_far), (far_c, d_far_c))):
        j = me ^ (2 + turn)
        for k in range(16):
            cols = slice(128 * k, 128 * k + 128)
            wg[pl.ds(pl.multiple_of(j * 160, 32), 160), cols] = piece[k, 0:160, :]
            wu[pl.ds(pl.multiple_of(j * 160, 32), 160), cols] = piece[k, 160:320, :]
        wd[pl.ds(pl.multiple_of(j * 512, 512), 512), :] = d_p[...]
    gain_res = gains[1:2, 640:1280]

    def put(owner, write):
        pl.when(core == owner % 2)(lambda: write(keep))
        pl.when(core != owner % 2)(lambda: write(give))

    def forward(n, carry):
        cols = pl.ds(pl.multiple_of(n * PART, PART), PART)
        g = dot(feed_in[...], wg[:, cols])
        u = dot(feed_in[...], wu[:, cols])
        t = jnp.tanh(GELU_A * (g + GELU_B * g * g * g))
        half = 0.5 * (1.0 + t)
        slope = half + 0.5 * g * (1.0 - t * t) * (GELU_A * (1.0 + 3.0 * GELU_B * g * g))
        gelu = g * half
        gate[:, cols] = gelu
        up[:, cols] = u * slope
        activated[:, cols] = (gelu * u).astype(BF16)
        return carry

    lax.fori_loop(0, FF // PART, forward, 0)
    down_raw = dot(activated[...], wd[...])
    layer_out[...] = (residual[...] + down_raw * inverse_rms(down_raw) * gain_res).astype(BF16)
    upstream = cotangent[...].astype(F32)
    down_back, share = norm_back(down_raw, gain_res, upstream)
    gain_back[...] = jnp.broadcast_to(jnp.sum(share, axis=0, keepdims=True), (8, D))
    down_low[...] = down_back.astype(BF16)
    turn_down = down_low[...].T
    feed_back[...] = jnp.zeros_like(feed_back)

    def backward(n, carry):
        cols = pl.ds(pl.multiple_of(n * PART, PART), PART)
        act_back = dot_nt(down_low[...], wd[cols, :])
        gate_low = (act_back * up[:, cols]).astype(BF16)
        up_low = (act_back * gate[:, cols]).astype(BF16)
        feed_back[...] += dot_nt(gate_low, wg[:, cols]) + dot_nt(up_low, wu[:, cols])
        for base, low in ((0, gate_low), (160, up_low)):
            grad = dot(turn_low[...], low).astype(BF16)
            for i, ref in enumerate((keep, keep, give, give)):
                for b in range(PART // 128):
                    ref[n * (PART // 128) + b, i % 2, base : base + 160, :] = grad[
                        160 * i : 160 * i + 160, 128 * b : 128 * b + 128
                    ]
        grad = dot(turn_down, activated[:, cols]).astype(BF16)
        j = n // (512 // PART)
        first = (n % (512 // PART)) * (PART // 128)

        def write_down(ref):
            for b in range(PART // 128):
                for r in range(4):
                    ref[(first + b) * 4 + r, j // 2, 320:480, :] = grad[160 * r : 160 * r + 160, 128 * b : 128 * b + 128]
        put(j, write_down)
        return carry

    lax.fori_loop(0, FF // PART, backward, 0)


def output_kernel(place, cotangent, attended, gains, wo, out_raw, residual, feed_back, result_gain_back,
                  give, keep, attended_back, residual_back, gain_back):
    core = place[2]
    gain_att, gain_feed = gains[0:1, 640:1280], gains[1:2, :640]
    part, share = norm_back(residual[...], gain_feed, feed_back[...])
    gain_back[1:2, :] = jnp.sum(share, axis=0, keepdims=True)
    back = cotangent[...].astype(F32) + part
    residual_back[...] = back
    out_back, share = norm_back(out_raw[...], gain_att, back)
    gain_back[0:1, :] = jnp.sum(share, axis=0, keepdims=True)
    gain_back[2:, :] = result_gain_back[2:, :]
    out_low = out_back.astype(BF16)
    attended_back[...] = dot_nt(out_low, wo[...]).astype(BF16)
    turn_out = out_low.T
    for ref, side in ((keep, core), (give, 1 - core)):
        for z in range(2):
            cols = pl.ds(pl.multiple_of((2 * z + side) * 256, 256), 256)
            grad = dot(turn_out, attended[:, cols]).astype(BF16)
            for b in range(2):
                for r in range(8):
                    ref[8 * b + r, z, :, :] = grad[80 * r : 80 * r + 80, 128 * b : 128 * b + 128]


FEED_SCRATCH = [((D, FF), BF16), ((D, FF), BF16), ((FF, D), BF16), ((T, FF), F32), ((T, FF), F32),
                ((T, FF), BF16), ((T, D), BF16)]
FEED_OUTS = [((T, D), BF16), ((16, 2, ROWS, 128), BF16), ((16, 2, ROWS, 128), BF16), ((T, D), F32), ((8, D), F32)]
MIX_OUTS = [((1024, D), BF16), ((T, D), F32), ((T, D), F32), ((T, D), BF16), ((D, T), BF16)]
OUTPUT_OUTS = [((16, 2, 80, 128), BF16), ((16, 2, 80, 128), BF16), ((T, 1024), BF16), ((T, D), F32), ((8, D), F32)]


def back_kernel(query_rot, key_rot, value_low, probs, attended, attended_back,
                query_raw, key_raw, gains, cosine, sine, weight,
                query_low, pair_low, head_back, before_back, key_sum, value_sum):
    key_sum[...] = jnp.zeros_like(key_sum)
    value_sum[...] = jnp.zeros_like(value_sum)
    gain_q, gain_k = gains[0:1, 1280:], gains[1:2, 1280:]
    gain_q_back = jnp.zeros((1, HD), F32)
    for i in range(T // TILE):
        rows, span = slice(i * TILE, (i + 1) * TILE), slice(i * TILE, i * TILE + SPAN)
        back = stacked(attended_back, rows)
        delta = jnp.sum(back.astype(F32) * stacked(attended, rows).astype(F32), axis=-1, keepdims=True)
        prob = probs[i]
        prob_back = dot_nt(back, value_low[span, :])
        score_back = (prob.astype(F32) * (prob_back - delta)).astype(BF16)
        value_sum[:, span] += dot(back.T, prob)
        key_sum[:, span] += dot(stacked(query_rot, rows).T, score_back) * SCALE
        query_back = dot(score_back, key_rot[span, :]) * SCALE
        cos, sin = cosine[T + i * TILE : T + (i + 1) * TILE, :], sine[T + i * TILE : T + (i + 1) * TILE, :]
        for h in range(HEADS):
            unturned = turned(query_back[h * TILE : (h + 1) * TILE], cos, -sin)
            raw_back, share = norm_back(query_raw[rows, h * HD : (h + 1) * HD], gain_q, unturned)
            gain_q_back += jnp.sum(share, axis=0, keepdims=True)
            query_low[rows, h * HD : (h + 1) * HD] = raw_back.astype(BF16)
    raw_back, share = norm_back(key_raw[...], gain_k, turned(key_sum[...].T, cosine[...], -sine[...]))
    gain_k_back = jnp.sum(share, axis=0, keepdims=True)
    pair_low[:, :HD] = raw_back.astype(BF16)
    pair_low[:, HD:] = value_sum[...].T.astype(BF16)

    before_back[...] = dot_nt(pair_low[:T, :], weight[:, 1024:]).astype(BF16)
    rows = lax.broadcasted_iota(jnp.int32, (8, HD), 0)
    head_back[...] = jnp.where(rows == 0, gain_q_back, gain_k_back)


def first_kernel(place, normed, query_low, pair_low, weight, head_back, gain_back, before, here, before_back,
                 give, keep, own_back, turned_all):
    def store(grad, block):
        for i, ref in enumerate((keep, keep, give, give)):
            for b in range(grad.shape[1] // 128):
                ref[i % 2, 160 * (block + b) : 160 * (block + b) + 160, :] = grad[
                    160 * i : 160 * i + 160, 128 * b : 128 * b + 128
                ]

    by_owner(turned_all, normed[...].T, place[2])
    for h in range(2):
        store(dot(turned_all[:, T:], query_low[:, 512 * h : 512 * h + 512]).astype(BF16), 4 * h)
    store(dot(turned_all[...], pair_low[...]).astype(BF16), 8)

    earlier = before_back[...].astype(F32)
    later = dot_nt(pair_low[T:, :], weight[:, 1024:]) + dot_nt(query_low[...], weight[:, :1024])
    own_back[...] = later
    values, values_before = here[...].astype(F32), before[...].astype(F32)
    gain_in_back = jnp.sum(later * (values * inverse_rms(values)), axis=0, keepdims=True) + jnp.sum(
        earlier * (values_before * inverse_rms(values_before)), axis=0, keepdims=True
    )
    rows = lax.broadcasted_iota(jnp.int32, (128, 128), 0)
    block = jnp.zeros((128, 128), F32)
    lines = [gain_in_back] + [gain_back[r : r + 1, :] for r in range(3)] + [head_back[0:1, :], head_back[1:2, :]]
    at = 0
    for line in lines:
        for b in range(line.shape[1] // 128):
            block = jnp.where(rows == at, line[:, 128 * b : 128 * b + 128], block)
            at += 1
    low = block.astype(BF16)
    for j in range(2):
        keep[j, 1920:, :] = low
        give[j, 1920:, :] = low


MERGED = 4


def merge_kernel(place, keep, got, out_keep, out_got, wide, up_keep, up_give, down_keep, down_give):
    half, mixed = place[1], place[5]
    for k in range(MERGED):
        for z in range(2):
            def added(rows, k=k, z=z):
                return keep[k, z, rows, :].astype(F32) + got[k, z, rows, :].astype(F32)

            wide[k, z, :160, :] = added(slice(0, 160)).astype(BF16)
            wide[k, z, 160:240, :] = (out_keep[k, z].astype(F32) + out_got[k, z].astype(F32)).astype(BF16)
            wide[k, z, 240:, :] = jnp.zeros((16, 128), BF16)
            one, two = added(slice(320, 400)), added(slice(400, 480))
            down_keep[k, z] = jnp.where(mixed == 0, one, two).astype(BF16)
            down_give[k, z] = jnp.where(mixed == 0, two, one).astype(BF16)
        one, two = (keep[k, z, 160:320, :].astype(F32) + got[k, z, 160:320, :].astype(F32) for z in range(2))
        up_keep[k] = jnp.where(half == 0, one, two).astype(BF16)
        up_give[k] = jnp.where(half == 0, two, one).astype(BF16)


def merge(place, keep, got, out_keep, out_got):
    def spec(*shape):
        return pl.BlockSpec((MERGED, *shape), lambda i: (i,) + (0,) * len(shape))

    outs = [(2, 256, 128), (160, 128), (160, 128), (2, 80, 128), (2, 80, 128)]
    return pl.pallas_call(
        merge_kernel,
        grid=(16 // MERGED,),
        out_shape=[jax.ShapeDtypeStruct((16, *o), BF16) for o in outs],
        in_specs=[pl.BlockSpec(memory_space=pltpu.SMEM)] + [spec(2, 480, 128)] * 2 + [spec(2, 80, 128)] * 2,
        out_specs=[spec(*o) for o in outs],
        compiler_params=pltpu.CompilerParams(vmem_limit_bytes=60 * 2**20),
        cost_estimate=pl.CostEstimate(flops=1_000_000, bytes_accessed=1_000_000, transcendentals=0),
    )(place, keep, got, out_keep, out_got)


def line_kernel(place, up_keep, up_got, down_keep, down_got, up_next, up_give, down_next, down_give):
    half, low = place[1], place[4]

    def parted(one, two, choice, stay, leave):
        stay[...] = jnp.where(choice == 0, one, two).astype(BF16)
        leave[...] = jnp.where(choice == 0, two, one).astype(BF16)

    one, two = (up_keep[:, r : r + 80, :].astype(F32) + up_got[:, r : r + 80, :].astype(F32) for r in (0, 80))
    parted(one, two, low, up_next, up_give)
    one, two = (down_keep[:, z].astype(F32) + down_got[:, z].astype(F32) for z in range(2))
    parted(one, two, half, down_next, down_give)


def rest_kernel(keep, got, up_keep, up_got, down_keep, down_got, rest):
    for z in range(2):
        for k in range(16):
            rows = slice(128 * k, 128 * k + 128)
            rest[k, 128 * z : 128 * z + 128, :] = (keep[z, rows, :].astype(F32) + got[z, rows, :].astype(F32)).astype(BF16)
    rest[:, 256:336, :] = (up_keep[...].astype(F32) + up_got[...].astype(F32)).astype(BF16)
    rest[:, 336:, :] = (down_keep[...].astype(F32) + down_got[...].astype(F32)).astype(BF16)


def finish_wide_kernel(place, own, other, gate, up, out):
    low = place[4]
    blocks = []
    for k in range(16):
        cols = slice(128 * k, 128 * k + 128)
        mine, theirs = own[k].astype(F32), other[k].astype(F32)
        one = jnp.where(low == 0, mine, theirs)
        two = jnp.where(low == 0, theirs, mine)
        gate[:128, cols] = one[:128]
        gate[128:, cols] = two[:32]
        up[:80, cols] = one[128:]
        up[80:, cols] = two[128:]
        blocks.append(two[32:112])
    for b in range(2):
        out[128 * b : 128 * b + 128, :] = jnp.concatenate(blocks[8 * b : 8 * b + 8], axis=0).T


def finish_rest_kernel(place, done, query, key, value, down, *gains):
    me = place[0]
    for b in range(4):
        block = jnp.concatenate([done[4 * b + r, 128:288, :] for r in range(4)], axis=0)
        down[128 * b : 128 * b + 128, :] = block.astype(F32).T
    for block in range(12):
        ref, at = ((query, block), (key, block - 8), (value, block - 10))[(block >= 8) + (block >= 10)]
        row = 0
        while row < 160:
            flat = 160 * block + row
            chunk, start = flat // 128, flat % 128
            size = min(160 - row, 128 - start)
            ref[row : row + size, 128 * at : 128 * at + 128] = done[chunk, start : start + size, :].astype(F32)
            row += size
    lines = done[15, 0:32, :]

    def pick(count, size):
        parts = []
        for b in range(count):
            source = lax.broadcasted_iota(jnp.int32, (128, size), 0) + 128 * b
            target = lax.broadcasted_iota(jnp.int32, (128, size), 1) + me * size
            parts.append(dot(lines, jnp.where(source == target, 1.0, 0.0).astype(BF16)))
        return parts

    for i, ref in enumerate(gains[:4]):
        parts = pick(5, 160) if i == 0 else parts
        ref[...] = sum(parts[b][5 * i + b : 5 * i + b + 1, :] for b in range(5)).reshape(160)
    parts = pick(2, 64)
    for i, ref in enumerate(gains[4:]):
        ref[...] = sum(parts[b][20 + 2 * i + b : 21 + 2 * i + b, :] for b in range(2)).reshape(64)


def call(kernel, outs, scratch, flops, *args):
    spec = [pl.BlockSpec(memory_space=pltpu.SMEM)] + [pl.BlockSpec(memory_space=pltpu.VMEM)] * (len(args) - 1)
    if kernel in (attend_kernel, rest_kernel, back_kernel):
        spec = [pl.BlockSpec(memory_space=pltpu.VMEM)] * len(args)
    shapes = [jax.ShapeDtypeStruct(s, d) for s, d in outs]
    size = sum(a.size * a.dtype.itemsize for a in args) + sum(s.size * s.dtype.itemsize for s in shapes)
    return pl.pallas_call(
        kernel,
        out_shape=shapes,
        in_specs=spec,
        out_specs=[pl.BlockSpec(memory_space=pltpu.VMEM)] * len(shapes),
        scratch_shapes=[pltpu.VMEM(s, d) for s, d in scratch],
        compiler_params=pltpu.CompilerParams(vmem_limit_bytes=60 * 2**20),
        cost_estimate=pl.CostEstimate(flops=flops, bytes_accessed=min(size, flops), transcendentals=0),
    )(*args)


def pick(block, index, axis):
    return lax.dynamic_index_in_dim(block, index, axis, keepdims=False)


def add(*terms):
    return sum(t.astype(F32) for t in terms).astype(BF16)


def plane_swap(chunks):
    return lax.all_to_all(chunks, PLANE, 0, 0)


def plane_total(chunks):
    return jnp.sum(chunks.astype(F32), axis=0)


def plane_gather(chunk):
    return lax.all_to_all(jnp.broadcast_to(chunk[None], (16,) + chunk.shape), PLANE, 0, 0)


def line_sum(part, half):
    keep, give = pick(part, half, 0).astype(BF16), pick(part, 1 - half, 0).astype(BF16)
    return add(keep, send(keep, TO_LOW), send(give, TO_HALF), send(give, TO_SAME))


def shards(
    hidden_in, cotangent, segments, positions,
    query_weight, key_weight, value_weight, output_weight, gate_weight, up_weight, down_weight,
    input_norm, attention_norm, feed_norm, result_norm, query_norm, key_norm,
):
    half, core, low = lax.axis_index("zh"), lax.axis_index("c"), lax.axis_index("zl")
    me = half * 2 + core
    spot = lax.axis_index("y") * 4 + lax.axis_index("x")
    place = jnp.stack([me, half, core, spot, low, low ^ half]).astype(jnp.int32)
    hidden = hidden_in.reshape(T, D)
    code = (segments * 65536 + positions).reshape(T) + 2**20

    gain_rows = [input_norm, attention_norm, feed_norm, result_norm, query_norm, key_norm]
    whole = pl.BlockSpec(memory_space=pltpu.VMEM)
    (first,) = pl.pallas_call(
        pack_kernel,
        out_shape=[jax.ShapeDtypeStruct((12 * BLOCK + 320, 128), BF16)],
        grid_spec=pltpu.PrefetchScalarGridSpec(
            num_scalar_prefetch=1,
            grid=(1,),
            in_specs=[pl.BlockSpec(a.shape, lambda i, s: (0, 0)) for a in (query_weight, key_weight, value_weight)]
            + [pl.BlockSpec(a.shape, lambda i, s: (0,)) for a in gain_rows]
            + [
                pl.BlockSpec((160, 128), lambda i, s: (0, s[3])),
                pl.BlockSpec((160, 128), lambda i, s: (0, s[3])),
            ],
            out_specs=[
                pl.BlockSpec((12 * BLOCK + 320, 128), lambda i, s: (0, 0)),
            ],
        ),
        compiler_params=pltpu.CompilerParams(vmem_limit_bytes=60 * 2**20),
    )(place, query_weight, key_weight, value_weight, *gain_rows, gate_weight, up_weight)

    first_far = send(first, TO_HALF)
    hidden_before = send(hidden, TO_NEXT)
    code_before = send(code, TO_NEXT)
    first_core = send(first, TO_CORE)
    codes = jnp.concatenate([code_before, code])
    own_places = positions.reshape(T)
    places = jnp.concatenate([own_places[0] - T + jnp.arange(T, dtype=jnp.int32), own_places])
    freqs = jnp.exp(-jnp.log(ROPE_BASE) * jnp.arange(HD // 2, dtype=F32) * 2.0 / HD)
    angles = places.astype(F32)[:, None] * freqs
    cosine, sine = jnp.cos(angles), jnp.sin(angles)
    first_far, hidden_before, codes, cosine, sine, output_late, down_late = lax.optimization_barrier(
        (first_far, hidden_before, codes, cosine, sine, output_weight, down_weight)
    )
    first_far_core = send(first_far, TO_CORE)
    far = plane_gather(first_far[12 * BLOCK :])
    out_far = send(output_late, TO_HALF)
    down_far = send(down_late, TO_HALF)
    out_core, gate_core, up_core, down_core = (
        send(w, TO_CORE) for w in (output_weight, gate_weight, up_weight, down_weight)
    )

    weight, gains, normed, query_raw, key_raw, query_rot, key_rot, value_low = call(
        project_kernel,
        [((D, 1536), BF16), ((16, 1536), F32), ((2 * T, D), BF16), ((T, 1024), F32), ((2 * T, HD), F32),
         ((T, 1024), BF16), ((2 * T, HD), BF16), ((2 * T, HD), BF16)],
        [],
        1_000_000,
        place, first, first_core, first_far, first_far_core, hidden_before, hidden, cosine, sine,
    )
    query_rot, out_core, gate_core, up_core, down_core, out_far = lax.optimization_barrier(
        (query_rot, out_core, gate_core, up_core, down_core, out_far)
    )
    out_far_core = send(out_far, TO_CORE)
    attended, probs = call(
        attend_kernel,
        [((T, 1024), BF16), ((T // TILE, HEADS * TILE, SPAN), BF16)],
        [],
        1_000_000,
        query_rot, key_rot, value_low, codes.reshape(1, 2 * T),
    )
    attended, out_far_core, down_far = lax.optimization_barrier((attended, out_far_core, down_far))
    down_far_core = send(down_far, TO_CORE)
    wo, out_raw, residual, feed_in, turn_low = call(
        mix_kernel, MIX_OUTS, [], 1_000_000,
        place, hidden, attended, gains, output_weight, out_core, out_far, out_far_core,
    )
    far, down_far_core, feed_in = lax.optimization_barrier((far, down_far_core, feed_in))
    layer_out, give, keep, feed_back, result_gain_back = call(
        feed_kernel, FEED_OUTS, FEED_SCRATCH, 1_000_000,
        place, residual, cotangent.reshape(T, D), gains, feed_in, turn_low,
        gate_weight, up_weight, down_weight, gate_core, up_core, down_core,
        far, send(far, TO_CORE), down_far, down_far_core,
    )
    out_give, out_keep, attended_back, residual_back, gain_back = call(
        output_kernel, OUTPUT_OUTS, [], 1_000_000,
        place, cotangent.reshape(T, D), attended, gains, wo, out_raw, residual, feed_back, result_gain_back,
    )
    got = send(give, TO_CORE)
    out_got = send(out_give, TO_CORE)
    wide, up_keep, up_give, down_keep, down_give, attended_back = lax.optimization_barrier(
        (*merge(place, keep, got, out_keep, out_got), attended_back)
    )
    wide_got = plane_swap(wide)
    up_got, down_got = send(up_give, TO_HALF), send(down_give, TO_LOW)
    query_low, pair_low, head_back, before_back = call(
        back_kernel,
        [((T, 1024), BF16), ((2 * T, 512), BF16), ((8, HD), F32), ((T, D), BF16)],
        [((HD, 2 * T), F32), ((HD, 2 * T), F32)],
        1_000_000,
        query_rot, key_rot, value_low, probs, attended, attended_back, query_raw, key_raw, gains, cosine, sine, weight,
    )
    up_keep, up_give, down_keep, down_give = call(
        line_kernel, [((16, 80, 128), BF16)] * 4, [], 0, place, up_keep, up_got, down_keep, down_got
    )
    query_low, up_keep, up_give, down_keep, down_give = lax.optimization_barrier(
        (query_low, up_keep, up_give, down_keep, down_give)
    )
    up_got, down_got = send(up_give, TO_LOW), send(down_give, TO_HALF)
    first_give, first_keep, own_back = call(
        first_kernel,
        [((2, 2048, 128), BF16), ((2, 2048, 128), BF16), ((T, D), F32)],
        [((D, 2 * T), BF16)],
        1_000_000,
        place, normed, query_low, pair_low, weight, head_back, gain_back, hidden_before, hidden, before_back,
    )
    first_give, up_got, down_got, before_back = lax.optimization_barrier((first_give, up_got, down_got, before_back))
    returned = send(before_back[: T // 2], TO_PREVIOUS)
    crossed = send(before_back[T // 2 :], TO_LOW)
    passed = send(crossed, TO_PREVIOUS_PAIR)
    (rest,) = call(
        rest_kernel, [((16, 416, 128), BF16)], [], 0,
        first_keep, send(first_give, TO_CORE), up_keep, up_got, down_keep, down_got,
    )
    rest, wide_got = lax.optimization_barrier((rest, wide_got))
    rest_got = plane_swap(rest)
    wide_part = plane_total(wide_got).reshape(2, 2, 128, 128)
    near, away = pick(wide_part, half, 0), pick(wide_part, 1 - half, 0)
    wide_part = add(
        pick(near, low, 0),
        send(pick(near, 1 - low, 0).astype(BF16), TO_LOW),
        send(pick(away, 1 - low, 0).astype(BF16), TO_HALF),
        send(pick(away, low, 0).astype(BF16), TO_SAME),
    )
    returned = jnp.concatenate([returned, jnp.where(low == 0, crossed, passed)])
    wide_part, rest_got, returned = lax.optimization_barrier((wide_part, rest_got, returned))
    rest_part = plane_total(rest_got)
    wide_done = plane_gather(jnp.concatenate([wide_part, rest_part[256:336].astype(BF16)]))
    down_part = rest_part[336:].astype(BF16)
    down_got = send(down_part, TO_LOW)
    slim_part = line_sum(rest_part[:256].reshape(2, 128, 128), half)
    mixed = low ^ half
    rest_part = jnp.concatenate(
        [slim_part, jnp.where(mixed == 0, down_part, down_got), jnp.where(mixed == 0, down_got, down_part)]
    )
    wide_other = send(wide_done, TO_LOW)
    rest_part, wide_done = lax.optimization_barrier((rest_part, wide_done))
    rest_done = plane_gather(rest_part)

    normed_back = own_back + returned.astype(F32)
    gain_in = gains[0, :640]
    inputs = hidden.astype(F32)
    part, _ = norm_back(inputs, gain_in, normed_back)
    input_gradient = (residual_back + part).astype(BF16)

    gate_out, up_out, output_out = call(
        finish_wide_kernel, [((160, FF), F32), ((160, FF), F32), ((256, D), F32)], [], 1_000_000, place, wide_done, wide_other
    )
    rest_out = call(
        finish_rest_kernel,
        [((160, 1024), F32), ((160, HD), F32), ((160, HD), F32), ((512, D), F32)]
        + [((160,), F32)] * 4 + [((64,), F32)] * 2,
        [], 1_000_000, place, rest_done,
    )
    return (
        layer_out.reshape(hidden_in.shape),
        input_gradient.reshape(hidden_in.shape),
        *rest_out[:3],
        output_out,
        gate_out,
        up_out,
        rest_out[3],
        *rest_out[4:],
    )


def solution(mesh):
    fine = Mesh(mesh.devices.reshape(SIZES), AXES)
    seq, fsdp = ("y", "x", "zl"), ("zh", "c")
    tokens, rows, line = P(fsdp, seq, None), P(fsdp, None), P(fsdp)
    placed = (tokens, tokens, P(fsdp, seq), P(fsdp, seq)) + (rows,) * 7 + (line,) * 6
    return jax.shard_map(
        shards,
        mesh=fine,
        in_specs=placed,
        out_specs=(tokens, tokens) + (rows,) * 7 + (line,) * 6,
        check_vma=False,
    )
```

```python
import jax
import jax.numpy as jnp
from jax import lax
from jax.experimental import pallas as pl
from jax.experimental.pallas import tpu as pltpu
from jax.sharding import Mesh, PartitionSpec as P

WINDOW = 512
EPSILON = 1e-06
ROPE_BASE = 10000.0
AXES = ("y", "x", "zl", "zh", "c")
SIZES = (4, 4, 2, 2, 2)
PLANE = ("y", "x")
T, D, HEADS, HD, FF = 512, 640, 4, 256, 2048
SCALE = HD ** (-0.5)
TILE = 128
SPAN = WINDOW + TILE
PART = 512
F32, BF16 = jnp.float32, jnp.bfloat16


def route(move):
    def index(y, x, zl, zh, c):
        return (((y * 4 + x) * 2 + zl) * 2 + zh) * 2 + c

    return [
        (index(y, x, zl, zh, c), index(*move(y, x, zl, zh, c)))
        for y in range(4)
        for x in range(4)
        for zl in range(2)
        for zh in range(2)
        for c in range(2)
    ]


TO_CORE = route(lambda y, x, zl, zh, c: (y, x, zl, zh, 1 - c))
TO_HALF = route(lambda y, x, zl, zh, c: (y, x, 1 - zl, 1 - zh, c))
TO_LOW = route(lambda y, x, zl, zh, c: (y, x, 1 - zl, zh, c))
TO_SAME = route(lambda y, x, zl, zh, c: (y, x, zl, 1 - zh, c))
TO_NEXT = [(i * 4 + f, i * 4 + 4 + f) for i in range(31) for f in range(4)]
TO_PREVIOUS = [(j, i) for i, j in TO_NEXT]
TO_PREVIOUS_PAIR = [(i * 8 + 12 + f, i * 8 + 4 + f) for i in range(15) for f in range(4)]


def send(block, pairs):
    return lax.ppermute(block, AXES, pairs)


def dot(left, right):
    return jnp.dot(left, right, preferred_element_type=F32)


def dot_nt(left, right):
    return lax.dot_general(left, right, (((1,), (1,)), ((), ())), preferred_element_type=F32)


def inverse_rms(values):
    return lax.rsqrt(jnp.mean(values * values, axis=-1, keepdims=True) + EPSILON)


def norm_back(values, gain, upstream):
    inverse = inverse_rms(values)
    unit = values * inverse
    scaled = upstream * gain
    back = inverse * (scaled - unit * jnp.mean(scaled * unit, axis=-1, keepdims=True))
    return back, upstream * unit


def turned(values, cosine, sine):
    first, second = values[:, : HD // 2], values[:, HD // 2 :]
    return jnp.concatenate([first * cosine - second * sine, second * cosine + first * sine], axis=-1)


BLOCK = 176


def pack_kernel(place, wq, wk, wv, g_in, g_att, g_feed, g_res, g_q, g_k, gate, up, first):
    me = place[0]
    for b in range(12):
        ref, at = ((wq, b), (wk, b - 8), (wv, b - 10))[(b >= 8) + (b >= 10)]
        first[BLOCK * b : BLOCK * b + 160, :] = ref[:, 128 * at : 128 * at + 128]

    def placed(upper, lower, width):
        count = upper.shape[0]
        rows = lax.broadcasted_iota(jnp.int32, (16, count), 0)
        both = jnp.where(rows == 0, upper[...].astype(F32)[None, :], jnp.where(rows == 1, lower[...].astype(F32)[None, :], 0.0))
        source = lax.broadcasted_iota(jnp.int32, (count, width), 0)
        target = lax.broadcasted_iota(jnp.int32, (count, width), 1)
        pick = jnp.where(target == source + me * count, 1.0, 0.0).astype(BF16)
        return dot(both.astype(BF16), pick).astype(BF16)

    at = 0
    for upper, lower, width in ((g_in, g_feed, 640), (g_att, g_res, 640), (g_q, g_k, 256)):
        row = placed(upper, lower, width)
        for b in range(width // 128):
            first[BLOCK * at + 160 : BLOCK * at + BLOCK, :] = row[:, 128 * b : 128 * b + 128]
            at += 1
    first[12 * BLOCK : 12 * BLOCK + 160, :] = gate[...]
    first[12 * BLOCK + 160 :, :] = up[...]


def project_kernel(place, own, own_c, far, far_c, before, here, cosine, sine,
                   weight, gains, normed, query_raw, key_raw, query_rot, key_rot, value_low):
    me = place[0]
    for turn, piece in enumerate((own, own_c, far, far_c)):
        for b in range(12):
            weight[pl.ds(pl.multiple_of((me ^ turn) * 160, 32), 160), 128 * b : 128 * b + 128] = piece[
                BLOCK * b : BLOCK * b + 160, :
            ]
    for b in range(12):
        gains[:, 128 * b : 128 * b + 128] = sum(
            piece[BLOCK * b + 160 : BLOCK * b + BLOCK, :].astype(F32) for piece in (own, own_c, far, far_c)
        )
    total = gains[...]
    gain_in, gain_q, gain_k = total[0:1, :640], total[0:1, 1280:], total[1:2, 1280:]
    for base, source in ((0, before), (T, here)):
        values = source[...].astype(F32)
        normed[base : base + T, :] = (values * inverse_rms(values) * gain_in).astype(BF16)
    for base in (0, T):
        low = normed[base : base + T, :]
        cos, sin = cosine[base : base + T, :], sine[base : base + T, :]
        raw = dot(low, weight[:, 1024:1280])
        key_raw[base : base + T, :] = raw
        key_rot[base : base + T, :] = turned(raw * inverse_rms(raw) * gain_k, cos, sin).astype(BF16)
        value_low[base : base + T, :] = dot(low, weight[:, 1280:]).astype(BF16)
    low = normed[T:, :]
    cos, sin = cosine[T:, :], sine[T:, :]
    for h in range(HEADS):
        cols = slice(h * HD, (h + 1) * HD)
        raw = dot(low, weight[:, cols])
        query_raw[:, cols] = raw
        query_rot[:, cols] = turned(raw * inverse_rms(raw) * gain_q, cos, sin).astype(BF16)


def stacked(ref, rows):
    return jnp.concatenate([ref[rows, h * HD : (h + 1) * HD] for h in range(HEADS)], axis=0)


def attend_kernel(query_rot, key_rot, value_low, codes, attended, probs):
    for i in range(T // TILE):
        rows, span = slice(i * TILE, (i + 1) * TILE), slice(i * TILE, i * TILE + SPAN)
        scores = dot_nt(stacked(query_rot, rows), key_rot[span, :]) * SCALE
        own = slice(T + i * TILE, T + (i + 1) * TILE)
        gap = jnp.broadcast_to(codes[:, own], (8, TILE)).T[:, 0:1] - codes[:, span]
        visible = (gap >= 0) & (gap < WINDOW)
        scores = jnp.where(visible[None], scores.reshape(HEADS, TILE, SPAN), -1e30)
        top = jnp.max(scores, axis=-1, keepdims=True)
        raised = jnp.exp(scores - top)
        weight = raised * (1.0 / jnp.sum(raised, axis=-1, keepdims=True))
        low = weight.reshape(HEADS * TILE, SPAN).astype(BF16)
        probs[i] = low
        out = dot(low, value_low[span, :])
        for h in range(HEADS):
            attended[rows, h * HD : (h + 1) * HD] = out[h * TILE : (h + 1) * TILE].astype(BF16)


GELU_A, GELU_B = 0.7978845608028654, 0.044715
ROWS = 480


def by_owner(ref, rows, core):
    for j in range(4):
        at = 2 * ((core + j) % 2) + j // 2
        ref[pl.ds(pl.multiple_of(at * 160, 32), 160), :] = rows[160 * j : 160 * j + 160, :]


def mix_kernel(place, hidden, attended, gains, wo_own, wo_c, wo_far, wo_far_c,
               wo, out_raw, residual, feed_in, turn_low):
    me = place[0]
    for turn, piece in enumerate((wo_own, wo_c, wo_far, wo_far_c)):
        wo[pl.ds(pl.multiple_of((me ^ turn) * 256, 256), 256), :] = piece[...]
    out = dot(attended[...], wo[...])
    out_raw[...] = out
    total = hidden[...].astype(F32) + out * inverse_rms(out) * gains[0:1, 640:1280]
    residual[...] = total
    low = (total * inverse_rms(total) * gains[1:2, :640]).astype(BF16)
    feed_in[...] = low
    by_owner(turn_low, low.T, place[2])


def feed_kernel(place, residual, cotangent, gains, feed_in, turn_low,
                g_own, u_own, d_own, g_c, u_c, d_c, far, far_c, d_far, d_far_c,
                layer_out, give, keep, feed_back, gain_back,
                wg, wu, wd, gate, up, activated, down_low):
    me, core = place[0], place[2]
    for turn, (g_p, u_p, d_p) in enumerate(((g_own, u_own, d_own), (g_c, u_c, d_c))):
        j = me ^ turn
        wg[pl.ds(pl.multiple_of(j * 160, 32), 160), :] = g_p[...]
        wu[pl.ds(pl.multiple_of(j * 160, 32), 160), :] = u_p[...]
        wd[pl.ds(pl.multiple_of(j * 512, 512), 512), :] = d_p[...]
    for turn, (piece, d_p) in enumerate(((far, d_far), (far_c, d_far_c))):
        j = me ^ (2 + turn)
        for k in range(16):
            cols = slice(128 * k, 128 * k + 128)
            wg[pl.ds(pl.multiple_of(j * 160, 32), 160), cols] = piece[k, 0:160, :]
            wu[pl.ds(pl.multiple_of(j * 160, 32), 160), cols] = piece[k, 160:320, :]
        wd[pl.ds(pl.multiple_of(j * 512, 512), 512), :] = d_p[...]
    gain_res = gains[1:2, 640:1280]

    def put(owner, write):
        pl.when(core == owner % 2)(lambda: write(keep))
        pl.when(core != owner % 2)(lambda: write(give))

    def forward(n, carry):
        cols = pl.ds(pl.multiple_of(n * PART, PART), PART)
        g = dot(feed_in[...], wg[:, cols])
        u = dot(feed_in[...], wu[:, cols])
        t = jnp.tanh(GELU_A * (g + GELU_B * g * g * g))
        half = 0.5 * (1.0 + t)
        slope = half + 0.5 * g * (1.0 - t * t) * (GELU_A * (1.0 + 3.0 * GELU_B * g * g))
        gelu = g * half
        gate[:, cols] = gelu
        up[:, cols] = u * slope
        activated[:, cols] = (gelu * u).astype(BF16)
        return carry

    lax.fori_loop(0, FF // PART, forward, 0)
    down_raw = dot(activated[...], wd[...])
    layer_out[...] = (residual[...] + down_raw * inverse_rms(down_raw) * gain_res).astype(BF16)
    upstream = cotangent[...].astype(F32)
    down_back, share = norm_back(down_raw, gain_res, upstream)
    gain_back[...] = jnp.broadcast_to(jnp.sum(share, axis=0, keepdims=True), (8, D))
    down_low[...] = down_back.astype(BF16)
    turn_down = down_low[...].T
    feed_back[...] = jnp.zeros_like(feed_back)

    def backward(n, carry):
        cols = pl.ds(pl.multiple_of(n * PART, PART), PART)
        act_back = dot_nt(down_low[...], wd[cols, :])
        gate_low = (act_back * up[:, cols]).astype(BF16)
        up_low = (act_back * gate[:, cols]).astype(BF16)
        feed_back[...] += dot_nt(gate_low, wg[:, cols]) + dot_nt(up_low, wu[:, cols])
        for base, low in ((0, gate_low), (160, up_low)):
            grad = dot(turn_low[...], low).astype(BF16)
            for i, ref in enumerate((keep, keep, give, give)):
                for b in range(PART // 128):
                    ref[n * (PART // 128) + b, i % 2, base : base + 160, :] = grad[
                        160 * i : 160 * i + 160, 128 * b : 128 * b + 128
                    ]
        grad = dot(turn_down, activated[:, cols]).astype(BF16)
        j = n // (512 // PART)
        first = (n % (512 // PART)) * (PART // 128)

        def write_down(ref):
            for b in range(PART // 128):
                for r in range(4):
                    ref[(first + b) * 4 + r, j // 2, 320:480, :] = grad[160 * r : 160 * r + 160, 128 * b : 128 * b + 128]
        put(j, write_down)
        return carry

    lax.fori_loop(0, FF // PART, backward, 0)


def output_kernel(place, cotangent, attended, gains, wo, out_raw, residual, feed_back, result_gain_back,
                  give, keep, attended_back, residual_back, gain_back):
    core = place[2]
    gain_att, gain_feed = gains[0:1, 640:1280], gains[1:2, :640]
    part, share = norm_back(residual[...], gain_feed, feed_back[...])
    gain_back[1:2, :] = jnp.sum(share, axis=0, keepdims=True)
    back = cotangent[...].astype(F32) + part
    residual_back[...] = back
    out_back, share = norm_back(out_raw[...], gain_att, back)
    gain_back[0:1, :] = jnp.sum(share, axis=0, keepdims=True)
    gain_back[2:, :] = result_gain_back[2:, :]
    out_low = out_back.astype(BF16)
    attended_back[...] = dot_nt(out_low, wo[...]).astype(BF16)
    turn_out = out_low.T
    for ref, side in ((keep, core), (give, 1 - core)):
        for z in range(2):
            cols = pl.ds(pl.multiple_of((2 * z + side) * 256, 256), 256)
            grad = dot(turn_out, attended[:, cols]).astype(BF16)
            for b in range(2):
                for r in range(8):
                    ref[8 * b + r, z, :, :] = grad[80 * r : 80 * r + 80, 128 * b : 128 * b + 128]


FEED_SCRATCH = [((D, FF), BF16), ((D, FF), BF16), ((FF, D), BF16), ((T, FF), F32), ((T, FF), F32),
                ((T, FF), BF16), ((T, D), BF16)]
FEED_OUTS = [((T, D), BF16), ((16, 2, ROWS, 128), BF16), ((16, 2, ROWS, 128), BF16), ((T, D), F32), ((8, D), F32)]
MIX_OUTS = [((1024, D), BF16), ((T, D), F32), ((T, D), F32), ((T, D), BF16), ((D, T), BF16)]
OUTPUT_OUTS = [((16, 2, 80, 128), BF16), ((16, 2, 80, 128), BF16), ((T, 1024), BF16), ((T, D), F32), ((8, D), F32)]


def back_kernel(query_rot, key_rot, value_low, probs, attended, attended_back,
                query_raw, key_raw, gains, cosine, sine, weight,
                query_low, pair_low, head_back, before_back, key_sum, value_sum):
    key_sum[...] = jnp.zeros_like(key_sum)
    value_sum[...] = jnp.zeros_like(value_sum)
    gain_q, gain_k = gains[0:1, 1280:], gains[1:2, 1280:]
    gain_q_back = jnp.zeros((1, HD), F32)
    for i in range(T // TILE):
        rows, span = slice(i * TILE, (i + 1) * TILE), slice(i * TILE, i * TILE + SPAN)
        back = stacked(attended_back, rows)
        delta = jnp.sum(back.astype(F32) * stacked(attended, rows).astype(F32), axis=-1, keepdims=True)
        prob = probs[i]
        prob_back = dot_nt(back, value_low[span, :])
        score_back = (prob.astype(F32) * (prob_back - delta)).astype(BF16)
        value_sum[:, span] += dot(back.T, prob)
        key_sum[:, span] += dot(stacked(query_rot, rows).T, score_back) * SCALE
        query_back = dot(score_back, key_rot[span, :]) * SCALE
        cos, sin = cosine[T + i * TILE : T + (i + 1) * TILE, :], sine[T + i * TILE : T + (i + 1) * TILE, :]
        for h in range(HEADS):
            unturned = turned(query_back[h * TILE : (h + 1) * TILE], cos, -sin)
            raw_back, share = norm_back(query_raw[rows, h * HD : (h + 1) * HD], gain_q, unturned)
            gain_q_back += jnp.sum(share, axis=0, keepdims=True)
            query_low[rows, h * HD : (h + 1) * HD] = raw_back.astype(BF16)
    raw_back, share = norm_back(key_raw[...], gain_k, turned(key_sum[...].T, cosine[...], -sine[...]))
    gain_k_back = jnp.sum(share, axis=0, keepdims=True)
    pair_low[:, :HD] = raw_back.astype(BF16)
    pair_low[:, HD:] = value_sum[...].T.astype(BF16)

    before_back[...] = dot_nt(pair_low[:T, :], weight[:, 1024:]).astype(BF16)
    rows = lax.broadcasted_iota(jnp.int32, (8, HD), 0)
    head_back[...] = jnp.where(rows == 0, gain_q_back, gain_k_back)


def first_kernel(place, normed, query_low, pair_low, weight, head_back, gain_back, before, here, before_back,
                 give, keep, own_back, turned_all):
    def store(grad, block):
        for i, ref in enumerate((keep, keep, give, give)):
            for b in range(grad.shape[1] // 128):
                ref[i % 2, 160 * (block + b) : 160 * (block + b) + 160, :] = grad[
                    160 * i : 160 * i + 160, 128 * b : 128 * b + 128
                ]

    by_owner(turned_all, normed[...].T, place[2])
    for h in range(2):
        store(dot(turned_all[:, T:], query_low[:, 512 * h : 512 * h + 512]).astype(BF16), 4 * h)
    store(dot(turned_all[...], pair_low[...]).astype(BF16), 8)

    earlier = before_back[...].astype(F32)
    later = dot_nt(pair_low[T:, :], weight[:, 1024:]) + dot_nt(query_low[...], weight[:, :1024])
    own_back[...] = later
    values, values_before = here[...].astype(F32), before[...].astype(F32)
    gain_in_back = jnp.sum(later * (values * inverse_rms(values)), axis=0, keepdims=True) + jnp.sum(
        earlier * (values_before * inverse_rms(values_before)), axis=0, keepdims=True
    )
    rows = lax.broadcasted_iota(jnp.int32, (128, 128), 0)
    block = jnp.zeros((128, 128), F32)
    lines = [gain_in_back] + [gain_back[r : r + 1, :] for r in range(3)] + [head_back[0:1, :], head_back[1:2, :]]
    at = 0
    for line in lines:
        for b in range(line.shape[1] // 128):
            block = jnp.where(rows == at, line[:, 128 * b : 128 * b + 128], block)
            at += 1
    low = block.astype(BF16)
    for j in range(2):
        keep[j, 1920:, :] = low
        give[j, 1920:, :] = low


MERGED = 4


def merge_kernel(place, keep, got, out_keep, out_got, wide, up_keep, up_give, down_keep, down_give):
    half, mixed = place[1], place[5]
    for k in range(MERGED):
        for z in range(2):
            def added(rows, k=k, z=z):
                return keep[k, z, rows, :].astype(F32) + got[k, z, rows, :].astype(F32)

            wide[k, z, :160, :] = added(slice(0, 160)).astype(BF16)
            wide[k, z, 160:240, :] = (out_keep[k, z].astype(F32) + out_got[k, z].astype(F32)).astype(BF16)
            wide[k, z, 240:, :] = jnp.zeros((16, 128), BF16)
            one, two = added(slice(320, 400)), added(slice(400, 480))
            down_keep[k, z] = jnp.where(mixed == 0, one, two).astype(BF16)
            down_give[k, z] = jnp.where(mixed == 0, two, one).astype(BF16)
        one, two = (keep[k, z, 160:320, :].astype(F32) + got[k, z, 160:320, :].astype(F32) for z in range(2))
        up_keep[k] = jnp.where(half == 0, one, two).astype(BF16)
        up_give[k] = jnp.where(half == 0, two, one).astype(BF16)


def merge(place, keep, got, out_keep, out_got):
    def spec(*shape):
        return pl.BlockSpec((MERGED, *shape), lambda i: (i,) + (0,) * len(shape))

    outs = [(2, 256, 128), (160, 128), (160, 128), (2, 80, 128), (2, 80, 128)]
    return pl.pallas_call(
        merge_kernel,
        grid=(16 // MERGED,),
        out_shape=[jax.ShapeDtypeStruct((16, *o), BF16) for o in outs],
        in_specs=[pl.BlockSpec(memory_space=pltpu.SMEM)] + [spec(2, 480, 128)] * 2 + [spec(2, 80, 128)] * 2,
        out_specs=[spec(*o) for o in outs],
        compiler_params=pltpu.CompilerParams(vmem_limit_bytes=60 * 2**20),
        cost_estimate=pl.CostEstimate(flops=1_000_000, bytes_accessed=1_000_000, transcendentals=0),
    )(place, keep, got, out_keep, out_got)


def line_kernel(place, up_keep, up_got, down_keep, down_got, up_next, up_give, down_next, down_give):
    half, low = place[1], place[4]

    def parted(one, two, choice, stay, leave):
        stay[...] = jnp.where(choice == 0, one, two).astype(BF16)
        leave[...] = jnp.where(choice == 0, two, one).astype(BF16)

    one, two = (up_keep[:, r : r + 80, :].astype(F32) + up_got[:, r : r + 80, :].astype(F32) for r in (0, 80))
    parted(one, two, low, up_next, up_give)
    one, two = (down_keep[:, z].astype(F32) + down_got[:, z].astype(F32) for z in range(2))
    parted(one, two, half, down_next, down_give)


def rest_kernel(keep, got, up_keep, up_got, down_keep, down_got, rest):
    for z in range(2):
        for k in range(16):
            rows = slice(128 * k, 128 * k + 128)
            rest[k, 128 * z : 128 * z + 128, :] = (keep[z, rows, :].astype(F32) + got[z, rows, :].astype(F32)).astype(BF16)
    rest[:, 256:336, :] = (up_keep[...].astype(F32) + up_got[...].astype(F32)).astype(BF16)
    rest[:, 336:, :] = (down_keep[...].astype(F32) + down_got[...].astype(F32)).astype(BF16)


def finish_wide_kernel(place, own, other, gate, up, out):
    low = place[4]
    blocks = []
    for k in range(16):
        cols = slice(128 * k, 128 * k + 128)
        mine, theirs = own[k].astype(F32), other[k].astype(F32)
        one = jnp.where(low == 0, mine, theirs)
        two = jnp.where(low == 0, theirs, mine)
        gate[:128, cols] = one[:128]
        gate[128:, cols] = two[:32]
        up[:80, cols] = one[128:]
        up[80:, cols] = two[128:]
        blocks.append(two[32:112])
    for b in range(2):
        out[128 * b : 128 * b + 128, :] = jnp.concatenate(blocks[8 * b : 8 * b + 8], axis=0).T


def finish_rest_kernel(place, done, query, key, value, down, *gains):
    me = place[0]
    for b in range(4):
        block = jnp.concatenate([done[4 * b + r, 128:288, :] for r in range(4)], axis=0)
        down[128 * b : 128 * b + 128, :] = block.astype(F32).T
    for block in range(12):
        ref, at = ((query, block), (key, block - 8), (value, block - 10))[(block >= 8) + (block >= 10)]
        row = 0
        while row < 160:
            flat = 160 * block + row
            chunk, start = flat // 128, flat % 128
            size = min(160 - row, 128 - start)
            ref[row : row + size, 128 * at : 128 * at + 128] = done[chunk, start : start + size, :].astype(F32)
            row += size
    lines = done[15, 0:32, :]

    def pick(count, size):
        parts = []
        for b in range(count):
            source = lax.broadcasted_iota(jnp.int32, (128, size), 0) + 128 * b
            target = lax.broadcasted_iota(jnp.int32, (128, size), 1) + me * size
            parts.append(dot(lines, jnp.where(source == target, 1.0, 0.0).astype(BF16)))
        return parts

    for i, ref in enumerate(gains[:4]):
        parts = pick(5, 160) if i == 0 else parts
        ref[...] = sum(parts[b][5 * i + b : 5 * i + b + 1, :] for b in range(5)).reshape(160)
    parts = pick(2, 64)
    for i, ref in enumerate(gains[4:]):
        ref[...] = sum(parts[b][20 + 2 * i + b : 21 + 2 * i + b, :] for b in range(2)).reshape(64)


def call(kernel, outs, scratch, flops, *args):
    spec = [pl.BlockSpec(memory_space=pltpu.SMEM)] + [pl.BlockSpec(memory_space=pltpu.VMEM)] * (len(args) - 1)
    if kernel in (attend_kernel, rest_kernel, back_kernel):
        spec = [pl.BlockSpec(memory_space=pltpu.VMEM)] * len(args)
    shapes = [jax.ShapeDtypeStruct(s, d) for s, d in outs]
    size = sum(a.size * a.dtype.itemsize for a in args) + sum(s.size * s.dtype.itemsize for s in shapes)
    return pl.pallas_call(
        kernel,
        out_shape=shapes,
        in_specs=spec,
        out_specs=[pl.BlockSpec(memory_space=pltpu.VMEM)] * len(shapes),
        scratch_shapes=[pltpu.VMEM(s, d) for s, d in scratch],
        compiler_params=pltpu.CompilerParams(vmem_limit_bytes=60 * 2**20),
        cost_estimate=pl.CostEstimate(flops=flops, bytes_accessed=min(size, flops), transcendentals=0),
    )(*args)


def pick(block, index, axis):
    return lax.dynamic_index_in_dim(block, index, axis, keepdims=False)


def add(*terms):
    return sum(t.astype(F32) for t in terms).astype(BF16)


def plane_swap(chunks):
    return lax.all_to_all(chunks, PLANE, 0, 0)


def plane_total(chunks):
    return jnp.sum(chunks.astype(F32), axis=0)


def plane_gather(chunk):
    return lax.all_to_all(jnp.broadcast_to(chunk[None], (16,) + chunk.shape), PLANE, 0, 0)


def line_sum(part, half):
    keep, give = pick(part, half, 0).astype(BF16), pick(part, 1 - half, 0).astype(BF16)
    return add(keep, send(keep, TO_LOW), send(give, TO_HALF), send(give, TO_SAME))


def shards(
    hidden_in, cotangent, segments, positions,
    query_weight, key_weight, value_weight, output_weight, gate_weight, up_weight, down_weight,
    input_norm, attention_norm, feed_norm, result_norm, query_norm, key_norm,
):
    half, core, low = lax.axis_index("zh"), lax.axis_index("c"), lax.axis_index("zl")
    me = half * 2 + core
    spot = lax.axis_index("y") * 4 + lax.axis_index("x")
    place = jnp.stack([me, half, core, spot, low, low ^ half]).astype(jnp.int32)
    hidden = hidden_in.reshape(T, D)
    code = (segments * 65536 + positions).reshape(T) + 2**20

    gain_rows = [input_norm, attention_norm, feed_norm, result_norm, query_norm, key_norm]
    whole = pl.BlockSpec(memory_space=pltpu.VMEM)
    (first,) = pl.pallas_call(
        pack_kernel,
        out_shape=[jax.ShapeDtypeStruct((12 * BLOCK + 320, 128), BF16)],
        grid_spec=pltpu.PrefetchScalarGridSpec(
            num_scalar_prefetch=1,
            grid=(1,),
            in_specs=[pl.BlockSpec(a.shape, lambda i, s: (0, 0)) for a in (query_weight, key_weight, value_weight)]
            + [pl.BlockSpec(a.shape, lambda i, s: (0,)) for a in gain_rows]
            + [
                pl.BlockSpec((160, 128), lambda i, s: (0, s[3])),
                pl.BlockSpec((160, 128), lambda i, s: (0, s[3])),
            ],
            out_specs=[
                pl.BlockSpec((12 * BLOCK + 320, 128), lambda i, s: (0, 0)),
            ],
        ),
        compiler_params=pltpu.CompilerParams(vmem_limit_bytes=60 * 2**20),
    )(place, query_weight, key_weight, value_weight, *gain_rows, gate_weight, up_weight)

    first_far = send(first, TO_HALF)
    hidden_before = send(hidden, TO_NEXT)
    code_before = send(code, TO_NEXT)
    first_core = send(first, TO_CORE)
    codes = jnp.concatenate([code_before, code])
    own_places = positions.reshape(T)
    places = jnp.concatenate([own_places[0] - T + jnp.arange(T, dtype=jnp.int32), own_places])
    freqs = jnp.exp(-jnp.log(ROPE_BASE) * jnp.arange(HD // 2, dtype=F32) * 2.0 / HD)
    angles = places.astype(F32)[:, None] * freqs
    cosine, sine = jnp.cos(angles), jnp.sin(angles)
    first_far, hidden_before, codes, cosine, sine, output_late, down_late = lax.optimization_barrier(
        (first_far, hidden_before, codes, cosine, sine, output_weight, down_weight)
    )
    first_far_core = send(first_far, TO_CORE)
    far = plane_gather(first_far[12 * BLOCK :])
    out_far = send(output_late, TO_HALF)
    down_far = send(down_late, TO_HALF)
    out_core, gate_core, up_core, down_core = (
        send(w, TO_CORE) for w in (output_weight, gate_weight, up_weight, down_weight)
    )

    weight, gains, normed, query_raw, key_raw, query_rot, key_rot, value_low = call(
        project_kernel,
        [((D, 1536), BF16), ((16, 1536), F32), ((2 * T, D), BF16), ((T, 1024), F32), ((2 * T, HD), F32),
         ((T, 1024), BF16), ((2 * T, HD), BF16), ((2 * T, HD), BF16)],
        [],
        1_000_000,
        place, first, first_core, first_far, first_far_core, hidden_before, hidden, cosine, sine,
    )
    query_rot, out_core, gate_core, up_core, down_core, out_far = lax.optimization_barrier(
        (query_rot, out_core, gate_core, up_core, down_core, out_far)
    )
    out_far_core = send(out_far, TO_CORE)
    attended, probs = call(
        attend_kernel,
        [((T, 1024), BF16), ((T // TILE, HEADS * TILE, SPAN), BF16)],
        [],
        1_000_000,
        query_rot, key_rot, value_low, codes.reshape(1, 2 * T),
    )
    attended, out_far_core, down_far = lax.optimization_barrier((attended, out_far_core, down_far))
    down_far_core = send(down_far, TO_CORE)
    wo, out_raw, residual, feed_in, turn_low = call(
        mix_kernel, MIX_OUTS, [], 1_000_000,
        place, hidden, attended, gains, output_weight, out_core, out_far, out_far_core,
    )
    far, down_far_core, feed_in = lax.optimization_barrier((far, down_far_core, feed_in))
    layer_out, give, keep, feed_back, result_gain_back = call(
        feed_kernel, FEED_OUTS, FEED_SCRATCH, 1_000_000,
        place, residual, cotangent.reshape(T, D), gains, feed_in, turn_low,
        gate_weight, up_weight, down_weight, gate_core, up_core, down_core,
        far, send(far, TO_CORE), down_far, down_far_core,
    )
    out_give, out_keep, attended_back, residual_back, gain_back = call(
        output_kernel, OUTPUT_OUTS, [], 1_000_000,
        place, cotangent.reshape(T, D), attended, gains, wo, out_raw, residual, feed_back, result_gain_back,
    )
    got = send(give, TO_CORE)
    out_got = send(out_give, TO_CORE)
    wide, up_keep, up_give, down_keep, down_give, attended_back = lax.optimization_barrier(
        (*merge(place, keep, got, out_keep, out_got), attended_back)
    )
    wide_got = plane_swap(wide)
    up_got, down_got = send(up_give, TO_HALF), send(down_give, TO_LOW)
    query_low, pair_low, head_back, before_back = call(
        back_kernel,
        [((T, 1024), BF16), ((2 * T, 512), BF16), ((8, HD), F32), ((T, D), BF16)],
        [((HD, 2 * T), F32), ((HD, 2 * T), F32)],
        1_000_000,
        query_rot, key_rot, value_low, probs, attended, attended_back, query_raw, key_raw, gains, cosine, sine, weight,
    )
    up_keep, up_give, down_keep, down_give = call(
        line_kernel, [((16, 80, 128), BF16)] * 4, [], 0, place, up_keep, up_got, down_keep, down_got
    )
    query_low, up_keep, up_give, down_keep, down_give = lax.optimization_barrier(
        (query_low, up_keep, up_give, down_keep, down_give)
    )
    up_got, down_got = send(up_give, TO_LOW), send(down_give, TO_HALF)
    first_give, first_keep, own_back = call(
        first_kernel,
        [((2, 2048, 128), BF16), ((2, 2048, 128), BF16), ((T, D), F32)],
        [((D, 2 * T), BF16)],
        1_000_000,
        place, normed, query_low, pair_low, weight, head_back, gain_back, hidden_before, hidden, before_back,
    )
    first_give, up_got, down_got = lax.optimization_barrier((first_give, up_got, down_got))
    (rest,) = call(
        rest_kernel, [((16, 416, 128), BF16)], [], 0,
        first_keep, send(first_give, TO_CORE), up_keep, up_got, down_keep, down_got,
    )
    rest, wide_got = lax.optimization_barrier((rest, wide_got))
    rest_got = plane_swap(rest)
    wide_part = plane_total(wide_got).reshape(2, 2, 128, 128)
    near, away = pick(wide_part, half, 0), pick(wide_part, 1 - half, 0)
    wide_part = add(
        pick(near, low, 0),
        send(pick(near, 1 - low, 0).astype(BF16), TO_LOW),
        send(pick(away, 1 - low, 0).astype(BF16), TO_HALF),
        send(pick(away, low, 0).astype(BF16), TO_SAME),
    )
    wide_part, before_back = lax.optimization_barrier((wide_part, before_back))
    returned = send(before_back[: T // 2], TO_PREVIOUS)
    crossed = send(before_back[T // 2 :], TO_LOW)
    wide_part, rest_got, returned, crossed = lax.optimization_barrier((wide_part, rest_got, returned, crossed))
    passed = send(crossed, TO_PREVIOUS_PAIR)
    rest_part = plane_total(rest_got)
    wide_done = plane_gather(jnp.concatenate([wide_part, rest_part[256:336].astype(BF16)]))
    down_part = rest_part[336:].astype(BF16)
    down_got = send(down_part, TO_LOW)
    slim_part = line_sum(rest_part[:256].reshape(2, 128, 128), half)
    mixed = low ^ half
    rest_part = jnp.concatenate(
        [slim_part, jnp.where(mixed == 0, down_part, down_got), jnp.where(mixed == 0, down_got, down_part)]
    )
    wide_other = send(wide_done, TO_LOW)
    rest_part, wide_done, passed = lax.optimization_barrier((rest_part, wide_done, passed))
    returned = jnp.concatenate([returned, jnp.where(low == 0, crossed, passed)])
    rest_done = plane_gather(rest_part)

    normed_back = own_back + returned.astype(F32)
    gain_in = gains[0, :640]
    inputs = hidden.astype(F32)
    part, _ = norm_back(inputs, gain_in, normed_back)
    input_gradient = (residual_back + part).astype(BF16)

    gate_out, up_out, output_out = call(
        finish_wide_kernel, [((160, FF), F32), ((160, FF), F32), ((256, D), F32)], [], 1_000_000, place, wide_done, wide_other
    )
    rest_out = call(
        finish_rest_kernel,
        [((160, 1024), F32), ((160, HD), F32), ((160, HD), F32), ((512, D), F32)]
        + [((160,), F32)] * 4 + [((64,), F32)] * 2,
        [], 1_000_000, place, rest_done,
    )
    return (
        layer_out.reshape(hidden_in.shape),
        input_gradient.reshape(hidden_in.shape),
        *rest_out[:3],
        output_out,
        gate_out,
        up_out,
        rest_out[3],
        *rest_out[4:],
    )


def solution(mesh):
    fine = Mesh(mesh.devices.reshape(SIZES), AXES)
    seq, fsdp = ("y", "x", "zl"), ("zh", "c")
    tokens, rows, line = P(fsdp, seq, None), P(fsdp, None), P(fsdp)
    placed = (tokens, tokens, P(fsdp, seq), P(fsdp, seq)) + (rows,) * 7 + (line,) * 6
    return jax.shard_map(
        shards,
        mesh=fine,
        in_specs=placed,
        out_specs=(tokens, tokens) + (rows,) * 7 + (line,) * 6,
        check_vma=False,
    )
```

```python
import jax
import jax.numpy as jnp
from jax import lax
from jax.experimental import pallas as pl
from jax.experimental.pallas import tpu as pltpu
from jax.sharding import Mesh, PartitionSpec as P

WINDOW = 512
EPSILON = 1e-06
ROPE_BASE = 10000.0
AXES = ("y", "x", "zl", "zh", "c")
SIZES = (4, 4, 2, 2, 2)
PLANE = ("y", "x")
T, D, HEADS, HD, FF = 512, 640, 4, 256, 2048
SCALE = HD ** (-0.5)
TILE = 128
SPAN = WINDOW + TILE
PART = 512
F32, BF16 = jnp.float32, jnp.bfloat16


def route(move):
    def index(y, x, zl, zh, c):
        return (((y * 4 + x) * 2 + zl) * 2 + zh) * 2 + c

    return [
        (index(y, x, zl, zh, c), index(*move(y, x, zl, zh, c)))
        for y in range(4)
        for x in range(4)
        for zl in range(2)
        for zh in range(2)
        for c in range(2)
    ]


TO_CORE = route(lambda y, x, zl, zh, c: (y, x, zl, zh, 1 - c))
TO_HALF = route(lambda y, x, zl, zh, c: (y, x, 1 - zl, 1 - zh, c))
TO_LOW = route(lambda y, x, zl, zh, c: (y, x, 1 - zl, zh, c))
TO_SAME = route(lambda y, x, zl, zh, c: (y, x, zl, 1 - zh, c))
TO_NEXT = [(i * 4 + f, i * 4 + 4 + f) for i in range(31) for f in range(4)]
TO_PREVIOUS = [(j, i) for i, j in TO_NEXT]
TO_PREVIOUS_PAIR = [(i * 8 + 12 + f, i * 8 + 4 + f) for i in range(15) for f in range(4)]


def send(block, pairs):
    return lax.ppermute(block, AXES, pairs)


def dot(left, right):
    return jnp.dot(left, right, preferred_element_type=F32)


def dot_nt(left, right):
    return lax.dot_general(left, right, (((1,), (1,)), ((), ())), preferred_element_type=F32)


def inverse_rms(values):
    return lax.rsqrt(jnp.mean(values * values, axis=-1, keepdims=True) + EPSILON)


def norm_back(values, gain, upstream):
    inverse = inverse_rms(values)
    unit = values * inverse
    scaled = upstream * gain
    back = inverse * (scaled - unit * jnp.mean(scaled * unit, axis=-1, keepdims=True))
    return back, upstream * unit


def turned(values, cosine, sine):
    first, second = values[:, : HD // 2], values[:, HD // 2 :]
    return jnp.concatenate([first * cosine - second * sine, second * cosine + first * sine], axis=-1)


BLOCK = 176


def pack_kernel(place, wq, wk, wv, g_in, g_att, g_feed, g_res, g_q, g_k, gate, up, first):
    me = place[0]
    for b in range(12):
        ref, at = ((wq, b), (wk, b - 8), (wv, b - 10))[(b >= 8) + (b >= 10)]
        first[BLOCK * b : BLOCK * b + 160, :] = ref[:, 128 * at : 128 * at + 128]

    def placed(upper, lower, width):
        count = upper.shape[0]
        rows = lax.broadcasted_iota(jnp.int32, (16, count), 0)
        both = jnp.where(rows == 0, upper[...].astype(F32)[None, :], jnp.where(rows == 1, lower[...].astype(F32)[None, :], 0.0))
        source = lax.broadcasted_iota(jnp.int32, (count, width), 0)
        target = lax.broadcasted_iota(jnp.int32, (count, width), 1)
        pick = jnp.where(target == source + me * count, 1.0, 0.0).astype(BF16)
        return dot(both.astype(BF16), pick).astype(BF16)

    at = 0
    for upper, lower, width in ((g_in, g_feed, 640), (g_att, g_res, 640), (g_q, g_k, 256)):
        row = placed(upper, lower, width)
        for b in range(width // 128):
            first[BLOCK * at + 160 : BLOCK * at + BLOCK, :] = row[:, 128 * b : 128 * b + 128]
            at += 1
    first[12 * BLOCK : 12 * BLOCK + 160, :] = gate[...]
    first[12 * BLOCK + 160 :, :] = up[...]


def project_kernel(place, own, own_c, far, far_c, before, here, cosine, sine,
                   weight, gains, normed, query_raw, key_raw, query_rot, key_rot, value_low):
    me = place[0]
    for turn, piece in enumerate((own, own_c, far, far_c)):
        for b in range(12):
            weight[pl.ds(pl.multiple_of((me ^ turn) * 160, 32), 160), 128 * b : 128 * b + 128] = piece[
                BLOCK * b : BLOCK * b + 160, :
            ]
    for b in range(12):
        gains[:, 128 * b : 128 * b + 128] = sum(
            piece[BLOCK * b + 160 : BLOCK * b + BLOCK, :].astype(F32) for piece in (own, own_c, far, far_c)
        )
    total = gains[...]
    gain_in, gain_q, gain_k = total[0:1, :640], total[0:1, 1280:], total[1:2, 1280:]
    for base, source in ((0, before), (T, here)):
        values = source[...].astype(F32)
        normed[base : base + T, :] = (values * inverse_rms(values) * gain_in).astype(BF16)
    for base in (0, T):
        low = normed[base : base + T, :]
        cos, sin = cosine[base : base + T, :], sine[base : base + T, :]
        raw = dot(low, weight[:, 1024:1280])
        key_raw[base : base + T, :] = raw
        key_rot[base : base + T, :] = turned(raw * inverse_rms(raw) * gain_k, cos, sin).astype(BF16)
        value_low[base : base + T, :] = dot(low, weight[:, 1280:]).astype(BF16)
    low = normed[T:, :]
    cos, sin = cosine[T:, :], sine[T:, :]
    for h in range(HEADS):
        cols = slice(h * HD, (h + 1) * HD)
        raw = dot(low, weight[:, cols])
        query_raw[:, cols] = raw
        query_rot[:, cols] = turned(raw * inverse_rms(raw) * gain_q, cos, sin).astype(BF16)


def stacked(ref, rows):
    return jnp.concatenate([ref[rows, h * HD : (h + 1) * HD] for h in range(HEADS)], axis=0)


def attend_kernel(query_rot, key_rot, value_low, codes, attended, probs):
    for i in range(T // TILE):
        rows, span = slice(i * TILE, (i + 1) * TILE), slice(i * TILE, i * TILE + SPAN)
        scores = dot_nt(stacked(query_rot, rows), key_rot[span, :]) * SCALE
        own = slice(T + i * TILE, T + (i + 1) * TILE)
        gap = jnp.broadcast_to(codes[:, own], (8, TILE)).T[:, 0:1] - codes[:, span]
        visible = (gap >= 0) & (gap < WINDOW)
        scores = jnp.where(visible[None], scores.reshape(HEADS, TILE, SPAN), -1e30)
        top = jnp.max(scores, axis=-1, keepdims=True)
        raised = jnp.exp(scores - top)
        weight = raised * (1.0 / jnp.sum(raised, axis=-1, keepdims=True))
        low = weight.reshape(HEADS * TILE, SPAN).astype(BF16)
        probs[i] = low
        out = dot(low, value_low[span, :])
        for h in range(HEADS):
            attended[rows, h * HD : (h + 1) * HD] = out[h * TILE : (h + 1) * TILE].astype(BF16)


GELU_A, GELU_B = 0.7978845608028654, 0.044715
ROWS = 480


def by_owner(ref, rows, core):
    for j in range(4):
        at = 2 * ((core + j) % 2) + j // 2
        ref[pl.ds(pl.multiple_of(at * 160, 32), 160), :] = rows[160 * j : 160 * j + 160, :]


def mix_kernel(place, hidden, attended, gains, wo_own, wo_c, wo_far, wo_far_c,
               wo, out_raw, residual, feed_in, turn_low):
    me = place[0]
    for turn, piece in enumerate((wo_own, wo_c, wo_far, wo_far_c)):
        wo[pl.ds(pl.multiple_of((me ^ turn) * 256, 256), 256), :] = piece[...]
    out = dot(attended[...], wo[...])
    out_raw[...] = out
    total = hidden[...].astype(F32) + out * inverse_rms(out) * gains[0:1, 640:1280]
    residual[...] = total
    low = (total * inverse_rms(total) * gains[1:2, :640]).astype(BF16)
    feed_in[...] = low
    by_owner(turn_low, low.T, place[2])


def feed_kernel(place, residual, cotangent, gains, feed_in, turn_low,
                g_own, u_own, d_own, g_c, u_c, d_c, far, far_c, d_far, d_far_c,
                layer_out, give, keep, feed_back, gain_back,
                wg, wu, wd, gate, up, activated, down_low):
    me, core = place[0], place[2]
    for turn, (g_p, u_p, d_p) in enumerate(((g_own, u_own, d_own), (g_c, u_c, d_c))):
        j = me ^ turn
        wg[pl.ds(pl.multiple_of(j * 160, 32), 160), :] = g_p[...]
        wu[pl.ds(pl.multiple_of(j * 160, 32), 160), :] = u_p[...]
        wd[pl.ds(pl.multiple_of(j * 512, 512), 512), :] = d_p[...]
    for turn, (piece, d_p) in enumerate(((far, d_far), (far_c, d_far_c))):
        j = me ^ (2 + turn)
        for k in range(16):
            cols = slice(128 * k, 128 * k + 128)
            wg[pl.ds(pl.multiple_of(j * 160, 32), 160), cols] = piece[k, 0:160, :]
            wu[pl.ds(pl.multiple_of(j * 160, 32), 160), cols] = piece[k, 160:320, :]
        wd[pl.ds(pl.multiple_of(j * 512, 512), 512), :] = d_p[...]
    gain_res = gains[1:2, 640:1280]

    def put(owner, write):
        pl.when(core == owner % 2)(lambda: write(keep))
        pl.when(core != owner % 2)(lambda: write(give))

    def forward(n, carry):
        cols = pl.ds(pl.multiple_of(n * PART, PART), PART)
        g = dot(feed_in[...], wg[:, cols])
        u = dot(feed_in[...], wu[:, cols])
        t = jnp.tanh(GELU_A * (g + GELU_B * g * g * g))
        half = 0.5 * (1.0 + t)
        slope = half + 0.5 * g * (1.0 - t * t) * (GELU_A * (1.0 + 3.0 * GELU_B * g * g))
        gelu = g * half
        gate[:, cols] = gelu
        up[:, cols] = u * slope
        activated[:, cols] = (gelu * u).astype(BF16)
        return carry

    lax.fori_loop(0, FF // PART, forward, 0)
    down_raw = dot(activated[...], wd[...])
    layer_out[...] = (residual[...] + down_raw * inverse_rms(down_raw) * gain_res).astype(BF16)
    upstream = cotangent[...].astype(F32)
    down_back, share = norm_back(down_raw, gain_res, upstream)
    gain_back[...] = jnp.broadcast_to(jnp.sum(share, axis=0, keepdims=True), (8, D))
    down_low[...] = down_back.astype(BF16)
    turn_down = down_low[...].T
    feed_back[...] = jnp.zeros_like(feed_back)

    def backward(n, carry):
        cols = pl.ds(pl.multiple_of(n * PART, PART), PART)
        act_back = dot_nt(down_low[...], wd[cols, :])
        gate_low = (act_back * up[:, cols]).astype(BF16)
        up_low = (act_back * gate[:, cols]).astype(BF16)
        feed_back[...] += dot_nt(gate_low, wg[:, cols]) + dot_nt(up_low, wu[:, cols])
        for base, low in ((0, gate_low), (160, up_low)):
            grad = dot(turn_low[...], low).astype(BF16)
            for i, ref in enumerate((keep, keep, give, give)):
                for b in range(PART // 128):
                    ref[n * (PART // 128) + b, i % 2, base : base + 160, :] = grad[
                        160 * i : 160 * i + 160, 128 * b : 128 * b + 128
                    ]
        grad = dot(turn_down, activated[:, cols]).astype(BF16)
        j = n // (512 // PART)
        first = (n % (512 // PART)) * (PART // 128)

        def write_down(ref):
            for b in range(PART // 128):
                for r in range(4):
                    ref[(first + b) * 4 + r, j // 2, 320:480, :] = grad[160 * r : 160 * r + 160, 128 * b : 128 * b + 128]
        put(j, write_down)
        return carry

    lax.fori_loop(0, FF // PART, backward, 0)


def output_kernel(place, cotangent, attended, gains, wo, out_raw, residual, feed_back, result_gain_back,
                  give, keep, attended_back, residual_back, gain_back):
    core = place[2]
    gain_att, gain_feed = gains[0:1, 640:1280], gains[1:2, :640]
    part, share = norm_back(residual[...], gain_feed, feed_back[...])
    gain_back[1:2, :] = jnp.sum(share, axis=0, keepdims=True)
    back = cotangent[...].astype(F32) + part
    residual_back[...] = back
    out_back, share = norm_back(out_raw[...], gain_att, back)
    gain_back[0:1, :] = jnp.sum(share, axis=0, keepdims=True)
    gain_back[2:, :] = result_gain_back[2:, :]
    out_low = out_back.astype(BF16)
    attended_back[...] = dot_nt(out_low, wo[...]).astype(BF16)
    turn_out = out_low.T
    for ref, side in ((keep, core), (give, 1 - core)):
        for z in range(2):
            cols = pl.ds(pl.multiple_of((2 * z + side) * 256, 256), 256)
            grad = dot(turn_out, attended[:, cols]).astype(BF16)
            for b in range(2):
                for r in range(8):
                    ref[8 * b + r, z, :, :] = grad[80 * r : 80 * r + 80, 128 * b : 128 * b + 128]


FEED_SCRATCH = [((D, FF), BF16), ((D, FF), BF16), ((FF, D), BF16), ((T, FF), F32), ((T, FF), F32),
                ((T, FF), BF16), ((T, D), BF16)]
FEED_OUTS = [((T, D), BF16), ((16, 2, ROWS, 128), BF16), ((16, 2, ROWS, 128), BF16), ((T, D), F32), ((8, D), F32)]
MIX_OUTS = [((1024, D), BF16), ((T, D), F32), ((T, D), F32), ((T, D), BF16), ((D, T), BF16)]
OUTPUT_OUTS = [((16, 2, 80, 128), BF16), ((16, 2, 80, 128), BF16), ((T, 1024), BF16), ((T, D), F32), ((8, D), F32)]


def back_kernel(query_rot, key_rot, value_low, probs, attended, attended_back,
                query_raw, key_raw, gains, cosine, sine, weight,
                query_low, pair_low, head_back, before_back, key_sum, value_sum):
    key_sum[...] = jnp.zeros_like(key_sum)
    value_sum[...] = jnp.zeros_like(value_sum)
    gain_q, gain_k = gains[0:1, 1280:], gains[1:2, 1280:]
    gain_q_back = jnp.zeros((1, HD), F32)
    for i in range(T // TILE):
        rows, span = slice(i * TILE, (i + 1) * TILE), slice(i * TILE, i * TILE + SPAN)
        back = stacked(attended_back, rows)
        delta = jnp.sum(back.astype(F32) * stacked(attended, rows).astype(F32), axis=-1, keepdims=True)
        prob = probs[i]
        prob_back = dot_nt(back, value_low[span, :])
        score_back = (prob.astype(F32) * (prob_back - delta)).astype(BF16)
        value_sum[:, span] += dot(back.T, prob)
        key_sum[:, span] += dot(stacked(query_rot, rows).T, score_back) * SCALE
        query_back = dot(score_back, key_rot[span, :]) * SCALE
        cos, sin = cosine[T + i * TILE : T + (i + 1) * TILE, :], sine[T + i * TILE : T + (i + 1) * TILE, :]
        for h in range(HEADS):
            unturned = turned(query_back[h * TILE : (h + 1) * TILE], cos, -sin)
            raw_back, share = norm_back(query_raw[rows, h * HD : (h + 1) * HD], gain_q, unturned)
            gain_q_back += jnp.sum(share, axis=0, keepdims=True)
            query_low[rows, h * HD : (h + 1) * HD] = raw_back.astype(BF16)
    raw_back, share = norm_back(key_raw[...], gain_k, turned(key_sum[...].T, cosine[...], -sine[...]))
    gain_k_back = jnp.sum(share, axis=0, keepdims=True)
    pair_low[:, :HD] = raw_back.astype(BF16)
    pair_low[:, HD:] = value_sum[...].T.astype(BF16)

    before_back[...] = dot_nt(pair_low[:T, :], weight[:, 1024:]).astype(BF16)
    rows = lax.broadcasted_iota(jnp.int32, (8, HD), 0)
    head_back[...] = jnp.where(rows == 0, gain_q_back, gain_k_back)


def first_kernel(place, normed, query_low, pair_low, weight, head_back, gain_back, before, here, before_back,
                 give, keep, own_back, turned_all):
    def store(grad, block):
        for i, ref in enumerate((keep, keep, give, give)):
            for b in range(grad.shape[1] // 128):
                ref[i % 2, 160 * (block + b) : 160 * (block + b) + 160, :] = grad[
                    160 * i : 160 * i + 160, 128 * b : 128 * b + 128
                ]

    by_owner(turned_all, normed[...].T, place[2])
    for h in range(2):
        store(dot(turned_all[:, T:], query_low[:, 512 * h : 512 * h + 512]).astype(BF16), 4 * h)
    store(dot(turned_all[...], pair_low[...]).astype(BF16), 8)

    earlier = before_back[...].astype(F32)
    later = dot_nt(pair_low[T:, :], weight[:, 1024:]) + dot_nt(query_low[...], weight[:, :1024])
    own_back[...] = later
    values, values_before = here[...].astype(F32), before[...].astype(F32)
    gain_in_back = jnp.sum(later * (values * inverse_rms(values)), axis=0, keepdims=True) + jnp.sum(
        earlier * (values_before * inverse_rms(values_before)), axis=0, keepdims=True
    )
    rows = lax.broadcasted_iota(jnp.int32, (128, 128), 0)
    block = jnp.zeros((128, 128), F32)
    lines = [gain_in_back] + [gain_back[r : r + 1, :] for r in range(3)] + [head_back[0:1, :], head_back[1:2, :]]
    at = 0
    for line in lines:
        for b in range(line.shape[1] // 128):
            block = jnp.where(rows == at, line[:, 128 * b : 128 * b + 128], block)
            at += 1
    low = block.astype(BF16)
    for j in range(2):
        keep[j, 1920:, :] = low
        give[j, 1920:, :] = low


MERGED = 4


def merge_kernel(place, keep, got, out_keep, out_got, wide, up_keep, up_give, down_keep, down_give):
    half, mixed = place[1], place[5]
    for k in range(MERGED):
        for z in range(2):
            def added(rows, k=k, z=z):
                return keep[k, z, rows, :].astype(F32) + got[k, z, rows, :].astype(F32)

            wide[k, z, :160, :] = added(slice(0, 160)).astype(BF16)
            wide[k, z, 160:240, :] = (out_keep[k, z].astype(F32) + out_got[k, z].astype(F32)).astype(BF16)
            wide[k, z, 240:, :] = jnp.zeros((16, 128), BF16)
            one, two = added(slice(320, 400)), added(slice(400, 480))
            down_keep[k, z] = jnp.where(mixed == 0, one, two).astype(BF16)
            down_give[k, z] = jnp.where(mixed == 0, two, one).astype(BF16)
        one, two = (keep[k, z, 160:320, :].astype(F32) + got[k, z, 160:320, :].astype(F32) for z in range(2))
        up_keep[k] = jnp.where(half == 0, one, two).astype(BF16)
        up_give[k] = jnp.where(half == 0, two, one).astype(BF16)


def merge(place, keep, got, out_keep, out_got):
    def spec(*shape):
        return pl.BlockSpec((MERGED, *shape), lambda i: (i,) + (0,) * len(shape))

    outs = [(2, 256, 128), (160, 128), (160, 128), (2, 80, 128), (2, 80, 128)]
    return pl.pallas_call(
        merge_kernel,
        grid=(16 // MERGED,),
        out_shape=[jax.ShapeDtypeStruct((16, *o), BF16) for o in outs],
        in_specs=[pl.BlockSpec(memory_space=pltpu.SMEM)] + [spec(2, 480, 128)] * 2 + [spec(2, 80, 128)] * 2,
        out_specs=[spec(*o) for o in outs],
        compiler_params=pltpu.CompilerParams(vmem_limit_bytes=60 * 2**20),
        cost_estimate=pl.CostEstimate(flops=1_000_000, bytes_accessed=1_000_000, transcendentals=0),
    )(place, keep, got, out_keep, out_got)


def line_kernel(place, up_keep, up_got, down_keep, down_got, up_next, up_give, down_next, down_give):
    half, low = place[1], place[4]

    def parted(one, two, choice, stay, leave):
        stay[...] = jnp.where(choice == 0, one, two).astype(BF16)
        leave[...] = jnp.where(choice == 0, two, one).astype(BF16)

    one, two = (up_keep[:, r : r + 80, :].astype(F32) + up_got[:, r : r + 80, :].astype(F32) for r in (0, 80))
    parted(one, two, low, up_next, up_give)
    one, two = (down_keep[:, z].astype(F32) + down_got[:, z].astype(F32) for z in range(2))
    parted(one, two, half, down_next, down_give)


def rest_kernel(keep, got, up_keep, up_got, down_keep, down_got, rest):
    for z in range(2):
        for k in range(16):
            rows = slice(128 * k, 128 * k + 128)
            rest[k, 128 * z : 128 * z + 128, :] = (keep[z, rows, :].astype(F32) + got[z, rows, :].astype(F32)).astype(BF16)
    rest[:, 256:336, :] = (up_keep[...].astype(F32) + up_got[...].astype(F32)).astype(BF16)
    rest[:, 336:, :] = (down_keep[...].astype(F32) + down_got[...].astype(F32)).astype(BF16)


def finish_wide_kernel(place, own, other, gate, up, out):
    low = place[4]
    blocks = []
    for k in range(16):
        cols = slice(128 * k, 128 * k + 128)
        mine, theirs = own[k].astype(F32), other[k].astype(F32)
        one = jnp.where(low == 0, mine, theirs)
        two = jnp.where(low == 0, theirs, mine)
        gate[:128, cols] = one[:128]
        gate[128:, cols] = two[:32]
        up[:80, cols] = one[128:]
        up[80:, cols] = two[128:]
        blocks.append(two[32:112])
    for b in range(2):
        out[128 * b : 128 * b + 128, :] = jnp.concatenate(blocks[8 * b : 8 * b + 8], axis=0).T


def finish_rest_kernel(place, done, query, key, value, down, *gains):
    me = place[0]
    for b in range(4):
        block = jnp.concatenate([done[4 * b + r, 128:288, :] for r in range(4)], axis=0)
        down[128 * b : 128 * b + 128, :] = block.astype(F32).T
    for block in range(12):
        ref, at = ((query, block), (key, block - 8), (value, block - 10))[(block >= 8) + (block >= 10)]
        row = 0
        while row < 160:
            flat = 160 * block + row
            chunk, start = flat // 128, flat % 128
            size = min(160 - row, 128 - start)
            ref[row : row + size, 128 * at : 128 * at + 128] = done[chunk, start : start + size, :].astype(F32)
            row += size
    lines = done[15, 0:32, :]

    def pick(count, size):
        parts = []
        for b in range(count):
            source = lax.broadcasted_iota(jnp.int32, (128, size), 0) + 128 * b
            target = lax.broadcasted_iota(jnp.int32, (128, size), 1) + me * size
            parts.append(dot(lines, jnp.where(source == target, 1.0, 0.0).astype(BF16)))
        return parts

    for i, ref in enumerate(gains[:4]):
        parts = pick(5, 160) if i == 0 else parts
        ref[...] = sum(parts[b][5 * i + b : 5 * i + b + 1, :] for b in range(5)).reshape(160)
    parts = pick(2, 64)
    for i, ref in enumerate(gains[4:]):
        ref[...] = sum(parts[b][20 + 2 * i + b : 21 + 2 * i + b, :] for b in range(2)).reshape(64)


def call(kernel, outs, scratch, flops, *args):
    spec = [pl.BlockSpec(memory_space=pltpu.SMEM)] + [pl.BlockSpec(memory_space=pltpu.VMEM)] * (len(args) - 1)
    if kernel in (attend_kernel, rest_kernel, back_kernel):
        spec = [pl.BlockSpec(memory_space=pltpu.VMEM)] * len(args)
    shapes = [jax.ShapeDtypeStruct(s, d) for s, d in outs]
    size = sum(a.size * a.dtype.itemsize for a in args) + sum(s.size * s.dtype.itemsize for s in shapes)
    return pl.pallas_call(
        kernel,
        out_shape=shapes,
        in_specs=spec,
        out_specs=[pl.BlockSpec(memory_space=pltpu.VMEM)] * len(shapes),
        scratch_shapes=[pltpu.VMEM(s, d) for s, d in scratch],
        compiler_params=pltpu.CompilerParams(vmem_limit_bytes=60 * 2**20),
        cost_estimate=pl.CostEstimate(flops=flops, bytes_accessed=min(size, flops), transcendentals=0),
    )(*args)


def pick(block, index, axis):
    return lax.dynamic_index_in_dim(block, index, axis, keepdims=False)


def add(*terms):
    return sum(t.astype(F32) for t in terms).astype(BF16)


def plane_swap(chunks):
    return lax.all_to_all(chunks, PLANE, 0, 0)


def plane_total(chunks):
    return jnp.sum(chunks.astype(F32), axis=0)


def plane_gather(chunk):
    return lax.all_to_all(jnp.broadcast_to(chunk[None], (16,) + chunk.shape), PLANE, 0, 0)


def line_sum(part, half):
    keep, give = pick(part, half, 0).astype(BF16), pick(part, 1 - half, 0).astype(BF16)
    return add(keep, send(keep, TO_LOW), send(give, TO_HALF), send(give, TO_SAME))


def shards(
    hidden_in, cotangent, segments, positions,
    query_weight, key_weight, value_weight, output_weight, gate_weight, up_weight, down_weight,
    input_norm, attention_norm, feed_norm, result_norm, query_norm, key_norm,
):
    half, core, low = lax.axis_index("zh"), lax.axis_index("c"), lax.axis_index("zl")
    me = half * 2 + core
    spot = lax.axis_index("y") * 4 + lax.axis_index("x")
    place = jnp.stack([me, half, core, spot, low, low ^ half]).astype(jnp.int32)
    hidden = hidden_in.reshape(T, D)
    code = (segments * 65536 + positions).reshape(T) + 2**20

    gain_rows = [input_norm, attention_norm, feed_norm, result_norm, query_norm, key_norm]
    whole = pl.BlockSpec(memory_space=pltpu.VMEM)
    (first,) = pl.pallas_call(
        pack_kernel,
        out_shape=[jax.ShapeDtypeStruct((12 * BLOCK + 320, 128), BF16)],
        grid_spec=pltpu.PrefetchScalarGridSpec(
            num_scalar_prefetch=1,
            grid=(1,),
            in_specs=[pl.BlockSpec(a.shape, lambda i, s: (0, 0)) for a in (query_weight, key_weight, value_weight)]
            + [pl.BlockSpec(a.shape, lambda i, s: (0,)) for a in gain_rows]
            + [
                pl.BlockSpec((160, 128), lambda i, s: (0, s[3])),
                pl.BlockSpec((160, 128), lambda i, s: (0, s[3])),
            ],
            out_specs=[
                pl.BlockSpec((12 * BLOCK + 320, 128), lambda i, s: (0, 0)),
            ],
        ),
        compiler_params=pltpu.CompilerParams(vmem_limit_bytes=60 * 2**20),
    )(place, query_weight, key_weight, value_weight, *gain_rows, gate_weight, up_weight)

    first_far = send(first, TO_HALF)
    hidden_before = send(hidden, TO_NEXT)
    code_before = send(code, TO_NEXT)
    first_core = send(first, TO_CORE)
    codes = jnp.concatenate([code_before, code])
    own_places = positions.reshape(T)
    places = jnp.concatenate([own_places[0] - T + jnp.arange(T, dtype=jnp.int32), own_places])
    freqs = jnp.exp(-jnp.log(ROPE_BASE) * jnp.arange(HD // 2, dtype=F32) * 2.0 / HD)
    angles = places.astype(F32)[:, None] * freqs
    cosine, sine = jnp.cos(angles), jnp.sin(angles)
    first_far, hidden_before, codes, cosine, sine, output_late, down_late = lax.optimization_barrier(
        (first_far, hidden_before, codes, cosine, sine, output_weight, down_weight)
    )
    first_far_core = send(first_far, TO_CORE)
    far = plane_gather(first_far[12 * BLOCK :])
    out_far = send(output_late, TO_HALF)
    down_far = send(down_late, TO_HALF)
    out_core, gate_core, up_core, down_core = (
        send(w, TO_CORE) for w in (output_weight, gate_weight, up_weight, down_weight)
    )

    weight, gains, normed, query_raw, key_raw, query_rot, key_rot, value_low = call(
        project_kernel,
        [((D, 1536), BF16), ((16, 1536), F32), ((2 * T, D), BF16), ((T, 1024), F32), ((2 * T, HD), F32),
         ((T, 1024), BF16), ((2 * T, HD), BF16), ((2 * T, HD), BF16)],
        [],
        1_000_000,
        place, first, first_core, first_far, first_far_core, hidden_before, hidden, cosine, sine,
    )
    query_rot, out_core, gate_core, up_core, down_core, out_far = lax.optimization_barrier(
        (query_rot, out_core, gate_core, up_core, down_core, out_far)
    )
    out_far_core = send(out_far, TO_CORE)
    attended, probs = call(
        attend_kernel,
        [((T, 1024), BF16), ((T // TILE, HEADS * TILE, SPAN), BF16)],
        [],
        1_000_000,
        query_rot, key_rot, value_low, codes.reshape(1, 2 * T),
    )
    attended, out_far_core, down_far = lax.optimization_barrier((attended, out_far_core, down_far))
    down_far_core = send(down_far, TO_CORE)
    wo, out_raw, residual, feed_in, turn_low = call(
        mix_kernel, MIX_OUTS, [], 1_000_000,
        place, hidden, attended, gains, output_weight, out_core, out_far, out_far_core,
    )
    far, down_far_core, feed_in = lax.optimization_barrier((far, down_far_core, feed_in))
    layer_out, give, keep, feed_back, result_gain_back = call(
        feed_kernel, FEED_OUTS, FEED_SCRATCH, 1_000_000,
        place, residual, cotangent.reshape(T, D), gains, feed_in, turn_low,
        gate_weight, up_weight, down_weight, gate_core, up_core, down_core,
        far, send(far, TO_CORE), down_far, down_far_core,
    )
    out_give, out_keep, attended_back, residual_back, gain_back = call(
        output_kernel, OUTPUT_OUTS, [], 1_000_000,
        place, cotangent.reshape(T, D), attended, gains, wo, out_raw, residual, feed_back, result_gain_back,
    )
    got = send(give, TO_CORE)
    out_got = send(out_give, TO_CORE)
    wide, up_keep, up_give, down_keep, down_give, attended_back = lax.optimization_barrier(
        (*merge(place, keep, got, out_keep, out_got), attended_back)
    )
    wide_got = plane_swap(wide)
    up_got, down_got = send(up_give, TO_HALF), send(down_give, TO_LOW)
    query_low, pair_low, head_back, before_back = call(
        back_kernel,
        [((T, 1024), BF16), ((2 * T, 512), BF16), ((8, HD), F32), ((T, D), BF16)],
        [((HD, 2 * T), F32), ((HD, 2 * T), F32)],
        1_000_000,
        query_rot, key_rot, value_low, probs, attended, attended_back, query_raw, key_raw, gains, cosine, sine, weight,
    )
    up_keep, up_give, down_keep, down_give = call(
        line_kernel, [((16, 80, 128), BF16)] * 4, [], 0, place, up_keep, up_got, down_keep, down_got
    )
    query_low, up_keep, up_give, down_keep, down_give = lax.optimization_barrier(
        (query_low, up_keep, up_give, down_keep, down_give)
    )
    up_got, down_got = send(up_give, TO_LOW), send(down_give, TO_HALF)
    first_give, first_keep, own_back = call(
        first_kernel,
        [((2, 2048, 128), BF16), ((2, 2048, 128), BF16), ((T, D), F32)],
        [((D, 2 * T), BF16)],
        1_000_000,
        place, normed, query_low, pair_low, weight, head_back, gain_back, hidden_before, hidden, before_back,
    )
    first_give, up_got, down_got = lax.optimization_barrier((first_give, up_got, down_got))
    (rest,) = call(
        rest_kernel, [((16, 416, 128), BF16)], [], 0,
        first_keep, send(first_give, TO_CORE), up_keep, up_got, down_keep, down_got,
    )
    rest, wide_got = lax.optimization_barrier((rest, wide_got))
    rest_got = plane_swap(rest)
    wide_part = plane_total(wide_got).reshape(2, 2, 128, 128)
    near, away = pick(wide_part, half, 0), pick(wide_part, 1 - half, 0)
    wide_part = add(
        pick(near, low, 0),
        send(pick(near, 1 - low, 0).astype(BF16), TO_LOW),
        send(pick(away, 1 - low, 0).astype(BF16), TO_HALF),
        send(pick(away, low, 0).astype(BF16), TO_SAME),
    )
    wide_part, before_back = lax.optimization_barrier((wide_part, before_back))
    returned = send(before_back[: T // 2], TO_PREVIOUS)
    crossed = send(before_back[T // 2 :], TO_LOW)
    wide_part, rest_got, returned, crossed = lax.optimization_barrier((wide_part, rest_got, returned, crossed))
    passed = send(crossed, TO_PREVIOUS_PAIR)
    rest_part = plane_total(rest_got)
    wide_done = plane_gather(jnp.concatenate([wide_part, rest_part[256:336].astype(BF16)]))
    down_part = rest_part[336:].astype(BF16)
    down_got = send(down_part, TO_LOW)
    slim_part = line_sum(rest_part[:256].reshape(2, 128, 128), half)
    mixed = low ^ half
    rest_part = jnp.concatenate(
        [slim_part, jnp.where(mixed == 0, down_part, down_got), jnp.where(mixed == 0, down_got, down_part)]
    )
    wide_other = send(wide_done, TO_LOW)
    rest_part, wide_done = lax.optimization_barrier((rest_part, wide_done))
    returned = jnp.concatenate([returned, jnp.where(low == 0, crossed, passed)])
    rest_done = plane_gather(rest_part)

    normed_back = own_back + returned.astype(F32)
    gain_in = gains[0, :640]
    inputs = hidden.astype(F32)
    part, _ = norm_back(inputs, gain_in, normed_back)
    input_gradient = (residual_back + part).astype(BF16)

    gate_out, up_out, output_out = call(
        finish_wide_kernel, [((160, FF), F32), ((160, FF), F32), ((256, D), F32)], [], 1_000_000, place, wide_done, wide_other
    )
    rest_out = call(
        finish_rest_kernel,
        [((160, 1024), F32), ((160, HD), F32), ((160, HD), F32), ((512, D), F32)]
        + [((160,), F32)] * 4 + [((64,), F32)] * 2,
        [], 1_000_000, place, rest_done,
    )
    return (
        layer_out.reshape(hidden_in.shape),
        input_gradient.reshape(hidden_in.shape),
        *rest_out[:3],
        output_out,
        gate_out,
        up_out,
        rest_out[3],
        *rest_out[4:],
    )


def solution(mesh):
    fine = Mesh(mesh.devices.reshape(SIZES), AXES)
    seq, fsdp = ("y", "x", "zl"), ("zh", "c")
    tokens, rows, line = P(fsdp, seq, None), P(fsdp, None), P(fsdp)
    placed = (tokens, tokens, P(fsdp, seq), P(fsdp, seq)) + (rows,) * 7 + (line,) * 6
    return jax.shard_map(
        shards,
        mesh=fine,
        in_specs=placed,
        out_specs=(tokens, tokens) + (rows,) * 7 + (line,) * 6,
        check_vma=False,
    )
```

```python
import jax
import jax.numpy as jnp
from jax import lax
from jax.experimental import pallas as pl
from jax.experimental.pallas import tpu as pltpu
from jax.sharding import Mesh, PartitionSpec as P

WINDOW = 512
EPSILON = 1e-06
ROPE_BASE = 10000.0
AXES = ("y", "x", "zl", "zh", "c")
SIZES = (4, 4, 2, 2, 2)
PLANE = ("y", "x")
T, D, HEADS, HD, FF = 512, 640, 4, 256, 2048
SCALE = HD ** (-0.5)
TILE = 128
SPAN = WINDOW + TILE
PART = 512
F32, BF16 = jnp.float32, jnp.bfloat16


def route(move):
    def index(y, x, zl, zh, c):
        return (((y * 4 + x) * 2 + zl) * 2 + zh) * 2 + c

    return [
        (index(y, x, zl, zh, c), index(*move(y, x, zl, zh, c)))
        for y in range(4)
        for x in range(4)
        for zl in range(2)
        for zh in range(2)
        for c in range(2)
    ]


TO_CORE = route(lambda y, x, zl, zh, c: (y, x, zl, zh, 1 - c))
TO_HALF = route(lambda y, x, zl, zh, c: (y, x, 1 - zl, 1 - zh, c))
TO_LOW = route(lambda y, x, zl, zh, c: (y, x, 1 - zl, zh, c))
TO_SAME = route(lambda y, x, zl, zh, c: (y, x, zl, 1 - zh, c))
TO_NEXT = [(i * 4 + f, i * 4 + 4 + f) for i in range(31) for f in range(4)]
TO_PREVIOUS = [(j, i) for i, j in TO_NEXT]
TO_PREVIOUS_PAIR = [(i * 8 + 12 + f, i * 8 + 4 + f) for i in range(15) for f in range(4)]


def send(block, pairs):
    return lax.ppermute(block, AXES, pairs)


def dot(left, right):
    return jnp.dot(left, right, preferred_element_type=F32)


def dot_nt(left, right):
    return lax.dot_general(left, right, (((1,), (1,)), ((), ())), preferred_element_type=F32)


def inverse_rms(values):
    return lax.rsqrt(jnp.mean(values * values, axis=-1, keepdims=True) + EPSILON)


def norm_back(values, gain, upstream):
    inverse = inverse_rms(values)
    unit = values * inverse
    scaled = upstream * gain
    back = inverse * (scaled - unit * jnp.mean(scaled * unit, axis=-1, keepdims=True))
    return back, upstream * unit


def turned(values, cosine, sine):
    first, second = values[:, : HD // 2], values[:, HD // 2 :]
    return jnp.concatenate([first * cosine - second * sine, second * cosine + first * sine], axis=-1)


BLOCK = 176


def pack_kernel(place, wq, wk, wv, g_in, g_att, g_feed, g_res, g_q, g_k, gate, up, first):
    me = place[0]
    for b in range(12):
        ref, at = ((wq, b), (wk, b - 8), (wv, b - 10))[(b >= 8) + (b >= 10)]
        first[BLOCK * b : BLOCK * b + 160, :] = ref[:, 128 * at : 128 * at + 128]

    def placed(upper, lower, width):
        count = upper.shape[0]
        rows = lax.broadcasted_iota(jnp.int32, (16, count), 0)
        both = jnp.where(rows == 0, upper[...].astype(F32)[None, :], jnp.where(rows == 1, lower[...].astype(F32)[None, :], 0.0))
        source = lax.broadcasted_iota(jnp.int32, (count, width), 0)
        target = lax.broadcasted_iota(jnp.int32, (count, width), 1)
        pick = jnp.where(target == source + me * count, 1.0, 0.0).astype(BF16)
        return dot(both.astype(BF16), pick).astype(BF16)

    at = 0
    for upper, lower, width in ((g_in, g_feed, 640), (g_att, g_res, 640), (g_q, g_k, 256)):
        row = placed(upper, lower, width)
        for b in range(width // 128):
            first[BLOCK * at + 160 : BLOCK * at + BLOCK, :] = row[:, 128 * b : 128 * b + 128]
            at += 1
    first[12 * BLOCK : 12 * BLOCK + 160, :] = gate[...]
    first[12 * BLOCK + 160 :, :] = up[...]


def project_kernel(place, own, own_c, far, far_c, before, here, cosine, sine,
                   weight, gains, normed, query_raw, key_raw, query_rot, key_rot, value_low):
    me = place[0]
    for turn, piece in enumerate((own, own_c, far, far_c)):
        for b in range(12):
            weight[pl.ds(pl.multiple_of((me ^ turn) * 160, 32), 160), 128 * b : 128 * b + 128] = piece[
                BLOCK * b : BLOCK * b + 160, :
            ]
    for b in range(12):
        gains[:, 128 * b : 128 * b + 128] = sum(
            piece[BLOCK * b + 160 : BLOCK * b + BLOCK, :].astype(F32) for piece in (own, own_c, far, far_c)
        )
    total = gains[...]
    gain_in, gain_q, gain_k = total[0:1, :640], total[0:1, 1280:], total[1:2, 1280:]
    for base, source in ((0, before), (T, here)):
        values = source[...].astype(F32)
        normed[base : base + T, :] = (values * inverse_rms(values) * gain_in).astype(BF16)
    for base in (0, T):
        low = normed[base : base + T, :]
        cos, sin = cosine[base : base + T, :], sine[base : base + T, :]
        raw = dot(low, weight[:, 1024:1280])
        key_raw[base : base + T, :] = raw
        key_rot[base : base + T, :] = turned(raw * inverse_rms(raw) * gain_k, cos, sin).astype(BF16)
        value_low[base : base + T, :] = dot(low, weight[:, 1280:]).astype(BF16)
    low = normed[T:, :]
    cos, sin = cosine[T:, :], sine[T:, :]
    for h in range(HEADS):
        cols = slice(h * HD, (h + 1) * HD)
        raw = dot(low, weight[:, cols])
        query_raw[:, cols] = raw
        query_rot[:, cols] = turned(raw * inverse_rms(raw) * gain_q, cos, sin).astype(BF16)


def stacked(ref, rows):
    return jnp.concatenate([ref[rows, h * HD : (h + 1) * HD] for h in range(HEADS)], axis=0)


def attend_kernel(query_rot, key_rot, value_low, codes, attended, probs):
    for i in range(T // TILE):
        rows, span = slice(i * TILE, (i + 1) * TILE), slice(i * TILE, i * TILE + SPAN)
        scores = dot_nt(stacked(query_rot, rows), key_rot[span, :]) * SCALE
        own = slice(T + i * TILE, T + (i + 1) * TILE)
        gap = jnp.broadcast_to(codes[:, own], (8, TILE)).T[:, 0:1] - codes[:, span]
        visible = (gap >= 0) & (gap < WINDOW)
        scores = jnp.where(visible[None], scores.reshape(HEADS, TILE, SPAN), -1e30)
        top = jnp.max(scores, axis=-1, keepdims=True)
        raised = jnp.exp(scores - top)
        weight = raised * (1.0 / jnp.sum(raised, axis=-1, keepdims=True))
        low = weight.reshape(HEADS * TILE, SPAN).astype(BF16)
        probs[i] = low
        out = dot(low, value_low[span, :])
        for h in range(HEADS):
            attended[rows, h * HD : (h + 1) * HD] = out[h * TILE : (h + 1) * TILE].astype(BF16)


GELU_A, GELU_B = 0.7978845608028654, 0.044715
ROWS = 480


def by_owner(ref, rows, core):
    for j in range(4):
        at = 2 * ((core + j) % 2) + j // 2
        ref[pl.ds(pl.multiple_of(at * 160, 32), 160), :] = rows[160 * j : 160 * j + 160, :]


def mix_kernel(place, hidden, attended, gains, wo_own, wo_c, wo_far, wo_far_c,
               wo, out_raw, residual, feed_in, turn_low):
    me = place[0]
    for turn, piece in enumerate((wo_own, wo_c, wo_far, wo_far_c)):
        wo[pl.ds(pl.multiple_of((me ^ turn) * 256, 256), 256), :] = piece[...]
    out = dot(attended[...], wo[...])
    out_raw[...] = out
    total = hidden[...].astype(F32) + out * inverse_rms(out) * gains[0:1, 640:1280]
    residual[...] = total
    low = (total * inverse_rms(total) * gains[1:2, :640]).astype(BF16)
    feed_in[...] = low
    by_owner(turn_low, low.T, place[2])


def feed_kernel(place, residual, cotangent, gains, feed_in, turn_low,
                g_own, u_own, d_own, g_c, u_c, d_c, far, far_c, d_far, d_far_c,
                layer_out, give, keep, feed_back, gain_back,
                wg, wu, wd, gate, up, activated, down_low):
    me, core = place[0], place[2]
    for turn, (g_p, u_p, d_p) in enumerate(((g_own, u_own, d_own), (g_c, u_c, d_c))):
        j = me ^ turn
        wg[pl.ds(pl.multiple_of(j * 160, 32), 160), :] = g_p[...]
        wu[pl.ds(pl.multiple_of(j * 160, 32), 160), :] = u_p[...]
        wd[pl.ds(pl.multiple_of(j * 512, 512), 512), :] = d_p[...]
    for turn, (piece, d_p) in enumerate(((far, d_far), (far_c, d_far_c))):
        j = me ^ (2 + turn)
        for k in range(16):
            cols = slice(128 * k, 128 * k + 128)
            wg[pl.ds(pl.multiple_of(j * 160, 32), 160), cols] = piece[k, 0:160, :]
            wu[pl.ds(pl.multiple_of(j * 160, 32), 160), cols] = piece[k, 160:320, :]
        wd[pl.ds(pl.multiple_of(j * 512, 512), 512), :] = d_p[...]
    gain_res = gains[1:2, 640:1280]

    def put(owner, write):
        pl.when(core == owner % 2)(lambda: write(keep))
        pl.when(core != owner % 2)(lambda: write(give))

    def forward(n, carry):
        cols = pl.ds(pl.multiple_of(n * PART, PART), PART)
        g = dot(feed_in[...], wg[:, cols])
        u = dot(feed_in[...], wu[:, cols])
        t = jnp.tanh(GELU_A * (g + GELU_B * g * g * g))
        half = 0.5 * (1.0 + t)
        slope = half + 0.5 * g * (1.0 - t * t) * (GELU_A * (1.0 + 3.0 * GELU_B * g * g))
        gelu = g * half
        gate[:, cols] = gelu
        up[:, cols] = u * slope
        activated[:, cols] = (gelu * u).astype(BF16)
        return carry

    lax.fori_loop(0, FF // PART, forward, 0)
    down_raw = dot(activated[...], wd[...])
    layer_out[...] = (residual[...] + down_raw * inverse_rms(down_raw) * gain_res).astype(BF16)
    upstream = cotangent[...].astype(F32)
    down_back, share = norm_back(down_raw, gain_res, upstream)
    gain_back[...] = jnp.broadcast_to(jnp.sum(share, axis=0, keepdims=True), (8, D))
    down_low[...] = down_back.astype(BF16)
    turn_down = down_low[...].T
    feed_back[...] = jnp.zeros_like(feed_back)

    def backward(n, carry):
        cols = pl.ds(pl.multiple_of(n * PART, PART), PART)
        act_back = dot_nt(down_low[...], wd[cols, :])
        gate_low = (act_back * up[:, cols]).astype(BF16)
        up_low = (act_back * gate[:, cols]).astype(BF16)
        feed_back[...] += dot_nt(gate_low, wg[:, cols]) + dot_nt(up_low, wu[:, cols])
        for base, low in ((0, gate_low), (160, up_low)):
            grad = dot(turn_low[...], low).astype(BF16)
            for i, ref in enumerate((keep, keep, give, give)):
                for b in range(PART // 128):
                    ref[n * (PART // 128) + b, i % 2, base : base + 160, :] = grad[
                        160 * i : 160 * i + 160, 128 * b : 128 * b + 128
                    ]
        grad = dot(turn_down, activated[:, cols]).astype(BF16)
        j = n // (512 // PART)
        first = (n % (512 // PART)) * (PART // 128)

        def write_down(ref):
            for b in range(PART // 128):
                for r in range(4):
                    ref[(first + b) * 4 + r, j // 2, 320:480, :] = grad[160 * r : 160 * r + 160, 128 * b : 128 * b + 128]
        put(j, write_down)
        return carry

    lax.fori_loop(0, FF // PART, backward, 0)


def output_kernel(place, cotangent, attended, gains, wo, out_raw, residual, feed_back, result_gain_back,
                  give, keep, attended_back, residual_back, gain_back):
    core = place[2]
    gain_att, gain_feed = gains[0:1, 640:1280], gains[1:2, :640]
    part, share = norm_back(residual[...], gain_feed, feed_back[...])
    gain_back[1:2, :] = jnp.sum(share, axis=0, keepdims=True)
    back = cotangent[...].astype(F32) + part
    residual_back[...] = back
    out_back, share = norm_back(out_raw[...], gain_att, back)
    gain_back[0:1, :] = jnp.sum(share, axis=0, keepdims=True)
    gain_back[2:, :] = result_gain_back[2:, :]
    out_low = out_back.astype(BF16)
    attended_back[...] = dot_nt(out_low, wo[...]).astype(BF16)
    turn_out = out_low.T
    for ref, side in ((keep, core), (give, 1 - core)):
        for z in range(2):
            cols = pl.ds(pl.multiple_of((2 * z + side) * 256, 256), 256)
            grad = dot(turn_out, attended[:, cols]).astype(BF16)
            for b in range(2):
                for r in range(8):
                    ref[8 * b + r, z, :, :] = grad[80 * r : 80 * r + 80, 128 * b : 128 * b + 128]


FEED_SCRATCH = [((D, FF), BF16), ((D, FF), BF16), ((FF, D), BF16), ((T, FF), F32), ((T, FF), F32),
                ((T, FF), BF16), ((T, D), BF16)]
FEED_OUTS = [((T, D), BF16), ((16, 2, ROWS, 128), BF16), ((16, 2, ROWS, 128), BF16), ((T, D), F32), ((8, D), F32)]
MIX_OUTS = [((1024, D), BF16), ((T, D), F32), ((T, D), F32), ((T, D), BF16), ((D, T), BF16)]
OUTPUT_OUTS = [((16, 2, 80, 128), BF16), ((16, 2, 80, 128), BF16), ((T, 1024), BF16), ((T, D), F32), ((8, D), F32)]


def back_kernel(query_rot, key_rot, value_low, probs, attended, attended_back,
                query_raw, key_raw, gains, cosine, sine, weight,
                query_low, pair_low, head_back, before_back, key_sum, value_sum):
    key_sum[...] = jnp.zeros_like(key_sum)
    value_sum[...] = jnp.zeros_like(value_sum)
    gain_q, gain_k = gains[0:1, 1280:], gains[1:2, 1280:]
    gain_q_back = jnp.zeros((1, HD), F32)
    for i in range(T // TILE):
        rows, span = slice(i * TILE, (i + 1) * TILE), slice(i * TILE, i * TILE + SPAN)
        back = stacked(attended_back, rows)
        delta = jnp.sum(back.astype(F32) * stacked(attended, rows).astype(F32), axis=-1, keepdims=True)
        prob = probs[i]
        prob_back = dot_nt(back, value_low[span, :])
        score_back = (prob.astype(F32) * (prob_back - delta)).astype(BF16)
        value_sum[:, span] += dot(back.T, prob)
        key_sum[:, span] += dot(stacked(query_rot, rows).T, score_back) * SCALE
        query_back = dot(score_back, key_rot[span, :]) * SCALE
        cos, sin = cosine[T + i * TILE : T + (i + 1) * TILE, :], sine[T + i * TILE : T + (i + 1) * TILE, :]
        for h in range(HEADS):
            unturned = turned(query_back[h * TILE : (h + 1) * TILE], cos, -sin)
            raw_back, share = norm_back(query_raw[rows, h * HD : (h + 1) * HD], gain_q, unturned)
            gain_q_back += jnp.sum(share, axis=0, keepdims=True)
            query_low[rows, h * HD : (h + 1) * HD] = raw_back.astype(BF16)
    raw_back, share = norm_back(key_raw[...], gain_k, turned(key_sum[...].T, cosine[...], -sine[...]))
    gain_k_back = jnp.sum(share, axis=0, keepdims=True)
    pair_low[:, :HD] = raw_back.astype(BF16)
    pair_low[:, HD:] = value_sum[...].T.astype(BF16)

    before_back[...] = dot_nt(pair_low[:T, :], weight[:, 1024:]).astype(BF16)
    rows = lax.broadcasted_iota(jnp.int32, (8, HD), 0)
    head_back[...] = jnp.where(rows == 0, gain_q_back, gain_k_back)


def first_kernel(place, normed, query_low, pair_low, weight, head_back, gain_back, before, here, before_back,
                 give, keep, own_back, turned_all):
    def store(grad, block):
        for i, ref in enumerate((keep, keep, give, give)):
            for b in range(grad.shape[1] // 128):
                ref[i % 2, 160 * (block + b) : 160 * (block + b) + 160, :] = grad[
                    160 * i : 160 * i + 160, 128 * b : 128 * b + 128
                ]

    by_owner(turned_all, normed[...].T, place[2])
    for h in range(2):
        store(dot(turned_all[:, T:], query_low[:, 512 * h : 512 * h + 512]).astype(BF16), 4 * h)
    store(dot(turned_all[...], pair_low[...]).astype(BF16), 8)

    earlier = before_back[...].astype(F32)
    later = dot_nt(pair_low[T:, :], weight[:, 1024:]) + dot_nt(query_low[...], weight[:, :1024])
    own_back[...] = later
    values, values_before = here[...].astype(F32), before[...].astype(F32)
    gain_in_back = jnp.sum(later * (values * inverse_rms(values)), axis=0, keepdims=True) + jnp.sum(
        earlier * (values_before * inverse_rms(values_before)), axis=0, keepdims=True
    )
    rows = lax.broadcasted_iota(jnp.int32, (128, 128), 0)
    block = jnp.zeros((128, 128), F32)
    lines = [gain_in_back] + [gain_back[r : r + 1, :] for r in range(3)] + [head_back[0:1, :], head_back[1:2, :]]
    at = 0
    for line in lines:
        for b in range(line.shape[1] // 128):
            block = jnp.where(rows == at, line[:, 128 * b : 128 * b + 128], block)
            at += 1
    low = block.astype(BF16)
    for j in range(2):
        keep[j, 1920:, :] = low
        give[j, 1920:, :] = low


MERGED = 4


def merge_kernel(place, keep, got, out_keep, out_got, wide, up_keep, up_give, down_keep, down_give):
    half, mixed = place[1], place[5]
    for k in range(MERGED):
        for z in range(2):
            def added(rows, k=k, z=z):
                return keep[k, z, rows, :].astype(F32) + got[k, z, rows, :].astype(F32)

            wide[k, z, :160, :] = added(slice(0, 160)).astype(BF16)
            wide[k, z, 160:240, :] = (out_keep[k, z].astype(F32) + out_got[k, z].astype(F32)).astype(BF16)
            wide[k, z, 240:, :] = jnp.zeros((16, 128), BF16)
            one, two = added(slice(320, 400)), added(slice(400, 480))
            down_keep[k, z] = jnp.where(mixed == 0, one, two).astype(BF16)
            down_give[k, z] = jnp.where(mixed == 0, two, one).astype(BF16)
        one, two = (keep[k, z, 160:320, :].astype(F32) + got[k, z, 160:320, :].astype(F32) for z in range(2))
        up_keep[k] = jnp.where(half == 0, one, two).astype(BF16)
        up_give[k] = jnp.where(half == 0, two, one).astype(BF16)


def merge(place, keep, got, out_keep, out_got):
    def spec(*shape):
        return pl.BlockSpec((MERGED, *shape), lambda i: (i,) + (0,) * len(shape))

    outs = [(2, 256, 128), (160, 128), (160, 128), (2, 80, 128), (2, 80, 128)]
    return pl.pallas_call(
        merge_kernel,
        grid=(16 // MERGED,),
        out_shape=[jax.ShapeDtypeStruct((16, *o), BF16) for o in outs],
        in_specs=[pl.BlockSpec(memory_space=pltpu.SMEM)] + [spec(2, 480, 128)] * 2 + [spec(2, 80, 128)] * 2,
        out_specs=[spec(*o) for o in outs],
        compiler_params=pltpu.CompilerParams(vmem_limit_bytes=60 * 2**20),
        cost_estimate=pl.CostEstimate(flops=1_000_000, bytes_accessed=1_000_000, transcendentals=0),
    )(place, keep, got, out_keep, out_got)


def line_kernel(place, up_keep, up_got, down_keep, down_got, up_next, up_give, down_next, down_give):
    half, low = place[1], place[4]

    def parted(one, two, choice, stay, leave):
        stay[...] = jnp.where(choice == 0, one, two).astype(BF16)
        leave[...] = jnp.where(choice == 0, two, one).astype(BF16)

    one, two = (up_keep[:, r : r + 80, :].astype(F32) + up_got[:, r : r + 80, :].astype(F32) for r in (0, 80))
    parted(one, two, low, up_next, up_give)
    one, two = (down_keep[:, z].astype(F32) + down_got[:, z].astype(F32) for z in range(2))
    parted(one, two, half, down_next, down_give)


def rest_kernel(keep, got, up_keep, up_got, down_keep, down_got, rest):
    for z in range(2):
        for k in range(16):
            rows = slice(128 * k, 128 * k + 128)
            rest[k, 128 * z : 128 * z + 128, :] = (keep[z, rows, :].astype(F32) + got[z, rows, :].astype(F32)).astype(BF16)
    rest[:, 256:336, :] = (up_keep[...].astype(F32) + up_got[...].astype(F32)).astype(BF16)
    rest[:, 336:, :] = (down_keep[...].astype(F32) + down_got[...].astype(F32)).astype(BF16)


def finish_wide_kernel(place, own, other, gate, up, out):
    low = place[4]
    blocks = []
    for k in range(16):
        cols = slice(128 * k, 128 * k + 128)
        mine, theirs = own[k].astype(F32), other[k].astype(F32)
        one = jnp.where(low == 0, mine, theirs)
        two = jnp.where(low == 0, theirs, mine)
        gate[:128, cols] = one[:128]
        gate[128:, cols] = two[:32]
        up[:80, cols] = one[128:]
        up[80:, cols] = two[128:]
        blocks.append(two[32:112])
    for b in range(2):
        out[128 * b : 128 * b + 128, :] = jnp.concatenate(blocks[8 * b : 8 * b + 8], axis=0).T


def finish_rest_kernel(place, done, query, key, value, down, *gains):
    me = place[0]
    for b in range(4):
        block = jnp.concatenate([done[4 * b + r, 128:288, :] for r in range(4)], axis=0)
        down[128 * b : 128 * b + 128, :] = block.astype(F32).T
    for block in range(12):
        ref, at = ((query, block), (key, block - 8), (value, block - 10))[(block >= 8) + (block >= 10)]
        row = 0
        while row < 160:
            flat = 160 * block + row
            chunk, start = flat // 128, flat % 128
            size = min(160 - row, 128 - start)
            ref[row : row + size, 128 * at : 128 * at + 128] = done[chunk, start : start + size, :].astype(F32)
            row += size
    lines = done[15, 0:32, :]

    def pick(count, size):
        parts = []
        for b in range(count):
            source = lax.broadcasted_iota(jnp.int32, (128, size), 0) + 128 * b
            target = lax.broadcasted_iota(jnp.int32, (128, size), 1) + me * size
            parts.append(dot(lines, jnp.where(source == target, 1.0, 0.0).astype(BF16)))
        return parts

    for i, ref in enumerate(gains[:4]):
        parts = pick(5, 160) if i == 0 else parts
        ref[...] = sum(parts[b][5 * i + b : 5 * i + b + 1, :] for b in range(5)).reshape(160)
    parts = pick(2, 64)
    for i, ref in enumerate(gains[4:]):
        ref[...] = sum(parts[b][20 + 2 * i + b : 21 + 2 * i + b, :] for b in range(2)).reshape(64)


def call(kernel, outs, scratch, flops, *args):
    spec = [pl.BlockSpec(memory_space=pltpu.SMEM)] + [pl.BlockSpec(memory_space=pltpu.VMEM)] * (len(args) - 1)
    if kernel in (attend_kernel, rest_kernel, back_kernel):
        spec = [pl.BlockSpec(memory_space=pltpu.VMEM)] * len(args)
    shapes = [jax.ShapeDtypeStruct(s, d) for s, d in outs]
    size = sum(a.size * a.dtype.itemsize for a in args) + sum(s.size * s.dtype.itemsize for s in shapes)
    return pl.pallas_call(
        kernel,
        out_shape=shapes,
        in_specs=spec,
        out_specs=[pl.BlockSpec(memory_space=pltpu.VMEM)] * len(shapes),
        scratch_shapes=[pltpu.VMEM(s, d) for s, d in scratch],
        compiler_params=pltpu.CompilerParams(vmem_limit_bytes=60 * 2**20),
        cost_estimate=pl.CostEstimate(flops=flops, bytes_accessed=min(size, flops), transcendentals=0),
    )(*args)


def pick(block, index, axis):
    return lax.dynamic_index_in_dim(block, index, axis, keepdims=False)


def add(*terms):
    return sum(t.astype(F32) for t in terms).astype(BF16)


def plane_swap(chunks):
    return lax.all_to_all(chunks, PLANE, 0, 0)


def plane_total(chunks):
    return jnp.sum(chunks.astype(F32), axis=0)


def plane_gather(chunk):
    return lax.all_to_all(jnp.broadcast_to(chunk[None], (16,) + chunk.shape), PLANE, 0, 0)


def line_sum(part, half):
    keep, give = pick(part, half, 0).astype(BF16), pick(part, 1 - half, 0).astype(BF16)
    return add(keep, send(keep, TO_LOW), send(give, TO_HALF), send(give, TO_SAME))


def shards(
    hidden_in, cotangent, segments, positions,
    query_weight, key_weight, value_weight, output_weight, gate_weight, up_weight, down_weight,
    input_norm, attention_norm, feed_norm, result_norm, query_norm, key_norm,
):
    half, core, low = lax.axis_index("zh"), lax.axis_index("c"), lax.axis_index("zl")
    me = half * 2 + core
    spot = lax.axis_index("y") * 4 + lax.axis_index("x")
    place = jnp.stack([me, half, core, spot, low, low ^ half]).astype(jnp.int32)
    hidden = hidden_in.reshape(T, D)
    code = (segments * 65536 + positions).reshape(T) + 2**20

    gain_rows = [input_norm, attention_norm, feed_norm, result_norm, query_norm, key_norm]
    whole = pl.BlockSpec(memory_space=pltpu.VMEM)
    (first,) = pl.pallas_call(
        pack_kernel,
        out_shape=[jax.ShapeDtypeStruct((12 * BLOCK + 320, 128), BF16)],
        grid_spec=pltpu.PrefetchScalarGridSpec(
            num_scalar_prefetch=1,
            grid=(1,),
            in_specs=[pl.BlockSpec(a.shape, lambda i, s: (0, 0)) for a in (query_weight, key_weight, value_weight)]
            + [pl.BlockSpec(a.shape, lambda i, s: (0,)) for a in gain_rows]
            + [
                pl.BlockSpec((160, 128), lambda i, s: (0, s[3])),
                pl.BlockSpec((160, 128), lambda i, s: (0, s[3])),
            ],
            out_specs=[
                pl.BlockSpec((12 * BLOCK + 320, 128), lambda i, s: (0, 0)),
            ],
        ),
        compiler_params=pltpu.CompilerParams(vmem_limit_bytes=60 * 2**20),
    )(place, query_weight, key_weight, value_weight, *gain_rows, gate_weight, up_weight)

    first_far = send(first, TO_HALF)
    hidden_before = send(hidden, TO_NEXT)
    code_before = send(code, TO_NEXT)
    first_core = send(first, TO_CORE)
    codes = jnp.concatenate([code_before, code])
    own_places = positions.reshape(T)
    places = jnp.concatenate([own_places[0] - T + jnp.arange(T, dtype=jnp.int32), own_places])
    freqs = jnp.exp(-jnp.log(ROPE_BASE) * jnp.arange(HD // 2, dtype=F32) * 2.0 / HD)
    angles = places.astype(F32)[:, None] * freqs
    cosine, sine = jnp.cos(angles), jnp.sin(angles)
    first_far, hidden_before, codes, cosine, sine, output_late, down_late = lax.optimization_barrier(
        (first_far, hidden_before, codes, cosine, sine, output_weight, down_weight)
    )
    first_far_core = send(first_far, TO_CORE)
    far = plane_gather(first_far[12 * BLOCK :])
    out_far = send(output_late, TO_HALF)
    down_far = send(down_late, TO_HALF)
    out_core, gate_core, up_core, down_core = (
        send(w, TO_CORE) for w in (output_weight, gate_weight, up_weight, down_weight)
    )

    weight, gains, normed, query_raw, key_raw, query_rot, key_rot, value_low = call(
        project_kernel,
        [((D, 1536), BF16), ((16, 1536), F32), ((2 * T, D), BF16), ((T, 1024), F32), ((2 * T, HD), F32),
         ((T, 1024), BF16), ((2 * T, HD), BF16), ((2 * T, HD), BF16)],
        [],
        1_000_000,
        place, first, first_core, first_far, first_far_core, hidden_before, hidden, cosine, sine,
    )
    query_rot, out_core, gate_core, up_core, down_core, out_far = lax.optimization_barrier(
        (query_rot, out_core, gate_core, up_core, down_core, out_far)
    )
    out_far_core = send(out_far, TO_CORE)
    attended, probs = call(
        attend_kernel,
        [((T, 1024), BF16), ((T // TILE, HEADS * TILE, SPAN), BF16)],
        [],
        1_000_000,
        query_rot, key_rot, value_low, codes.reshape(1, 2 * T),
    )
    attended, out_far_core, down_far = lax.optimization_barrier((attended, out_far_core, down_far))
    down_far_core = send(down_far, TO_CORE)
    wo, out_raw, residual, feed_in, turn_low = call(
        mix_kernel, MIX_OUTS, [], 1_000_000,
        place, hidden, attended, gains, output_weight, out_core, out_far, out_far_core,
    )
    far, down_far_core, feed_in = lax.optimization_barrier((far, down_far_core, feed_in))
    layer_out, give, keep, feed_back, result_gain_back = call(
        feed_kernel, FEED_OUTS, FEED_SCRATCH, 1_000_000,
        place, residual, cotangent.reshape(T, D), gains, feed_in, turn_low,
        gate_weight, up_weight, down_weight, gate_core, up_core, down_core,
        far, send(far, TO_CORE), down_far, down_far_core,
    )
    out_give, out_keep, attended_back, residual_back, gain_back = call(
        output_kernel, OUTPUT_OUTS, [], 1_000_000,
        place, cotangent.reshape(T, D), attended, gains, wo, out_raw, residual, feed_back, result_gain_back,
    )
    got = send(give, TO_CORE)
    out_got = send(out_give, TO_CORE)
    wide, up_keep, up_give, down_keep, down_give, attended_back = lax.optimization_barrier(
        (*merge(place, keep, got, out_keep, out_got), attended_back)
    )
    wide_got = plane_swap(wide)
    up_got, down_got = send(up_give, TO_HALF), send(down_give, TO_LOW)
    query_low, pair_low, head_back, before_back = call(
        back_kernel,
        [((T, 1024), BF16), ((2 * T, 512), BF16), ((8, HD), F32), ((T, D), BF16)],
        [((HD, 2 * T), F32), ((HD, 2 * T), F32)],
        1_000_000,
        query_rot, key_rot, value_low, probs, attended, attended_back, query_raw, key_raw, gains, cosine, sine, weight,
    )
    up_keep, up_give, down_keep, down_give = call(
        line_kernel, [((16, 80, 128), BF16)] * 4, [], 0, place, up_keep, up_got, down_keep, down_got
    )
    query_low, up_keep, up_give, down_keep, down_give = lax.optimization_barrier(
        (query_low, up_keep, up_give, down_keep, down_give)
    )
    up_got, down_got = send(up_give, TO_LOW), send(down_give, TO_HALF)
    first_give, first_keep, own_back = call(
        first_kernel,
        [((2, 2048, 128), BF16), ((2, 2048, 128), BF16), ((T, D), F32)],
        [((D, 2 * T), BF16)],
        1_000_000,
        place, normed, query_low, pair_low, weight, head_back, gain_back, hidden_before, hidden, before_back,
    )
    first_give, up_got, down_got = lax.optimization_barrier((first_give, up_got, down_got))
    (rest,) = call(
        rest_kernel, [((16, 416, 128), BF16)], [], 0,
        first_keep, send(first_give, TO_CORE), up_keep, up_got, down_keep, down_got,
    )
    rest, wide_got = lax.optimization_barrier((rest, wide_got))
    rest_got = plane_swap(rest)
    wide_part = plane_total(wide_got).reshape(2, 2, 128, 128)
    near, away = pick(wide_part, half, 0), pick(wide_part, 1 - half, 0)
    wide_part = add(
        pick(near, low, 0),
        send(pick(near, 1 - low, 0).astype(BF16), TO_LOW),
        send(pick(away, 1 - low, 0).astype(BF16), TO_HALF),
        send(pick(away, low, 0).astype(BF16), TO_SAME),
    )
    wide_part, before_back = lax.optimization_barrier((wide_part, before_back))
    returned = send(before_back[: T // 2], TO_PREVIOUS)
    crossed = send(before_back[T // 2 :], TO_LOW)
    wide_part, rest_got, returned, crossed = lax.optimization_barrier((wide_part, rest_got, returned, crossed))
    passed = send(crossed, TO_PREVIOUS_PAIR)
    rest_part = plane_total(rest_got)
    wide_done = plane_gather(jnp.concatenate([wide_part, rest_part[256:336].astype(BF16)]))
    down_part = rest_part[336:].astype(BF16)
    down_got = send(down_part, TO_LOW)
    slim_part = line_sum(rest_part[:256].reshape(2, 128, 128), half)
    mixed = low ^ half
    rest_part = jnp.concatenate(
        [slim_part, jnp.where(mixed == 0, down_part, down_got), jnp.where(mixed == 0, down_got, down_part)]
    )
    wide_other = send(wide_done, TO_LOW)
    rest_part, wide_done = lax.optimization_barrier((rest_part, wide_done))
    passed, wide_other = lax.optimization_barrier((passed, wide_other))
    returned = jnp.concatenate([returned, jnp.where(low == 0, crossed, passed)])
    rest_done = plane_gather(rest_part)

    normed_back = own_back + returned.astype(F32)
    gain_in = gains[0, :640]
    inputs = hidden.astype(F32)
    part, _ = norm_back(inputs, gain_in, normed_back)
    input_gradient = (residual_back + part).astype(BF16)

    gate_out, up_out, output_out = call(
        finish_wide_kernel, [((160, FF), F32), ((160, FF), F32), ((256, D), F32)], [], 1_000_000, place, wide_done, wide_other
    )
    rest_out = call(
        finish_rest_kernel,
        [((160, 1024), F32), ((160, HD), F32), ((160, HD), F32), ((512, D), F32)]
        + [((160,), F32)] * 4 + [((64,), F32)] * 2,
        [], 1_000_000, place, rest_done,
    )
    return (
        layer_out.reshape(hidden_in.shape),
        input_gradient.reshape(hidden_in.shape),
        *rest_out[:3],
        output_out,
        gate_out,
        up_out,
        rest_out[3],
        *rest_out[4:],
    )


def solution(mesh):
    fine = Mesh(mesh.devices.reshape(SIZES), AXES)
    seq, fsdp = ("y", "x", "zl"), ("zh", "c")
    tokens, rows, line = P(fsdp, seq, None), P(fsdp, None), P(fsdp)
    placed = (tokens, tokens, P(fsdp, seq), P(fsdp, seq)) + (rows,) * 7 + (line,) * 6
    return jax.shard_map(
        shards,
        mesh=fine,
        in_specs=placed,
        out_specs=(tokens, tokens) + (rows,) * 7 + (line,) * 6,
        check_vma=False,
    )
```
